32 devices in a mesh: samp: 8 (over z, x), head: 4 (over y, core).
Axes of the slice: x: 2, y: 2, z: 4, core: 2. Of those that a mesh axis runs over, the one named last changes fastest.
Arguments:
- single: bfloat16 [64, 768, 768], P('samp', 'head'), may hold values from -6 to 6
- cond: bfloat16 [64, 768, 384], P('samp', 'head'), may hold values from -6 to 6
- pair: bfloat16 [2, 768, 768, 128], P(None, 'head', 'samp'), may hold values from -6 to 6
- complex_length: int32 [2], replicated, may hold values from 384 to 768, as said below
- sample_complex: int32 [64], P('samp'), may hold values from 0 to 1
- cotangent: bfloat16 [64, 768, 768], P('samp', 'head'), may hold values from -6 to 6
- gain_one: bfloat16 [384], replicated, may hold values from 0.5 to 1.5
- w_scale_one: bfloat16 [384, 768], replicated, may hold values from -0.3125 to 0.3125
- b_scale_one: bfloat16 [768], replicated, may hold values from -3 to 3
- w_shift_one: bfloat16 [384, 768], replicated, may hold values from -0.3125 to 0.3125
- w_query: bfloat16 [768, 768], replicated, may hold values from -0.21875 to 0.21875
- b_query: bfloat16 [768], replicated, may hold values from -3 to 3
- w_key: bfloat16 [768, 768], replicated, may hold values from -0.21875 to 0.21875
- w_value: bfloat16 [768, 768], replicated, may hold values from -0.21875 to 0.21875
- w_gate: bfloat16 [768, 768], replicated, may hold values from -0.21875 to 0.21875
- w_out: bfloat16 [768, 768], replicated, may hold values from -0.875 to 0.875
- w_pair: bfloat16 [128, 16], replicated, may hold values from -0.5 to 0.5
- w_attn_cond: bfloat16 [384, 768], replicated, may hold values from -0.3125 to 0.3125
- b_attn_cond: bfloat16 [768], replicated, may hold values from -3 to 3
- gain_two: bfloat16 [384], replicated, may hold values from 0.5 to 1.5
- w_scale_two: bfloat16 [384, 768], replicated, may hold values from -0.3125 to 0.3125
- b_scale_two: bfloat16 [768], replicated, may hold values from -3 to 3
- w_shift_two: bfloat16 [384, 768], replicated, may hold values from -0.3125 to 0.3125
- w_hidden_gate: bfloat16 [768, 1536], replicated, may hold values from -0.21875 to 0.21875
- w_hidden_up: bfloat16 [768, 1536], replicated, may hold values from -0.21875 to 0.21875
- w_hidden_down: bfloat16 [1536, 768], replicated, may hold values from -0.15625 to 0.15625
- w_tr_cond: bfloat16 [384, 768], replicated, may hold values from -0.3125 to 0.3125
- b_tr_cond: bfloat16 [768], replicated, may hold values from -3 to 3
Outputs:
- block_out: bfloat16 [64, 768, 768], P('samp', 'head')
- grad_single: float32 [64, 768, 768], P('samp', 'head')
- grad_pair: float32 [2, 768, 768, 128], P(None, 'head', 'samp')
- grad_gain_one: float32 [384], replicated
- grad_w_scale_one: float32 [384, 768], P('samp', 'head')
- grad_b_scale_one: float32 [768], replicated
- grad_w_shift_one: float32 [384, 768], P('samp', 'head')
- grad_w_query: float32 [768, 768], P('samp', 'head')
- grad_b_query: float32 [768], replicated
- grad_w_key: float32 [768, 768], P('samp', 'head')
- grad_w_value: float32 [768, 768], P('samp', 'head')
- grad_w_gate: float32 [768, 768], P('samp', 'head')
- grad_w_out: float32 [768, 768], P('samp', 'head')
- grad_w_pair: float32 [128, 16], replicated
- grad_w_attn_cond: float32 [384, 768], P('samp', 'head')
- grad_b_attn_cond: float32 [768], replicated
- grad_gain_two: float32 [384], replicated
- grad_w_scale_two: float32 [384, 768], P('samp', 'head')
- grad_b_scale_two: float32 [768], replicated
- grad_w_shift_two: float32 [384, 768], P('samp', 'head')
- grad_w_hidden_gate: float32 [768, 1536], P('samp', 'head')
- grad_w_hidden_up: float32 [768, 1536], P('samp', 'head')
- grad_w_hidden_down: float32 [1536, 768], P('samp', 'head')
- grad_w_tr_cond: float32 [384, 768], P('samp', 'head')
- grad_b_tr_cond: float32 [768], replicated
The draws below stay inside these ranges and needn't reach their ends.
Inputs may be any that keep to these rules, and one draw needn't show every extreme that they name: A sample attends to the first complex_length tokens of its complex; one complex, drawn from the seed, has more than 672.
All inputs are finite; a program needn't handle non-finite values.
Results may differ from the reference program's by a relative error of at most 0.017.
Values may be sent and summed in bfloat16 or wider, within the bound.
No kernel may reach another device: no remote copies, remote signals or barrier semaphores. Data moves between devices by JAX's collectives and lax.ppermute only.
A program may use at most 320 MiB of HBM per device.

```python
import math
import jax
import jax.numpy as jnp
from jax import lax

C = 768
H = 16
CZ = 128
CS = 384
FF = 1536
L = 768
NC = 2
SAMPLES = 64


def draw_complex_length(key, part):
    key = jax.random.fold_in(key, 11)
    key_long, key_short, key_pick = jax.random.split(key, 3)
    long_len = L - jax.random.randint(key_long, (NC,), 0, L // 8)
    short_len = jax.random.randint(key_short, (NC,), L // 2, 7 * L // 8 + 1)
    chosen = jax.random.randint(key_pick, (), 0, NC)
    return jnp.where(jnp.arange(NC) == chosen, long_len, short_len).astype(jnp.int32)


def touch_ends(array, own_key, low, largest):
    place = [jax.random.randint(jax.random.fold_in(own_key, axis), (), 0, length) for axis, length in enumerate(array.shape)]
    longest = array.shape.index(max(array.shape))
    beside = place[:longest] + [(place[longest] + 1) % array.shape[longest]] + place[longest + 1:]
    return array.at[tuple(place)].set(low).at[tuple(beside)].set(largest)


def block_levels(stream_key, shape, shards, low, largest):
    level = 1.0
    for position, parts in shards:
        heights = jax.random.uniform(jax.random.fold_in(jax.random.fold_in(stream_key, 6), position), (parts,), jnp.float32, low / len(shards), largest / len(shards))
        level = level * jnp.repeat(jnp.exp(heights), shape[position] // parts).reshape((-1,) + (1,) * (len(shape) - 1 - position))
    return level


def gaussian(key, dims, width, limit, pieces=(), held_as=jnp.bfloat16):
    values = width * jax.random.normal(key, dims, jnp.float32)
    if pieces:
        values = values * block_levels(key, dims, pieces, -0.22, 0.18)
    return jnp.clip(values, -limit, limit).astype(held_as)


def setup_inputs(seed: int = 0) -> dict:
    seeds = jax.random.split(jax.random.key(seed), 29)
    single = gaussian(seeds[0], (SAMPLES, L, C), 1.0, 6.0, ((0, 8), (1, 4)))
    cond = gaussian(seeds[1], (SAMPLES, L, CS), 1.0, 6.0, ((0, 8), (1, 4)))
    pair = gaussian(seeds[2], (NC, L, L, CZ), 1.0, 6.0, ((1, 4), (2, 8)))
    complex_length = draw_complex_length(jax.random.fold_in(seeds[28], 71), 0)
    sample_complex = touch_ends(jax.random.randint(seeds[4], (SAMPLES,), 0, NC), jax.random.fold_in(seeds[4], 1), 0, NC - 1).astype(jnp.int32)
    cotangent = gaussian(seeds[5], (SAMPLES, L, C), 1.0, 6.0, ((0, 8), (1, 4)))
    gain_one = jnp.clip(1.0 + 0.1 * jax.random.normal(seeds[6], (CS,), jnp.float32), 0.5, 1.5).astype(jnp.bfloat16)
    w_scale_one = gaussian(seeds[7], (CS, C), CS ** -0.5, 0.3125)
    b_scale_one = gaussian(seeds[8], (C,), 0.5, 3.0)
    w_shift_one = gaussian(seeds[9], (CS, C), CS ** -0.5, 0.3125)
    w_query = gaussian(seeds[10], (C, C), C ** -0.5, 0.21875)
    b_query = gaussian(seeds[11], (C,), 0.5, 3.0)
    w_key = gaussian(seeds[12], (C, C), C ** -0.5, 0.21875)
    w_value = gaussian(seeds[13], (C, C), C ** -0.5, 0.21875)
    w_gate = gaussian(seeds[14], (C, C), C ** -0.5, 0.21875)
    w_out = gaussian(seeds[15], (C, C), (C // 16) ** -0.5, 0.875)
    w_pair = gaussian(seeds[16], (CZ, H), CZ ** -0.5, 0.5)
    w_attn_cond = gaussian(seeds[17], (CS, C), CS ** -0.5, 0.3125)
    b_attn_cond = gaussian(seeds[18], (C,), 0.5, 3.0)
    gain_two = jnp.clip(1.0 + 0.1 * jax.random.normal(seeds[19], (CS,), jnp.float32), 0.5, 1.5).astype(jnp.bfloat16)
    w_scale_two = gaussian(seeds[20], (CS, C), CS ** -0.5, 0.3125)
    b_scale_two = gaussian(seeds[21], (C,), 0.5, 3.0)
    w_shift_two = gaussian(seeds[22], (CS, C), CS ** -0.5, 0.3125)
    w_hidden_gate = gaussian(seeds[23], (C, FF), C ** -0.5, 0.21875)
    w_hidden_up = gaussian(seeds[24], (C, FF), C ** -0.5, 0.21875)
    w_hidden_down = gaussian(seeds[25], (FF, C), FF ** -0.5, 0.15625)
    w_tr_cond = gaussian(seeds[26], (CS, C), CS ** -0.5, 0.3125)
    b_tr_cond = gaussian(seeds[27], (C,), 0.5, 3.0)
    return dict(single=single, cond=cond, pair=pair, complex_length=complex_length, sample_complex=sample_complex, cotangent=cotangent, gain_one=gain_one, w_scale_one=w_scale_one, b_scale_one=b_scale_one, w_shift_one=w_shift_one, w_query=w_query, b_query=b_query, w_key=w_key, w_value=w_value, w_gate=w_gate, w_out=w_out, w_pair=w_pair, w_attn_cond=w_attn_cond, b_attn_cond=b_attn_cond, gain_two=gain_two, w_scale_two=w_scale_two, b_scale_two=b_scale_two, w_shift_two=w_shift_two, w_hidden_gate=w_hidden_gate, w_hidden_up=w_hidden_up, w_hidden_down=w_hidden_down, w_tr_cond=w_tr_cond, b_tr_cond=b_tr_cond)


@jax.custom_vjp
def low(v):
    return lax.optimization_barrier(v.astype(jnp.bfloat16)).astype(jnp.float32)

@jax.custom_vjp
def low_back(v):
    return v

def low_keep(v):
    return (low(v), None)

def low_pass(kept, grad):
    return (grad,)

def back_keep(v):
    return (v, None)

def back_low(kept, grad):
    return (low(grad),)
low.defvjp(low_keep, low_pass)
low_back.defvjp(back_keep, back_low)
highest = lax.Precision.HIGHEST

def norm_last(inputs):
    mean_val = lax.optimization_barrier(jnp.mean(inputs, axis=-1, keepdims=True))
    centered = inputs - mean_val
    variance = lax.optimization_barrier(jnp.mean(centered * centered, axis=-1, keepdims=True))
    return centered * lax.rsqrt(variance + 1e-05)

def project(inputs, weight):
    return jnp.dot(inputs, weight, precision=highest, preferred_element_type=jnp.float32)

def adaptive(inputs, cond_hat, gain, w_scale, b_scale, w_shift):
    cond_low = low(cond_hat * gain)
    scale_logit = low_back(project(cond_low, w_scale) + b_scale)
    shifted = low_back(project(cond_low, w_shift))
    return jax.nn.sigmoid(scale_logit) * norm_last(inputs) + shifted

def block(weights, bias_all, key_valid, sample_group):
    gain_one, w_scale_one, b_scale_one, w_shift_one, w_query, b_query, w_key, w_value, w_gate, w_out, w_pair, w_attn_cond, b_attn_cond, gain_two, w_scale_two, b_scale_two, w_shift_two, w_hidden_gate, w_hidden_up, w_hidden_down, w_tr_cond, b_tr_cond = weights
    single_g, cond_g, complex_g = sample_group
    count = single_g.shape[0]
    heads = w_pair.shape[1]
    head_dim = C // heads
    cond_hat = norm_last(cond_g)
    x_one = low(adaptive(single_g, cond_hat, gain_one, w_scale_one, b_scale_one, w_shift_one))
    query = low(low_back(project(x_one, w_query) + b_query)).reshape(count, L, heads, head_dim)
    keys_proj = low(low_back(project(x_one, w_key))).reshape(count, L, heads, head_dim)
    values = low(low_back(project(x_one, w_value))).reshape(count, L, heads, head_dim)
    gate_val = jax.nn.sigmoid(low_back(project(x_one, w_gate)))
    raw = jnp.einsum('bihd,bjhd->bhij', query, keys_proj, precision=highest)
    scores = low_back(raw * (1.0 / math.sqrt(head_dim)) + bias_all[complex_g])
    scores = jnp.where(key_valid[complex_g][:, None, None, :], scores, -1e+30)
    row_max = lax.optimization_barrier(jnp.max(scores, axis=-1, keepdims=True))
    exp_scores = jnp.exp(scores - row_max)
    probs = exp_scores / lax.optimization_barrier(jnp.sum(exp_scores, axis=-1, keepdims=True))
    attended = jnp.einsum('bhij,bjhd->bihd', low(probs), values, precision=highest).reshape(count, L, C)
    attended = low(low_back(attended))
    gated = low(attended * gate_val)
    attn_branch = low_back(project(gated, w_out))
    attn_cond = jax.nn.sigmoid(low_back(project(cond_g, w_attn_cond) + b_attn_cond))
    middle = single_g + attn_cond * attn_branch
    x_two = low(adaptive(middle, cond_hat, gain_two, w_scale_two, b_scale_two, w_shift_two))
    hidden_gate = low_back(project(x_two, w_hidden_gate))
    hidden_up = low_back(project(x_two, w_hidden_up))
    hidden = low(jax.nn.silu(hidden_gate) * hidden_up)
    tr_branch = low_back(project(hidden, w_hidden_down))
    tr_cond = jax.nn.sigmoid(low_back(project(cond_g, w_tr_cond) + b_tr_cond))
    return middle + tr_cond * tr_branch

def reference(single, cond, pair, complex_length, sample_complex, cotangent, gain_one, w_scale_one, b_scale_one, w_shift_one, w_query, b_query, w_key, w_value, w_gate, w_out, w_pair, w_attn_cond, b_attn_cond, gain_two, w_scale_two, b_scale_two, w_shift_two, w_hidden_gate, w_hidden_up, w_hidden_down, w_tr_cond, b_tr_cond):
    weights = tuple((item.astype(jnp.float32) for item in (gain_one, w_scale_one, b_scale_one, w_shift_one, w_query, b_query, w_key, w_value, w_gate, w_out, w_pair, w_attn_cond, b_attn_cond, gain_two, w_scale_two, b_scale_two, w_shift_two, w_hidden_gate, w_hidden_up, w_hidden_down, w_tr_cond, b_tr_cond)))
    key_valid = jnp.arange(L, dtype=jnp.int32)[None, :] < complex_length[:, None]
    cond_groups = cond.astype(jnp.float32).reshape(SAMPLES // 2, 2, L, CS)
    complex_groups = sample_complex.reshape(SAMPLES // 2, 2)

    def forward(single_f, pair_f, params):
        pair_low = low(norm_last(pair_f))
        bias_all = low(low_back(jnp.einsum('cijz,zh->chij', pair_low, params[10], precision=highest)))
        single_groups = single_f.reshape(SAMPLES // 2, 2, L, C)

        def run_group(sample_group):
            return jax.checkpoint(block)(params, bias_all, key_valid, sample_group)
        outputs = lax.map(run_group, (single_groups, cond_groups, complex_groups))
        return outputs.reshape(SAMPLES, L, C)
    result, pullback = jax.vjp(forward, single.astype(jnp.float32), pair.astype(jnp.float32), weights)
    grad_single, grad_pair, grads = pullback(cotangent.astype(jnp.float32))
    return (result.astype(jnp.bfloat16), grad_single, grad_pair, grads[0], grads[1], grads[2], grads[3], grads[4], grads[5], grads[6], grads[7], grads[8], grads[9], grads[10], grads[11], grads[12], grads[13], grads[14], grads[15], grads[16], grads[17], grads[18], grads[19], grads[20], grads[21])
```

```python
import functools
import math

import jax
import jax.numpy as jnp
from jax import lax
from jax.experimental import pallas as pl
from jax.experimental.pallas import tpu as pltpu
from jax.sharding import PartitionSpec as P

f32, bf16 = jnp.float32, jnp.bfloat16
epsilon = 1e-05
fill_value = -1e30
LOG2E = math.log2(math.e)
VMEM_BYTES = 60 << 20
NN, NT, TN = ((1,), (0,)), ((1,), (1,)), ((0,), (0,))


def dot(a, b, dims):
    return lax.dot_general(a, b, (dims, ((), ())), preferred_element_type=f32)


def norm_rows(inputs):
    mean_val = jnp.mean(inputs, axis=-1, keepdims=True)
    centered = inputs - mean_val
    variance = jnp.mean(centered * centered, axis=-1, keepdims=True)
    inverse = lax.rsqrt(variance + epsilon)
    return (centered * inverse, inverse)


def norm_back(normed, inverse, upstream):
    mean_grad = jnp.mean(upstream, axis=-1, keepdims=True)
    mean_dot = jnp.mean(upstream * normed, axis=-1, keepdims=True)
    return inverse * (upstream - mean_grad - normed * mean_dot)


def tile_of(tokens):
    return max(t for t in (8, 16, 32, 64, 128, 256) if tokens % t == 0)


def attend_kernel(meta, x0, x1, x2, x3, w_ref, bq_ref, bias_ref, o_ref, p_ref, q_ref, k_ref, v_ref, l_ref,
                  xs, ks, ss, *, nh, hd, rows, jc, nchunk, per_block, qscale):
    b = pl.program_id(0)
    g = meta[0]
    cplx = meta[1 + b]
    for r, x in enumerate((x0, x1, x2, x3)):
        xs[r * rows:(r + 1) * rows, :] = x[0]
    wch = nh * hd
    q = dot(w_ref[0:wch, :], xs[0:2 * rows, :], NT) + bq_ref[...]
    q_ref[0] = (q * qscale).astype(bf16)
    kv = dot(w_ref[wch:3 * wch, :], xs[...], NT).astype(bf16)
    k_ref[0] = kv[0:wch]
    v_ref[0] = kv[wch:]
    ones = jnp.ones((16, kv.shape[1]), bf16)
    outs = []
    sums = []
    for h in range(nh):
        ks[h % 2, :, :] = jnp.transpose(k_ref[0, h * hd:(h + 1) * hd, :])
        qT = q_ref[0, h * hd:(h + 1) * hd, :]
        m = None
        for t in range(nchunk):
            r, u = t // per_block, t % per_block
            s_idx = (r ^ g) * per_block + u
            s = dot(ks[h % 2, t * jc:(t + 1) * jc, :], qT, NN) + bias_ref[s_idx, cplx, h].astype(f32)
            ss[h % 2, t * jc:(t + 1) * jc, :] = s
            mt = jnp.max(s.reshape(jc // 8, 8, s.shape[1]), axis=0)
            m = mt if m is None else jnp.maximum(m, mt)
        m = jnp.max(m, axis=0, keepdims=True)
        for t in range(nchunk):
            p_ref[0, h, t * jc:(t + 1) * jc, :] = jnp.exp2(ss[h % 2, t * jc:(t + 1) * jc, :] - m).astype(bf16)
        va = jnp.concatenate([v_ref[0, h * hd:(h + 1) * hd, :], ones], axis=0)
        oT = dot(va, p_ref[0, h], NN)
        l = oT[hd:hd + 1, :]
        outs.append(oT[:hd] / l)
        sums.append(l)
    l_ref[0] = jnp.concatenate(sums, axis=0)
    o = jnp.transpose(jnp.concatenate(outs, axis=0)).astype(bf16)
    o_ref[0, 0] = o[:rows]
    o_ref[1, 0] = o[rows:]

def attend(meta, xb, wT, bq, bias, *, nh, hd):
    B, rows, C = xb[0].shape
    nchunk, ncx, _, jc, qi = bias.shape
    L = nchunk * jc
    wch = nh * hd
    kern = functools.partial(attend_kernel, nh=nh, hd=hd, rows=rows, jc=jc, nchunk=nchunk, per_block=nchunk // 4, qscale=LOG2E / math.sqrt(hd))
    xspec = pl.BlockSpec((1, rows, C), lambda b, m: (b, 0, 0))
    const = lambda shape: pl.BlockSpec(shape, lambda b, m: (0,) * len(shape), pipeline_mode=pl.Buffered(1))
    per = lambda shape: pl.BlockSpec((1,) + shape, lambda b, m: (b,) + (0,) * len(shape))
    return pl.pallas_call(
        kern,
        grid_spec=pltpu.PrefetchScalarGridSpec(
            num_scalar_prefetch=1, grid=(B,),
            in_specs=[xspec] * 4 + [const(wT.shape), const(bq.shape), const(bias.shape)],
            out_specs=[pl.BlockSpec((2, 1, rows, wch), lambda b, m: (0, b, 0, 0)), per((nh, L, qi)), per((wch, qi)), per((wch, L)), per((wch, L)), per((nh, qi))],
            scratch_shapes=[pltpu.VMEM((L, C), bf16), pltpu.VMEM((2, L, hd), bf16), pltpu.VMEM((2, L, qi), f32)],
        ),
        out_shape=[jax.ShapeDtypeStruct((2, B, rows, wch), bf16), jax.ShapeDtypeStruct((B, nh, L, qi), bf16),
                   jax.ShapeDtypeStruct((B, wch, qi), bf16), jax.ShapeDtypeStruct((B, wch, L), bf16), jax.ShapeDtypeStruct((B, wch, L), bf16),
                   jax.ShapeDtypeStruct((B, nh, qi), f32)],
        compiler_params=pltpu.CompilerParams(vmem_limit_bytes=VMEM_BYTES),
        cost_estimate=pl.CostEstimate(flops=int(30e9), bytes_accessed=int(60e6), transcendentals=int(9e6)),
        name="attend",
    )(meta, *xb, wT, bq, bias)

def attend_back_kernel(meta, x0, x1, x2, x3, w_ref, p_ref, q_ref, k_ref, v_ref, l_ref, o_ref, do0, do1, *rest,
                       nh, hd, rows, jc, nchunk, per_block, scale, chained):
    before = rest[0] if chained else None
    dx_ref, db_ref, gw_ref, gb_ref, xs, vs, ds, acc, dst = rest[1:] if chained else rest
    b = pl.program_id(0)
    g = meta[0]
    cplx = meta[1 + b]
    wch = nh * hd
    L = nchunk * jc

    @pl.when(b == 0)
    def _():
        acc[...] = jnp.zeros_like(acc)
        gw_ref[...] = jnp.zeros_like(gw_ref)
        gb_ref[...] = jnp.zeros_like(gb_ref)

    for r, x in enumerate((x0, x1, x2, x3)):
        xs[r * rows:(r + 1) * rows, :] = x[0]
    dO = jnp.transpose(jnp.concatenate([do0[0], do1[0]], axis=0).astype(f32))
    O = jnp.transpose(jnp.concatenate([o_ref[0, 0], o_ref[1, 0]], axis=0).astype(f32))
    prod = dO * O
    qi = dO.shape[1]
    row = lax.broadcasted_iota(jnp.int32, (16, qi), 0)
    ones = jnp.ones((16, L), bf16)
    for h in range(nh):
        hs = slice(h * hd, (h + 1) * hd)
        linv = 1.0 / l_ref[0, h:h + 1, :]
        dOh = (dO[hs] * linv).astype(bf16)
        delta = jnp.sum(prod[hs], axis=0, keepdims=True) * linv
        hi = delta.astype(bf16).astype(f32)
        extra = jnp.where(row == 0, -hi, jnp.where(row == 1, hi - delta, 0.0)).astype(bf16)
        dOa = jnp.concatenate([dOh, extra], axis=0)
        vs[h % 2] = jnp.transpose(jnp.concatenate([v_ref[0, hs, :], ones], axis=0))
        for t in range(nchunk):
            r, u = t // per_block, t % per_block
            s_idx = (r ^ g) * per_block + u
            ts = slice(t * jc, (t + 1) * jc)
            d = dot(vs[h % 2, ts, :], dOa, NN) * p_ref[0, h, ts, :].astype(f32)
            acc[s_idx, cplx, h] += d
            ds[h % 2, ts, :] = d.astype(bf16)
        dst[h * hd:(h + 1) * hd, 0:qi] = (dot(k_ref[0, hs, :], ds[h % 2], NN) * scale).astype(bf16)
        dst[wch + h * hd:wch + (h + 1) * hd, :] = (dot(q_ref[0, hs, :], ds[h % 2], NT) * (1.0 / LOG2E)).astype(bf16)
        dst[2 * wch + h * hd:2 * wch + (h + 1) * hd, :] = dot(dOh, p_ref[0, h], NT).astype(bf16)
    dq = dst[0:wch, 0:qi]
    gb_ref[...] += jnp.sum(dq.astype(f32), axis=1, keepdims=True)
    gw_ref[0:wch, :] += dot(dq, xs[0:qi, :], NN)
    gw_ref[wch:, :] += dot(dst[wch:, :], xs[...], NN)
    dkv = jnp.transpose(dst[wch:, :])
    dqr = jnp.transpose(dq)
    for r in range(4):
        rs = slice(r * rows, (r + 1) * rows)
        dx = dot(dkv[rs], w_ref[wch:, :], NN)
        if r < 2:
            dx += dot(dqr[rs], w_ref[0:wch, :], NN)
        if chained:
            dx += before[r, 0].astype(f32)
        dx_ref[r, 0] = dx.astype(bf16)

    @pl.when(b == pl.num_programs(0) - 1)
    def _():
        db_ref[...] = acc[...].astype(bf16)

def attend_back(meta, xb, wT, p, q, k, v, l, o, do0, do1, before, nchunk, ncx, *, nh, hd):
    B, rows, C = xb[0].shape
    L = k.shape[2]; qi = q.shape[2]; jc = L // nchunk
    wch = nh * hd
    kern = functools.partial(attend_back_kernel, nh=nh, hd=hd, rows=rows, jc=jc, nchunk=nchunk, per_block=nchunk // 4, scale=1.0 / math.sqrt(hd), chained=before is not None)
    xspec = pl.BlockSpec((1, rows, C), lambda b, m: (b, 0, 0))
    const = lambda shape: pl.BlockSpec(shape, lambda b, m: (0,) * len(shape), pipeline_mode=pl.Buffered(1))
    per = lambda shape: pl.BlockSpec((1,) + shape, lambda b, m: (b,) + (0,) * len(shape))
    db = (nchunk, ncx, nh, jc, qi)
    blockspec = pl.BlockSpec((4, 1, rows, C), lambda b, m: (0, b, 0, 0))
    extra = () if before is None else (before,)
    return pl.pallas_call(
        kern,
        grid_spec=pltpu.PrefetchScalarGridSpec(
            num_scalar_prefetch=1, grid=(B,),
            in_specs=[xspec] * 4 + [const(wT.shape), per((nh, L, qi)), per((wch, qi)), per((wch, L)), per((wch, L)), per((nh, qi)),
                      pl.BlockSpec((2, 1, rows, wch), lambda b, m: (0, b, 0, 0)), per((rows, wch)), per((rows, wch))]
            + [blockspec] * (before is not None),
            out_specs=[blockspec, const(db), const((3 * wch, C)), const((wch, 1))],
            scratch_shapes=[pltpu.VMEM((L, C), bf16), pltpu.VMEM((2, L, hd + 16), bf16), pltpu.VMEM((2, L, qi), bf16), pltpu.VMEM(db, f32), pltpu.VMEM((3 * wch, L), bf16)],
        ),
        out_shape=[jax.ShapeDtypeStruct((4, B, rows, C), bf16), jax.ShapeDtypeStruct(db, bf16), jax.ShapeDtypeStruct((3 * wch, C), f32), jax.ShapeDtypeStruct((wch, 1), f32)],
        compiler_params=pltpu.CompilerParams(vmem_limit_bytes=VMEM_BYTES),
        cost_estimate=pl.CostEstimate(flops=int(60e9), bytes_accessed=int(60e6), transcendentals=0),
        name="attend_back",
    )(meta, *xb, wT, p, q, k, v, l, o, do0, do1, *extra)


def fold8(v):
    return jnp.sum(v.reshape(v.shape[0] // 8, 8, v.shape[1]), axis=0)


def fixed(shape):
    return pl.BlockSpec(shape, lambda *_: (0,) * len(shape), pipeline_mode=pl.Buffered(1))


def tiled(rows, width):
    return pl.BlockSpec((rows, width), lambda t, *_: (t, 0))


def adapt_kernel(single_ref, cond_ref, gain, w_scale, b_scale, w_shift, x_ref):
    normed, _ = norm_rows(single_ref[...].astype(f32))
    cond_hat, _ = norm_rows(cond_ref[...].astype(f32))
    cond_low = (cond_hat * gain[...].astype(f32)).astype(bf16)
    gate = jax.nn.sigmoid(dot(cond_low, w_scale[...], NN) + b_scale[...].astype(f32))
    x_ref[...] = (gate * normed + dot(cond_low, w_shift[...], NN)).astype(bf16)


def adapt(single, cond, gain, w_scale, b_scale, w_shift):
    tokens, width = single.shape
    tile = tile_of(tokens)
    return pl.pallas_call(
        adapt_kernel,
        grid=(tokens // tile,),
        in_specs=[tiled(tile, width), tiled(tile, cond.shape[1])]
        + [fixed(v.shape) for v in (gain, w_scale, b_scale, w_shift)],
        out_specs=tiled(tile, width),
        out_shape=jax.ShapeDtypeStruct((tokens, width), bf16),
        compiler_params=pltpu.CompilerParams(vmem_limit_bytes=VMEM_BYTES),
        cost_estimate=pl.CostEstimate(
            flops=4 * tokens * width * cond.shape[1], bytes_accessed=8 * tokens * width, transcendentals=tokens * width
        ),
        name="adapt",
    )(single, cond, gain, w_scale, b_scale, w_shift)


def middle_kernel(
    meta, x_ref, single_ref, cond_ref, cot_ref, a0, a1, a2, a3,
    w_gate, w_out, w_ac, b_ac, gain, w_scale, b_scale, w_shift, w_hg, w_hu, w_dn, w_tc, b_tc,
    out_ref, dmid_ref, dxg_ref, da0, da1, da2, da3,
    g_gate, g_out, g_ac, g_scale, g_shift, g_hg, g_hu, g_dn, g_tc, s_ac, s_scale, s_tc, s_gain,
):
    core = meta[0] % 2

    @pl.when(pl.program_id(0) == 0)
    def _():
        for ref in (g_gate, g_out, g_ac, g_scale, g_shift, g_hg, g_hu, g_dn, g_tc, s_ac, s_scale, s_tc, s_gain):
            ref[...] = jnp.zeros_like(ref)

    x_one = x_ref[...]
    cond = cond_ref[...]
    gate = jax.nn.sigmoid(dot(x_one, w_gate[...], NN))
    first = core == 0
    att = jnp.concatenate(
        [
            jnp.where(first, a0[...], a1[...]),
            jnp.where(first, a1[...], a0[...]),
            jnp.where(first, a2[...], a3[...]),
            jnp.where(first, a3[...], a2[...]),
        ],
        axis=1,
    ).astype(f32)
    gated = (att * gate).astype(bf16)
    branch = dot(gated, w_out[...], NN)
    acond = jax.nn.sigmoid(dot(cond, w_ac[...], NN) + b_ac[...].astype(f32))
    mid = single_ref[...].astype(f32) + acond * branch
    cond_hat, _ = norm_rows(cond.astype(f32))
    cond_low = (cond_hat * gain[...].astype(f32)).astype(bf16)
    scale = jax.nn.sigmoid(dot(cond_low, w_scale[...], NN) + b_scale[...].astype(f32))
    normed, inverse = norm_rows(mid)
    x_two = (scale * normed + dot(cond_low, w_shift[...], NN)).astype(bf16)
    hgate = dot(x_two, w_hg[...], NN)
    hup = dot(x_two, w_hu[...], NN)
    sig = jax.nn.sigmoid(hgate)
    silu = hgate * sig
    hidden = (silu * hup).astype(bf16)
    tr_branch = dot(hidden, w_dn[...], NN)
    tcond = jax.nn.sigmoid(dot(cond, w_tc[...], NN) + b_tc[...].astype(f32))
    out_ref[...] = (mid + tcond * tr_branch).astype(bf16)
    dy = cot_ref[...].astype(f32)
    d_tr = (tcond * dy).astype(bf16)
    d_trc = dy * tr_branch * tcond * (1.0 - tcond)
    s_tc[...] += fold8(d_trc)
    g_tc[...] += dot(cond, d_trc.astype(bf16), TN)
    g_dn[...] += dot(hidden, d_tr, TN)
    d_hidden = dot(d_tr, w_dn[...], NT)
    d_hg = (d_hidden * hup * sig * (1.0 + hgate * (1.0 - sig))).astype(bf16)
    d_hu = (d_hidden * silu).astype(bf16)
    g_hg[...] += dot(x_two, d_hg, TN)
    g_hu[...] += dot(x_two, d_hu, TN)
    g_two = dot(d_hg, w_hg[...], NT) + dot(d_hu, w_hu[...], NT)
    d_scale = g_two * normed * scale * (1.0 - scale)
    s_scale[...] += fold8(d_scale)
    d_scale = d_scale.astype(bf16)
    d_shift = g_two.astype(bf16)
    g_scale[...] += dot(cond_low, d_scale, TN)
    g_shift[...] += dot(cond_low, d_shift, TN)
    d_cond = dot(d_scale, w_scale[...], NT) + dot(d_shift, w_shift[...], NT)
    s_gain[...] += fold8(d_cond * cond_hat)
    d_mid = dy + norm_back(normed, inverse, g_two * scale)
    dmid_ref[...] = d_mid
    d_attn = (acond * d_mid).astype(bf16)
    d_ac = d_mid * branch * acond * (1.0 - acond)
    s_ac[...] += fold8(d_ac)
    g_ac[...] += dot(cond, d_ac.astype(bf16), TN)
    g_out[...] += dot(gated, d_attn, TN)
    d_gated = dot(d_attn, w_out[...], NT)
    d_att = (d_gated * gate).astype(bf16)
    d_gate = (d_gated * att * gate * (1.0 - gate)).astype(bf16)
    g_gate[...] += dot(x_one, d_gate, TN)
    dxg_ref[...] = dot(d_gate, w_gate[...], NT).astype(bf16)
    q = d_att.shape[1] // 4
    parts = [d_att[:, i * q : (i + 1) * q] for i in range(4)]
    da0[...] = jnp.where(first, parts[0], parts[1])
    da1[...] = jnp.where(first, parts[1], parts[0])
    da2[...] = jnp.where(first, parts[2], parts[3])
    da3[...] = jnp.where(first, parts[3], parts[2])


def middle(meta, x_one, single, cond, cot, atts, weights):
    tokens, width = single.shape
    tile = tile_of(tokens)
    cs = cond.shape[1]
    quarter = atts[0].shape[1]
    w_gate, w_out, w_ac, b_ac, gain, w_scale, b_scale, w_shift, w_hg, w_hu, w_dn, w_tc, b_tc = weights
    total = lambda w: jax.ShapeDtypeStruct(w.shape, f32)
    fold = lambda n: jax.ShapeDtypeStruct((8, n), f32)
    grads = [total(w) for w in (w_gate, w_out, w_ac, w_scale, w_shift, w_hg, w_hu, w_dn, w_tc)] + [
        fold(width), fold(width), fold(width), fold(cs)]
    row_out = [((width,), bf16), ((width,), f32), ((width,), bf16)] + [((quarter,), bf16)] * 4
    macs = sum(w.size for w in weights if w.shape[0] > 1)
    return pl.pallas_call(
        middle_kernel,
        grid_spec=pltpu.PrefetchScalarGridSpec(
            num_scalar_prefetch=1,
            grid=(tokens // tile,),
            in_specs=[tiled(tile, width), tiled(tile, width), tiled(tile, cs), tiled(tile, width)]
            + [tiled(tile, quarter)] * 4
            + [fixed(w.shape) for w in weights],
            out_specs=[tiled(tile, w[0]) for w, _ in row_out] + [fixed(g.shape) for g in grads],
        ),
        out_shape=[jax.ShapeDtypeStruct((tokens, w[0]), d) for w, d in row_out] + grads,
        compiler_params=pltpu.CompilerParams(vmem_limit_bytes=VMEM_BYTES),
        cost_estimate=pl.CostEstimate(flops=6 * tokens * macs, bytes_accessed=60 << 20, transcendentals=8 * tokens * width),
        name="middle",
    )(meta, x_one, single, cond, cot, *atts, *weights)


def last_kernel(d0, d1, d2, d3, single_ref, cond_ref, dmid_ref, gain, w_scale, b_scale, w_shift,
                out_ref, g_scale, g_shift, s_scale, s_gain):
    @pl.when(pl.program_id(0) == 0)
    def _():
        for ref in (g_scale, g_shift, s_scale, s_gain):
            ref[...] = jnp.zeros_like(ref)

    g_one = d0[...].astype(f32) + d1[...].astype(f32) + d2[...].astype(f32) + d3[...].astype(f32)
    normed, inverse = norm_rows(single_ref[...].astype(f32))
    cond_hat, _ = norm_rows(cond_ref[...].astype(f32))
    cond_low = (cond_hat * gain[...].astype(f32)).astype(bf16)
    scale = jax.nn.sigmoid(dot(cond_low, w_scale[...], NN) + b_scale[...].astype(f32))
    d_scale = g_one * normed * scale * (1.0 - scale)
    s_scale[...] += fold8(d_scale)
    d_scale = d_scale.astype(bf16)
    d_shift = g_one.astype(bf16)
    g_scale[...] += dot(cond_low, d_scale, TN)
    g_shift[...] += dot(cond_low, d_shift, TN)
    d_cond = dot(d_scale, w_scale[...], NT) + dot(d_shift, w_shift[...], NT)
    s_gain[...] += fold8(d_cond * cond_hat)
    out_ref[...] = dmid_ref[...] + norm_back(normed, inverse, g_one * scale)


def last(ds, single, cond, dmid, gain, w_scale, b_scale, w_shift):
    tokens, width = single.shape
    tile = tile_of(tokens)
    cs = cond.shape[1]
    grads = [jax.ShapeDtypeStruct(s, f32) for s in (w_scale.shape, w_shift.shape, (8, width), (8, cs))]
    return pl.pallas_call(
        last_kernel,
        grid=(tokens // tile,),
        in_specs=[tiled(tile, width)] * 5
        + [tiled(tile, cs), tiled(tile, width)]
        + [fixed(w.shape) for w in (gain, w_scale, b_scale, w_shift)],
        out_specs=[tiled(tile, width)] + [fixed(g.shape) for g in grads],
        out_shape=[jax.ShapeDtypeStruct((tokens, width), f32)] + grads,
        compiler_params=pltpu.CompilerParams(vmem_limit_bytes=VMEM_BYTES),
        cost_estimate=pl.CostEstimate(flops=12 * tokens * width * cs, bytes_accessed=30 << 20, transcendentals=tokens * width),
        name="last",
    )(*ds, single, cond, dmid, gain, w_scale, b_scale, w_shift)


def swap(value, bit):
    size = lax.axis_size("head")
    return lax.ppermute(value, "head", [(i, i ^ bit) for i in range(size)])


def on_device(
    single,
    cond,
    pair,
    complex_length,
    sample_complex,
    cotangent,
    gain_one,
    w_scale_one,
    b_scale_one,
    w_shift_one,
    w_query,
    b_query,
    w_key,
    w_value,
    w_gate,
    w_out,
    w_pair,
    w_attn_cond,
    b_attn_cond,
    gain_two,
    w_scale_two,
    b_scale_two,
    w_shift_two,
    w_hidden_gate,
    w_hidden_up,
    w_hidden_down,
    w_tr_cond,
    b_tr_cond,
):
    groups = lax.axis_size("head")
    devices = lax.axis_size("samp")
    me = lax.axis_index("head")
    core = me % 2
    part = me // 2
    samples, rows, width = single.shape
    cs = cond.shape[2]
    tokens = samples * rows
    length = rows * groups
    heads = w_pair.shape[1]
    few = heads // groups
    dim = width // heads
    wide = few * dim
    complexes, _, columns, _ = pair.shape
    chunks = 2 * groups
    chunk = length // chunks

    pair_normed, pair_inverse = norm_rows(pair.astype(f32))
    pair_low = pair_normed.astype(bf16)
    bias = jnp.einsum("cijz,zh->chji", pair_low, w_pair, preferred_element_type=f32)
    column = lax.axis_index("samp") * columns + jnp.arange(columns)
    valid = column[None, :] < complex_length[:, None]
    bias = jnp.where(valid[:, None, :, None], bias * LOG2E, fill_value).astype(bf16)
    bias = bias.reshape(complexes, groups // 2, 2, few, columns, rows)
    mine = lax.dynamic_index_in_dim(bias, core, 2, keepdims=False)
    other = lax.dynamic_index_in_dim(bias, 1 - core, 2, keepdims=False)
    bias_rows = jnp.concatenate([mine, swap(other, 1)], axis=-1)

    def regroup(gathered):
        if columns == chunk:
            return gathered
        moved = gathered.transpose(1, 2, 0, 3, 4).reshape(complexes, few, chunks, chunk, 2 * rows)
        return moved.transpose(2, 0, 1, 3, 4)

    def ungroup(summed):
        if columns == chunk:
            return summed
        moved = summed.transpose(1, 2, 0, 3, 4).reshape(complexes, few, devices, columns, 2 * rows)
        return moved.transpose(2, 0, 1, 3, 4)

    biases = [regroup(lax.all_gather(bias_rows[:, k], "samp", axis=0)) for k in range(groups // 2)]

    single_t = single.reshape(tokens, width)
    cond_t = cond.reshape(tokens, cs)
    cot_t = cotangent.reshape(tokens, width)
    line = lambda v: v.reshape(1, -1)
    x_one = adapt(single_t, cond_t, line(gain_one), w_scale_one, line(b_scale_one), w_shift_one)
    x_far = swap(x_one, 2)
    x_near = swap(x_one, 1)
    x_cross = swap(x_far, 1)
    blocks = [v.reshape(samples, rows, width) for v in (x_one, x_near, x_far, x_cross)]

    meta = jnp.concatenate([me[None].astype(jnp.int32), sample_complex])

    def own_columns(w, k):
        return lax.dynamic_slice_in_dim(w, (2 * k + core) * wide, wide, w.ndim - 1)

    w_heads = [
        jnp.concatenate([own_columns(w, k).T for w in (w_query, w_key, w_value)], axis=0) for k in range(groups // 2)
    ]
    b_heads = [own_columns(b_query.astype(f32), k)[:, None] for k in range(groups // 2)]
    kept = [attend(meta, blocks, w_heads[k], b_heads[k], biases[k], nh=few, hd=dim) for k in range(groups // 2)]
    atts = []
    for k in range(groups // 2):
        out = kept[k][0]
        atts += [out[0].reshape(tokens, wide), swap(out[1], 1).reshape(tokens, wide)]

    (
        block_out, d_mid, d_xg, da0, da1, da2, da3,
        g_gate, g_out, g_ac, g_scale2, g_shift2, g_hg, g_hu, g_dn, g_tc, s_ac, s_scale2, s_tc, s_gain2,
    ) = middle(
        meta, x_one, single_t, cond_t, cot_t, atts,
        (w_gate, w_out, w_attn_cond, line(b_attn_cond), line(gain_two), w_scale_two, line(b_scale_two), w_shift_two,
         w_hidden_gate, w_hidden_up, w_hidden_down, w_tr_cond, line(b_tr_cond)),
    )

    shape = (samples, rows, wide)
    d_x = None
    bias_grads, w_grads, q_grads = [], [], []
    for k, (own, sent) in enumerate(((da0, da1), (da2, da3))):
        out, probs, q, key, value, total = kept[k]
        d_x, db, gw, gb = attend_back(
            meta, blocks, w_heads[k], probs, q, key, value, total, out, own.reshape(shape), swap(sent, 1).reshape(shape),
            d_x, chunks, complexes, nh=few, hd=dim)
        bias_grads.append(lax.psum_scatter(ungroup(db), "samp", scatter_dimension=0, tiled=False))
        w_grads.append(gw)
        q_grads.append(gb)

    near = swap(jnp.stack([d_x[3], d_x[1]]), 1)
    far = swap(d_x[2] + near[0], 2)
    flat = lambda v: v.reshape(tokens, width)
    grad_single, g_scale1, g_shift1, s_scale1, s_gain1 = last(
        (flat(d_x[0]), flat(near[1]), flat(far), d_xg), single_t, cond_t, d_mid,
        line(gain_one), w_scale_one, line(b_scale_one), w_shift_one,
    )

    db = jnp.stack(bias_grads, axis=1)
    own, sent = db[..., :rows], db[..., rows:]
    other = swap(sent, 1)
    first = core == 0
    db = jnp.stack([jnp.where(first, own, other), jnp.where(first, other, own)], axis=2)
    db = db.reshape(complexes, heads, columns, rows)
    grad_pair_weight = jnp.einsum("cijz,chji->zh", pair_low, db, preferred_element_type=f32)
    d_pair_norm = jnp.einsum("chji,zh->cijz", db, w_pair, preferred_element_type=f32)
    grad_pair = norm_back(pair_normed, pair_inverse, d_pair_norm)

    def total(stack):
        part_sum = lax.psum_scatter(stack.astype(bf16), "head", scatter_dimension=2, tiled=True).astype(f32)
        return lax.psum_scatter(part_sum, "samp", scatter_dimension=0, tiled=True)

    r_down = total(g_dn[:, None])
    r_hidden = total(jnp.stack([g_hg, g_hu], axis=1))
    r_square = total(jnp.stack([g_out, g_gate], axis=1))
    r_cond = total(jnp.stack([g_tc, g_ac, g_scale2, g_shift2], axis=1))
    r_cond1 = total(jnp.stack([g_scale1, g_shift1], axis=1))
    keep = jnp.where(part == 0, w_grads[0], w_grads[1])
    send = jnp.where(part == 0, w_grads[1], w_grads[0])
    r_heads = keep + swap(send.astype(bf16), 2).astype(f32)
    r_heads = lax.psum_scatter(r_heads.T, "samp", scatter_dimension=0, tiled=True)

    q_full = jnp.zeros((groups, wide), f32)
    for k in range(groups // 2):
        q_full = lax.dynamic_update_index_in_dim(q_full, q_grads[k][:, 0], 2 * k + core, 0)
    column_sum = lambda v: jnp.sum(v, axis=0)
    small = lax.psum(
        (
            grad_pair_weight,
            column_sum(s_gain1),
            column_sum(s_gain2),
            column_sum(s_scale1),
            q_full.reshape(-1),
            column_sum(s_ac),
            column_sum(s_scale2),
            column_sum(s_tc),
        ),
        ("samp", "head"),
    )
    whole = (samples, rows, width)
    return (
        block_out.reshape(whole),
        grad_single.reshape(whole),
        grad_pair,
        small[1],
        r_cond1[:, 0],
        small[3],
        r_cond1[:, 1],
        r_heads[:, :wide],
        small[4],
        r_heads[:, wide : 2 * wide],
        r_heads[:, 2 * wide :],
        r_square[:, 1],
        r_square[:, 0],
        small[0],
        r_cond[:, 1],
        small[5],
        small[2],
        r_cond[:, 2],
        small[6],
        r_cond[:, 3],
        r_hidden[:, 0],
        r_hidden[:, 1],
        r_down[:, 0],
        r_cond[:, 0],
        small[7],
    )


def solution(mesh):
    placed = (
        P("samp", "head", None),
        P("samp", "head", None),
        P(None, "head", "samp", None),
        P(),
        P("samp"),
        P("samp", "head", None),
        P(),
        P(),
        P(),
        P(),
        P(),
        P(),
        P(),
        P(),
        P(),
        P(),
        P(),
        P(),
        P(),
        P(),
        P(),
        P(),
        P(),
        P(),
        P(),
        P(),
        P(),
        P(),
    )
    return jax.shard_map(
        on_device,
        mesh=mesh,
        in_specs=placed,
        out_specs=(
            P("samp", "head", None),
            P("samp", "head", None),
            P(None, "head", "samp", None),
            P(),
            P("samp", "head"),
            P(),
            P("samp", "head"),
            P("samp", "head"),
            P(),
            P("samp", "head"),
            P("samp", "head"),
            P("samp", "head"),
            P("samp", "head"),
            P(),
            P("samp", "head"),
            P(),
            P(),
            P("samp", "head"),
            P(),
            P("samp", "head"),
            P("samp", "head"),
            P("samp", "head"),
            P("samp", "head"),
            P("samp", "head"),
            P(),
        ),
        check_vma=False,
    )
```

```python
import functools
import math

import jax
import jax.numpy as jnp
from jax import lax
from jax.experimental import pallas as pl
from jax.experimental.pallas import tpu as pltpu
from jax.sharding import PartitionSpec as P

f32, bf16 = jnp.float32, jnp.bfloat16
epsilon = 1e-05
fill_value = -1e30
LOG2E = math.log2(math.e)
VMEM_BYTES = 60 << 20
PAIR_LINES = (8, 16, 24, 32, 64)
NN, NT, TN = ((1,), (0,)), ((1,), (1,)), ((0,), (0,))


def dot(a, b, dims):
    return lax.dot_general(a, b, (dims, ((), ())), preferred_element_type=f32)


def norm_rows(inputs):
    mean_val = jnp.mean(inputs, axis=-1, keepdims=True)
    centered = inputs - mean_val
    variance = jnp.mean(centered * centered, axis=-1, keepdims=True)
    inverse = lax.rsqrt(variance + epsilon)
    return (centered * inverse, inverse)


def norm_back(normed, inverse, upstream):
    mean_grad = jnp.mean(upstream, axis=-1, keepdims=True)
    mean_dot = jnp.mean(upstream * normed, axis=-1, keepdims=True)
    return inverse * (upstream - mean_grad - normed * mean_dot)


def tile_of(tokens, sizes=(8, 16, 32, 64, 128, 256)):
    return max(t for t in sizes if tokens % t == 0)


def fixed(shape):
    return pl.BlockSpec(shape, lambda *_: (0,) * len(shape), pipeline_mode=pl.Buffered(1))


META = 6


def attend_kernel(meta, x0, x1, x2, x3, w_ref, bq_ref, *rest, nh, hd, rows, jc, nchunk, qscale):
    bias_hbm = rest[:nchunk]
    o_ref, p_ref, q_ref, k_ref, v_ref, l_ref, xs, ks, ss, bias_ref, sems = rest[nchunk:]
    b = pl.program_id(0)
    g = meta[0]
    cplx = meta[META + b]
    per_block = nchunk // 4

    def copies():
        return [
            pltpu.make_async_copy(bias_hbm[i], bias_ref.at[meta[META + pl.num_programs(0) + i]], sems.at[i])
            for i in range(nchunk)
        ]

    @pl.when(b == 0)
    def _():
        for copy in copies():
            copy.start()

    for r, x in enumerate((x0, x1, x2, x3)):
        xs[r * rows : (r + 1) * rows, :] = x[0]
    wch = nh * hd
    q = dot(w_ref[0:wch, :], xs[0 : 2 * rows, :], NT) + bq_ref[...]
    q_ref[0] = (q * qscale).astype(bf16)
    kv = dot(w_ref[wch : 3 * wch, :], xs[...], NT).astype(bf16)
    k_ref[0] = kv[0:wch]
    v_ref[0] = kv[wch:]

    @pl.when(b == 0)
    def _():
        for copy in copies():
            copy.wait()

    ones = jnp.ones((16, kv.shape[1]), bf16)
    outs = []
    sums = []
    for h in range(nh):
        ks[h % 2, :, :] = jnp.transpose(k_ref[0, h * hd : (h + 1) * hd, :])
        qT = q_ref[0, h * hd : (h + 1) * hd, :]
        m = None
        for t in range(nchunk):
            r, u = t // per_block, t % per_block
            s_idx = (r ^ g) * per_block + u
            s = dot(ks[h % 2, t * jc : (t + 1) * jc, :], qT, NN) + bias_ref[s_idx, cplx, h].astype(f32)
            ss[h % 2, t * jc : (t + 1) * jc, :] = s
            mt = jnp.max(s.reshape(jc // 8, 8, s.shape[1]), axis=0)
            m = mt if m is None else jnp.maximum(m, mt)
        m = jnp.max(m, axis=0, keepdims=True)
        for t in range(nchunk):
            part = slice(t * jc, (t + 1) * jc)
            p_ref[0, h, part, :] = jnp.exp2(ss[h % 2, part, :] - m).astype(bf16)
        va = jnp.concatenate([v_ref[0, h * hd : (h + 1) * hd, :], ones], axis=0)
        oT = dot(va, p_ref[0, h], NN)
        l = oT[hd : hd + 1, :]
        outs.append(oT[:hd] / l)
        sums.append(l)
    l_ref[0] = jnp.concatenate(sums, axis=0)
    o = jnp.transpose(jnp.concatenate(outs, axis=0)).astype(bf16)
    o_ref[0, 0] = o[:rows]
    o_ref[1, 0] = o[rows:]


def attend(meta, xb, wT, bq, biases, *, nh, hd):
    B, rows, C = xb[0].shape
    nchunk = len(biases)
    ncx, _, jc, qi = biases[0].shape
    L = nchunk * jc
    wch = nh * hd
    kern = functools.partial(
        attend_kernel, nh=nh, hd=hd, rows=rows, jc=jc, nchunk=nchunk, qscale=LOG2E / math.sqrt(hd)
    )
    xspec = pl.BlockSpec((1, rows, C), lambda b, m: (b, 0, 0))
    per = lambda shape: pl.BlockSpec((1,) + shape, lambda b, m: (b,) + (0,) * len(shape))
    return pl.pallas_call(
        kern,
        grid_spec=pltpu.PrefetchScalarGridSpec(
            num_scalar_prefetch=1,
            grid=(B,),
            in_specs=[xspec] * 4
            + [fixed(wT.shape), fixed(bq.shape)]
            + [pl.BlockSpec(memory_space=pl.ANY)] * nchunk,
            out_specs=[
                pl.BlockSpec((2, 1, rows, wch), lambda b, m: (0, b, 0, 0)),
                per((nh, L, qi)),
                per((wch, qi)),
                per((wch, L)),
                per((wch, L)),
                per((nh, qi)),
            ],
            scratch_shapes=[
                pltpu.VMEM((L, C), bf16),
                pltpu.VMEM((2, L, hd), bf16),
                pltpu.VMEM((2, L, qi), f32),
                pltpu.VMEM((nchunk, ncx, nh, jc, qi), bf16),
                pltpu.SemaphoreType.DMA((nchunk,)),
            ],
        ),
        out_shape=[
            jax.ShapeDtypeStruct((2, B, rows, wch), bf16),
            jax.ShapeDtypeStruct((B, nh, L, qi), bf16),
            jax.ShapeDtypeStruct((B, wch, qi), bf16),
            jax.ShapeDtypeStruct((B, wch, L), bf16),
            jax.ShapeDtypeStruct((B, wch, L), bf16),
            jax.ShapeDtypeStruct((B, nh, qi), f32),
        ],
        compiler_params=pltpu.CompilerParams(vmem_limit_bytes=VMEM_BYTES),
        cost_estimate=pl.CostEstimate(
            flops=12 * B * nh * L * qi * 256 // 3, bytes_accessed=60 << 20, transcendentals=B * nh * L * qi
        ),
        name="attend",
    )(meta, *xb, wT, bq, *biases)


def attend_back_kernel(
    meta, x0, x1, x2, x3, w_ref, p_ref, q_ref, k_ref, v_ref, l_ref, o_ref, do0, do1, *rest,
    nh, hd, rows, jc, nchunk, scale, chained, fast,
):
    before = rest[0] if chained else None
    rest = rest[1:] if chained else rest
    if fast:
        dx_ref, gw_out, gb_ref = rest[:3]
        sends, keeps = rest[3:7], rest[7:11]
        xs, vs, ds, acc, dst, gw_ref, gt = rest[11:]
    else:
        dx_ref, db_ref, gw_ref, gb_ref, xs, vs, ds, acc, dst = rest
    b = pl.program_id(0)
    g = meta[0]
    cplx = meta[META + b]
    per_block = nchunk // 4
    wch = nh * hd
    L = nchunk * jc

    @pl.when(b == 0)
    def _():
        acc[...] = jnp.zeros_like(acc)
        gw_ref[...] = jnp.zeros_like(gw_ref)
        gb_ref[...] = jnp.zeros_like(gb_ref)

    for r, x in enumerate((x0, x1, x2, x3)):
        xs[r * rows : (r + 1) * rows, :] = x[0]
    dO = jnp.transpose(jnp.concatenate([do0[0], do1[0]], axis=0).astype(f32))
    O = jnp.transpose(jnp.concatenate([o_ref[0, 0], o_ref[1, 0]], axis=0).astype(f32))
    prod = dO * O
    qi = dO.shape[1]
    row = lax.broadcasted_iota(jnp.int32, (16, qi), 0)
    ones = jnp.ones((16, L), bf16)
    for h in range(nh):
        hs = slice(h * hd, (h + 1) * hd)
        linv = 1.0 / l_ref[0, h : h + 1, :]
        dOh = (dO[hs] * linv).astype(bf16)
        delta = jnp.sum(prod[hs], axis=0, keepdims=True) * linv
        hi = delta.astype(bf16).astype(f32)
        extra = jnp.where(row == 0, -hi, jnp.where(row == 1, hi - delta, 0.0)).astype(bf16)
        dOa = jnp.concatenate([dOh, extra], axis=0)
        vs[h % 2] = jnp.transpose(jnp.concatenate([v_ref[0, hs, :], ones], axis=0))
        for t in range(nchunk):
            r, u = t // per_block, t % per_block
            s_idx = (r ^ g) * per_block + u
            ts = slice(t * jc, (t + 1) * jc)
            d = dot(vs[h % 2, ts, :], dOa, NN) * p_ref[0, h, ts, :].astype(f32)
            acc[s_idx, cplx, h] += d
            ds[h % 2, ts, :] = d.astype(bf16)
        dst[h * hd : (h + 1) * hd, 0:qi] = (dot(k_ref[0, hs, :], ds[h % 2], NN) * scale).astype(bf16)
        dk = dot(q_ref[0, hs, :], ds[h % 2], NT) * (1.0 / LOG2E)
        dst[wch + h * hd : wch + (h + 1) * hd, :] = dk.astype(bf16)
        dst[2 * wch + h * hd : 2 * wch + (h + 1) * hd, :] = dot(dOh, p_ref[0, h], NT).astype(bf16)
    dq = dst[0:wch, 0:qi]
    gb_ref[...] += jnp.sum(dq.astype(f32), axis=1, keepdims=True)
    gw_ref[0:wch, :] += dot(dq, xs[0:qi, :], NN)
    gw_ref[wch:, :] += dot(dst[wch:, :], xs[...], NN)
    dkv = jnp.transpose(dst[wch:, :])
    dqr = jnp.transpose(dq)
    for r in range(4):
        rs = slice(r * rows, (r + 1) * rows)
        dx = dot(dkv[rs], w_ref[wch:, :], NN)
        if r < 2:
            dx += dot(dqr[rs], w_ref[0:wch, :], NN)
        if chained:
            dx += before[r, 0].astype(f32)
        dx_ref[r, 0] = dx.astype(bf16)

    @pl.when(b == pl.num_programs(0) - 1)
    def _():
        if fast:
            for i in range(4):
                keeps[i][...] = acc[meta[2 + i] * 2 + meta[1]].astype(bf16)
                sends[i][...] = acc[meta[2 + i] * 2 + 1 - meta[1]].astype(bf16)
            gt[...] = jnp.transpose(gw_ref[...])
            n = gt.shape[0] // 8
            for i in range(4):
                for e in range(2):
                    start = pl.multiple_of((meta[2 + i] * 2 + (meta[1] ^ e)) * n, n)
                    gw_out[2 * i + e] = gt[pl.ds(start, n), :].astype(bf16)
        else:
            db_ref[...] = acc[...].astype(bf16)


def attend_back(meta, xb, wT, p, q, k, v, l, o, do0, do1, before, nchunk, ncx, *, nh, hd, fast):
    B, rows, C = xb[0].shape
    L = k.shape[2]
    qi = q.shape[2]
    jc = L // nchunk
    wch = nh * hd
    kern = functools.partial(
        attend_back_kernel, nh=nh, hd=hd, rows=rows, jc=jc, nchunk=nchunk, scale=1.0 / math.sqrt(hd),
        chained=before is not None, fast=fast)
    xspec = pl.BlockSpec((1, rows, C), lambda b, m: (b, 0, 0))
    per = lambda shape: pl.BlockSpec((1,) + shape, lambda b, m: (b,) + (0,) * len(shape))
    db = (nchunk, ncx, nh, jc, qi)
    block = pl.BlockSpec((4, 1, rows, C), lambda b, m: (0, b, 0, 0))
    extra = () if before is None else (before,)
    if fast:
        outs = [((8, C // 8, 3 * wch), bf16), ((wch, 1), f32)] + [(db[1:], bf16)] * 8
        more = [pltpu.VMEM((3 * wch, C), f32), pltpu.VMEM((C, 3 * wch), f32)]
    else:
        outs = [(db, bf16), ((3 * wch, C), f32), ((wch, 1), f32)]
        more = []
    return pl.pallas_call(
        kern,
        grid_spec=pltpu.PrefetchScalarGridSpec(
            num_scalar_prefetch=1,
            grid=(B,),
            in_specs=[xspec] * 4
            + [fixed(wT.shape), per((nh, L, qi)), per((wch, qi)), per((wch, L)), per((wch, L)), per((nh, qi))]
            + [pl.BlockSpec((2, 1, rows, wch), lambda b, m: (0, b, 0, 0)), per((rows, wch)), per((rows, wch))]
            + [block] * len(extra),
            out_specs=[block] + [fixed(s) for s, _ in outs],
            scratch_shapes=[
                pltpu.VMEM((L, C), bf16),
                pltpu.VMEM((2, L, hd + 16), bf16),
                pltpu.VMEM((2, L, qi), bf16),
                pltpu.VMEM(db, f32),
                pltpu.VMEM((3 * wch, L), bf16),
            ]
            + more,
        ),
        out_shape=[jax.ShapeDtypeStruct((4, B, rows, C), bf16)] + [jax.ShapeDtypeStruct(s, d) for s, d in outs],
        compiler_params=pltpu.CompilerParams(vmem_limit_bytes=VMEM_BYTES),
        cost_estimate=pl.CostEstimate(
            flops=8 * B * nh * L * qi * 256, bytes_accessed=60 << 20, transcendentals=0
        ),
        name="attend_back",
    )(meta, *xb, wT, p, q, k, v, l, o, do0, do1, *extra)


def blocked(w, count):
    across, heads = w.shape
    wide = jnp.tile(jnp.transpose(w), (count, count))
    row = lax.broadcasted_iota(jnp.int32, wide.shape, 0) // heads
    column = lax.broadcasted_iota(jnp.int32, wide.shape, 1) // across
    return jnp.where(row == column, wide, jnp.zeros_like(wide))


def pair_bias_kernel(meta, lens, pair_ref, wb_ref, low_ref, inv_ref, raw_ref, *rest, few, blocks, group):
    outs, scr = rest[:-1], rest[-1]
    c, t = pl.program_id(0), pl.program_id(1)
    lines, columns, cz = pair_ref.shape[1:]
    heads = few * blocks
    per = lines // group
    mean = jnp.full((cz, cz), 1.0 / cz, bf16)
    lane = lax.broadcasted_iota(jnp.int32, (columns, group * heads), 1) // heads
    table = []
    for n in range(per):
        x = [pair_ref[0, n * group + i] for i in range(group)]
        flat = columns % 16 == 0
        if flat:
            x = [jnp.concatenate(x, axis=0)]
        lows, inverses = [], []
        for v in x:
            centered = v.astype(f32) - dot(v, mean, NN)
            inverse = lax.rsqrt(dot((centered * centered).astype(bf16), mean, NN) + epsilon)
            lows.append((centered * inverse).astype(bf16))
            inverses.append(inverse)
        if flat:
            lows = [lows[0][i * columns : (i + 1) * columns] for i in range(group)]
            inverses = [inverses[0][i * columns : (i + 1) * columns] for i in range(group)]
        spread = inverses[0][:, : group * heads]
        for i in range(1, group):
            spread = jnp.where(lane == i, inverses[i][:, : group * heads], spread)
        inv_ref[0, n] = spread
        for i in range(group):
            low_ref[0, n * group + i] = lows[i]
        table.append(jnp.concatenate(lows, axis=1))
    out = dot(jnp.concatenate(table, axis=0), wb_ref[...], NT)
    for n in range(per):
        part = out[n * columns : (n + 1) * columns]
        raw_ref[0, n] = part
        start = pl.multiple_of((t * per + n) * group * heads, group * heads)
        scr[pl.ds(start, group * heads), :] = jnp.transpose(part)

    @pl.when(t == pl.num_programs(1) - 1)
    def _():
        core = meta[0] % 2
        rows = scr.shape[0] // heads
        place = lax.broadcasted_iota(jnp.int32, (columns, rows), 0) + meta[1] * columns
        valid = place < lens[c]
        half = len(outs) // 2
        for k in range(half):
            for f in range(few):
                for e in range(2):
                    h = (2 * k + (core ^ e)) * few + f
                    v = jnp.transpose(scr[pl.ds(h, rows, stride=heads), :])
                    outs[e * half + k][0, f] = jnp.where(valid, v * LOG2E, fill_value).astype(bf16)


def pair_specs(pair, heads, group):
    lines = tile_of(pair.shape[1], PAIR_LINES)
    columns, cz = pair.shape[2:]
    return (
        lines,
        pl.BlockSpec((1, lines, columns, cz), lambda c, t, *_: (c, t, 0, 0)),
        pl.BlockSpec((1, lines // group, columns, group * heads), lambda c, t, *_: (c, t, 0, 0)),
        jax.ShapeDtypeStruct((pair.shape[0], pair.shape[1] // group, columns, group * heads), f32),
    )


def pair_bias(meta, lens, pair, wb, *, few, blocks, group):
    ncx, rows, columns, cz = pair.shape
    heads = few * blocks
    lines, spec, thin, thin_shape = pair_specs(pair, heads, group)
    out = jax.ShapeDtypeStruct((ncx, few, columns, rows), bf16)
    return pl.pallas_call(
        functools.partial(pair_bias_kernel, few=few, blocks=blocks, group=group),
        grid_spec=pltpu.PrefetchScalarGridSpec(
            num_scalar_prefetch=2,
            grid=(ncx, rows // lines),
            in_specs=[spec, fixed(wb.shape)],
            out_specs=[spec, thin, thin]
            + [pl.BlockSpec((1, few, columns, rows), lambda c, t, *_: (c, 0, 0, 0))] * blocks,
            scratch_shapes=[pltpu.VMEM((rows * heads, columns), f32)],
        ),
        out_shape=[jax.ShapeDtypeStruct(pair.shape, bf16), thin_shape, thin_shape] + [out] * blocks,
        compiler_params=pltpu.CompilerParams(vmem_limit_bytes=VMEM_BYTES),
        cost_estimate=pl.CostEstimate(flops=1000 * pair.size, bytes_accessed=5 * pair.size, transcendentals=0),
        name="pair_bias",
    )(meta, lens, pair, wb)


def pair_back_kernel(meta, low_ref, inv_ref, raw_ref, w2_ref, mean_ref, *rest, few, blocks, group):
    grads = rest[:blocks]
    out_ref, gw_ref, scr, acc = rest[blocks:]
    c, t = pl.program_id(0), pl.program_id(1)
    lines, columns, cz = low_ref.shape[1:]
    heads = few * blocks
    per = lines // group

    @pl.when((c == 0) & (t == 0))
    def _():
        acc[...] = jnp.zeros_like(acc)

    @pl.when(t == 0)
    def _():
        core = meta[0] % 2
        rows = scr.shape[0] // heads
        half = blocks // 2
        for k in range(half):
            for f in range(few):
                for e in range(2):
                    h = (2 * k + (core ^ e)) * few + f
                    scr[pl.ds(h, rows, stride=heads), :] = jnp.transpose(grads[e * half + k][0, f].astype(f32))

    ds, prods, xs = [], [], []
    for n in range(per):
        start = pl.multiple_of((t * per + n) * group * heads, group * heads)
        x = jnp.transpose(scr[pl.ds(start, group * heads), :])
        d = x * inv_ref[0, n]
        prod = d * raw_ref[0, n]
        hi = prod.astype(bf16)
        d = d.astype(bf16)
        xs.append(x.astype(bf16))
        ds.append(jnp.concatenate([d, d], axis=1))
        prods.append(jnp.concatenate([hi, (prod - hi.astype(f32)).astype(bf16)], axis=1))
    upstream = dot(jnp.concatenate(ds, axis=0), w2_ref[...], NN)
    along = dot(jnp.concatenate(prods, axis=0), mean_ref[...], NN)
    table = []
    for n in range(per):
        lows = [low_ref[0, n * group + i] for i in range(group)]
        ns = slice(n * columns, (n + 1) * columns)
        for i in range(group):
            zs = slice(i * cz, (i + 1) * cz)
            out_ref[0, n * group + i] = upstream[ns, zs] - lows[i].astype(f32) * along[ns, zs]
        table.append(jnp.concatenate(lows, axis=1))
    acc[...] += dot(jnp.concatenate(xs, axis=0), jnp.concatenate(table, axis=0), TN)

    @pl.when((c == pl.num_programs(0) - 1) & (t == pl.num_programs(1) - 1))
    def _():
        total = acc[0:heads, 0:cz]
        for i in range(1, group):
            total += acc[i * heads : (i + 1) * heads, i * cz : (i + 1) * cz]
        gw_ref[...] = total


def pair_back(meta, low, inv, raw, w, grads, *, few, blocks, group):
    ncx, rows, columns, cz = low.shape
    heads = few * blocks
    lines, spec, thin, _ = pair_specs(low, heads, group)
    mean = jnp.mean(w.astype(f32), axis=0, keepdims=True)
    w2 = jnp.concatenate([blocked(w, group), blocked(jnp.broadcast_to(-mean, w.shape).astype(bf16), group)], axis=0)
    ones = blocked(jnp.full(w.shape, 1.0 / cz, bf16), group)
    ones = jnp.concatenate([ones, ones], axis=0)
    return pl.pallas_call(
        functools.partial(pair_back_kernel, few=few, blocks=blocks, group=group),
        grid_spec=pltpu.PrefetchScalarGridSpec(
            num_scalar_prefetch=1,
            grid=(ncx, rows // lines),
            in_specs=[spec, thin, thin, fixed(w2.shape), fixed(ones.shape)]
            + [pl.BlockSpec((1, few, columns, rows), lambda c, t, *_: (c, 0, 0, 0))] * blocks,
            out_specs=[spec, fixed((heads, cz))],
            scratch_shapes=[pltpu.VMEM((rows * heads, columns), f32), pltpu.VMEM((group * heads, group * cz), f32)],
        ),
        out_shape=[jax.ShapeDtypeStruct(low.shape, f32), jax.ShapeDtypeStruct((heads, cz), f32)],
        compiler_params=pltpu.CompilerParams(vmem_limit_bytes=VMEM_BYTES),
        cost_estimate=pl.CostEstimate(flops=1000 * low.size, bytes_accessed=8 * low.size, transcendentals=0),
        name="pair_back",
    )(meta, low, inv, raw, w2, ones, *grads)


def fold8(v):
    return jnp.sum(v.reshape(v.shape[0] // 8, 8, v.shape[1]), axis=0)


def fold1(ref):
    return jnp.sum(ref[...], axis=0, keepdims=True)


def tiled(rows, width, steps):
    return pl.BlockSpec((rows, width), lambda t, *_: (jnp.minimum(t, steps - 1), 0))


def adapt_kernel(single_ref, cond_ref, gain, w_scale, b_scale, w_shift, x_ref):
    normed, _ = norm_rows(single_ref[...].astype(f32))
    cond_hat, _ = norm_rows(cond_ref[...].astype(f32))
    cond_low = (cond_hat * gain[...].astype(f32)).astype(bf16)
    gate = jax.nn.sigmoid(dot(cond_low, w_scale[...], NN) + b_scale[...].astype(f32))
    x_ref[...] = (gate * normed + dot(cond_low, w_shift[...], NN)).astype(bf16)


def adapt(single, cond, gain, w_scale, b_scale, w_shift):
    tokens, width = single.shape
    tile = tile_of(tokens)
    steps = tokens // tile
    return pl.pallas_call(
        adapt_kernel,
        grid=(steps,),
        in_specs=[tiled(tile, width, steps), tiled(tile, cond.shape[1], steps)]
        + [fixed(v.shape) for v in (gain, w_scale, b_scale, w_shift)],
        out_specs=tiled(tile, width, steps),
        out_shape=jax.ShapeDtypeStruct((tokens, width), bf16),
        compiler_params=pltpu.CompilerParams(vmem_limit_bytes=VMEM_BYTES),
        cost_estimate=pl.CostEstimate(
            flops=4 * tokens * width * cond.shape[1], bytes_accessed=8 * tokens * width, transcendentals=tokens * width
        ),
        name="adapt",
    )(single, cond, gain, w_scale, b_scale, w_shift)


def emit_rows(meta, step, count):
    place = meta[2 + step // 2] * 2 + (meta[1] ^ (step % 2))
    return pl.ds(pl.multiple_of(place * count, count), count)


def middle_kernel(
    meta, x_ref, single_ref, cond_ref, cot_ref, a0, a1, a2, a3,
    w_gate, w_out, w_ac, b_ac, gain, w_scale, b_scale, w_shift, w_hg, w_hu, w_dn, w_tc, b_tc,
    out_ref, dmid_ref, dxg_ref, da0, da1, da2, da3, s_ac, s_scale, s_tc, s_gain, *rest, tiles, fast,
):
    core = meta[0] % 2
    step = pl.program_id(0)
    if fast:
        keep_ref, send_ref, g_hidden, g_square, g_cond, g_norm, g_dn = rest
    else:
        g_hidden, g_square, g_cond, g_norm, g_dn = rest

    @pl.when(step == 0)
    def _():
        for ref in (g_hidden, g_square, g_cond, g_norm, g_dn, s_ac, s_scale, s_tc, s_gain):
            ref[...] = jnp.zeros_like(ref)

    @pl.when(step < tiles)
    def _():
        x_one = x_ref[...]
        cond = cond_ref[...]
        gate = jax.nn.sigmoid(dot(x_one, w_gate[...], NN))
        first = core == 0
        att = jnp.concatenate(
            [
                jnp.where(first, a0[...], a1[...]),
                jnp.where(first, a1[...], a0[...]),
                jnp.where(first, a2[...], a3[...]),
                jnp.where(first, a3[...], a2[...]),
            ],
            axis=1,
        ).astype(f32)
        gated = (att * gate).astype(bf16)
        branch = dot(gated, w_out[...], NN)
        acond = jax.nn.sigmoid(dot(cond, w_ac[...], NN) + b_ac[...].astype(f32))
        mid = single_ref[...].astype(f32) + acond * branch
        cond_hat, _ = norm_rows(cond.astype(f32))
        cond_low = (cond_hat * gain[...].astype(f32)).astype(bf16)
        scale = jax.nn.sigmoid(dot(cond_low, w_scale[...], NN) + b_scale[...].astype(f32))
        normed, inverse = norm_rows(mid)
        x_two = (scale * normed + dot(cond_low, w_shift[...], NN)).astype(bf16)
        hgate = dot(x_two, w_hg[...], NN)
        hup = dot(x_two, w_hu[...], NN)
        sig = jax.nn.sigmoid(hgate)
        silu = hgate * sig
        hidden = (silu * hup).astype(bf16)
        tr_branch = dot(hidden, w_dn[...], NN)
        tcond = jax.nn.sigmoid(dot(cond, w_tc[...], NN) + b_tc[...].astype(f32))
        out_ref[...] = (mid + tcond * tr_branch).astype(bf16)
        dy = cot_ref[...].astype(f32)
        d_tr = (tcond * dy).astype(bf16)
        d_trc = dy * tr_branch * tcond * (1.0 - tcond)
        s_tc[...] += fold8(d_trc)
        g_cond[0] += dot(cond, d_trc.astype(bf16), TN)
        g_dn[...] += dot(hidden, d_tr, TN)
        d_hidden = dot(d_tr, w_dn[...], NT)
        d_hg = (d_hidden * hup * sig * (1.0 + hgate * (1.0 - sig))).astype(bf16)
        d_hu = (d_hidden * silu).astype(bf16)
        g_hidden[0] += dot(x_two, d_hg, TN)
        g_hidden[1] += dot(x_two, d_hu, TN)
        g_two = dot(d_hg, w_hg[...], NT) + dot(d_hu, w_hu[...], NT)
        d_scale = g_two * normed * scale * (1.0 - scale)
        s_scale[...] += fold8(d_scale)
        d_scale = d_scale.astype(bf16)
        d_shift = g_two.astype(bf16)
        g_norm[0] += dot(cond_low, d_scale, TN)
        g_norm[1] += dot(cond_low, d_shift, TN)
        d_cond = dot(d_scale, w_scale[...], NT) + dot(d_shift, w_shift[...], NT)
        s_gain[...] += fold8(d_cond * cond_hat)
        d_mid = dy + norm_back(normed, inverse, g_two * scale)
        dmid_ref[...] = d_mid
        d_attn = (acond * d_mid).astype(bf16)
        d_ac = d_mid * branch * acond * (1.0 - acond)
        s_ac[...] += fold8(d_ac)
        g_cond[1] += dot(cond, d_ac.astype(bf16), TN)
        g_square[0] += dot(gated, d_attn, TN)
        d_gated = dot(d_attn, w_out[...], NT)
        d_att = (d_gated * gate).astype(bf16)
        d_gate = (d_gated * att * gate * (1.0 - gate)).astype(bf16)
        g_square[1] += dot(x_one, d_gate, TN)
        dxg_ref[...] = dot(d_gate, w_gate[...], NT).astype(bf16)
        q = d_att.shape[1] // 4
        parts = [d_att[:, i * q : (i + 1) * q] for i in range(4)]
        da0[...] = jnp.where(first, parts[0], parts[1])
        da1[...] = jnp.where(first, parts[1], parts[0])
        da2[...] = jnp.where(first, parts[2], parts[3])
        da3[...] = jnp.where(first, parts[3], parts[2])

    if fast:

        @pl.when(step >= tiles)
        def _():
            emit = step - tiles
            for e, ref in enumerate((keep_ref, send_ref)):
                c = core ^ e
                for p in range(2):
                    side = (meta[0] // 2) ^ p
                    at = 0
                    for src, pieces in ((g_hidden, 2), (g_square, 1), (g_cond, 1), (g_norm, 1), (g_dn, 1)):
                        n = src.shape[-2] // 8
                        if src is g_dn:
                            place = meta[2 + emit // 2] * 2 + (meta[1] ^ (emit % 2))
                            rows = pl.ds(pl.multiple_of(place * n + c * (n // 2), n // 2), n // 2)
                            n = n // 2
                        else:
                            rows = emit_rows(meta, emit, n)
                        wide = src.shape[-1] // 2 // pieces
                        for piece in range(pieces):
                            lanes = pl.ds(pl.multiple_of((side * pieces + piece) * wide, wide), wide)
                            part = src[rows, lanes] if src is g_dn else src[c, rows, lanes]
                            ref[p, 0, at : at + n, :] = part.astype(bf16)
                            at += n


def middle(meta, x_one, single, cond, cot, atts, weights, fast):
    tokens, width = single.shape
    tile = tile_of(tokens)
    tiles = tokens // tile
    cs = cond.shape[1]
    quarter = atts[0].shape[1]
    w_gate, w_out, w_ac, b_ac, gain, w_scale, b_scale, w_shift, w_hg, w_hu, w_dn, w_tc, b_tc = weights
    fold = lambda n: jax.ShapeDtypeStruct((8, n), f32)
    sums = [fold(width), fold(width), fold(width), fold(cs)]
    grads = [(2,) + w_hg.shape, (2,) + w_out.shape, (2,) + w_ac.shape, (2,) + w_scale.shape, w_dn.shape]
    row_out = [(width, bf16), (width, f32), (width, bf16)] + [(quarter, bf16)] * 4
    macs = sum(w.size for w in weights if w.shape[0] > 1)
    if fast:
        lanes = width // 2
        rows = sum(w.size for w in weights if w.shape[0] > 1) // (8 * 4 * lanes)
        packed = pl.BlockSpec((2, 1, rows, lanes), lambda t, *_: (0, jnp.maximum(t - tiles, 0), 0, 0))
        more_specs = [packed] * 2
        more = [jax.ShapeDtypeStruct((2, 8, rows, lanes), bf16)] * 2
        scratch = [pltpu.VMEM(g, f32) for g in grads]
    else:
        more_specs = [fixed(g) for g in grads]
        more = [jax.ShapeDtypeStruct(g, f32) for g in grads]
        scratch = []
    return pl.pallas_call(
        functools.partial(middle_kernel, tiles=tiles, fast=fast),
        grid_spec=pltpu.PrefetchScalarGridSpec(
            num_scalar_prefetch=1,
            grid=(tiles + 8 * fast,),
            in_specs=[tiled(tile, w, tiles) for w in (width, width, cs, width)]
            + [tiled(tile, quarter, tiles)] * 4
            + [fixed(w.shape) for w in weights],
            out_specs=[tiled(tile, w, tiles) for w, _ in row_out] + [fixed(g.shape) for g in sums] + more_specs,
            scratch_shapes=scratch,
        ),
        out_shape=[jax.ShapeDtypeStruct((tokens, w), d) for w, d in row_out] + sums + more,
        compiler_params=pltpu.CompilerParams(vmem_limit_bytes=VMEM_BYTES),
        cost_estimate=pl.CostEstimate(
            flops=6 * tokens * macs, bytes_accessed=60 << 20, transcendentals=8 * tokens * width
        ),
        name="middle",
    )(meta, x_one, single, cond, cot, *atts, *weights)


def last_kernel(
    meta, d0, d1, d2, d3, single_ref, cond_ref, dmid_ref, gain, w_scale, b_scale, w_shift,
    out_ref, s_scale, s_gain, *rest, fast,
):
    if fast:
        keep_ref, send_ref, g_norm = rest
    else:
        (g_norm,) = rest

    @pl.when(pl.program_id(0) == 0)
    def _():
        for ref in (g_norm, s_scale, s_gain):
            ref[...] = jnp.zeros_like(ref)

    g_one = d0[...].astype(f32) + d1[...].astype(f32) + d2[...].astype(f32) + d3[...].astype(f32)
    normed, inverse = norm_rows(single_ref[...].astype(f32))
    cond_hat, _ = norm_rows(cond_ref[...].astype(f32))
    cond_low = (cond_hat * gain[...].astype(f32)).astype(bf16)
    scale = jax.nn.sigmoid(dot(cond_low, w_scale[...], NN) + b_scale[...].astype(f32))
    d_scale = g_one * normed * scale * (1.0 - scale)
    s_scale[...] += fold8(d_scale)
    d_scale = d_scale.astype(bf16)
    d_shift = g_one.astype(bf16)
    g_norm[0] += dot(cond_low, d_scale, TN)
    g_norm[1] += dot(cond_low, d_shift, TN)
    d_cond = dot(d_scale, w_scale[...], NT) + dot(d_shift, w_shift[...], NT)
    s_gain[...] += fold8(d_cond * cond_hat)
    out_ref[...] = dmid_ref[...] + norm_back(normed, inverse, g_one * scale)

    if fast:

        @pl.when(pl.program_id(0) == pl.num_programs(0) - 1)
        def _():
            n, wide = g_norm.shape[1] // 8, g_norm.shape[2] // 2
            for e, ref in enumerate((keep_ref, send_ref)):
                for p in range(2):
                    lanes = pl.ds(pl.multiple_of(((meta[0] // 2) ^ p) * wide, wide), wide)
                    for i in range(8):
                        ref[p, i] = g_norm[(meta[0] % 2) ^ e, emit_rows(meta, i, n), lanes].astype(bf16)


def last(meta, ds, single, cond, dmid, gain, w_scale, b_scale, w_shift, fast):
    tokens, width = single.shape
    tile = tile_of(tokens)
    steps = tokens // tile
    cs = cond.shape[1]
    grads = (2,) + w_scale.shape
    if fast:
        more = [jax.ShapeDtypeStruct((2, 8, cs // 8, width // 2), bf16)] * 2
        scratch = [pltpu.VMEM(grads, f32)]
    else:
        more = [jax.ShapeDtypeStruct(grads, f32)]
        scratch = []
    more = [jax.ShapeDtypeStruct((8, width), f32), jax.ShapeDtypeStruct((8, cs), f32)] + more
    row = tiled(tile, width, steps)
    return pl.pallas_call(
        functools.partial(last_kernel, fast=fast),
        grid_spec=pltpu.PrefetchScalarGridSpec(
            num_scalar_prefetch=1,
            grid=(steps,),
            in_specs=[row] * 5
            + [tiled(tile, cs, steps), row]
            + [fixed(w.shape) for w in (gain, w_scale, b_scale, w_shift)],
            out_specs=[row] + [fixed(g.shape) for g in more],
            scratch_shapes=scratch,
        ),
        out_shape=[jax.ShapeDtypeStruct((tokens, width), f32)] + more,
        compiler_params=pltpu.CompilerParams(vmem_limit_bytes=VMEM_BYTES),
        cost_estimate=pl.CostEstimate(
            flops=12 * tokens * width * cs, bytes_accessed=30 << 20, transcendentals=tokens * width
        ),
        name="last",
    )(meta, *ds, single, cond, dmid, gain, w_scale, b_scale, w_shift)


def swap(value, bit):
    return lax.ppermute(value, "head", [(i, i ^ bit) for i in range(lax.axis_size("head"))])


def across(value):
    return lax.ppermute(value, "samp", [(i, i ^ 1) for i in range(8)])


def along(value, right, places):
    step = 2 if right else -2
    return lax.ppermute(value, "samp", [(2 * z + x, 2 * z + x + step) for z in places for x in range(2)])


def add(*terms):
    total = terms[0].astype(f32)
    for term in terms[1:]:
        total = total + term.astype(f32)
    return total


def line_gather(own, z):
    inner = [own]
    right, left = own, own
    rights, lefts = [], []
    for t in range(3):
        right = along(right, True, range(t, 3))
        left = along(left, False, range(1, 4 - t))
        rights.append(right)
        lefts.append(left)
    inner.append(jnp.where(z % 2 == 0, lefts[0], rights[0]))
    inner.append(jnp.where(z == 0, lefts[1], jnp.where(z == 1, lefts[0], jnp.where(z == 2, rights[0], rights[1]))))
    inner.append(jnp.where(z == 0, lefts[2], jnp.where(z == 1, lefts[1], jnp.where(z == 2, rights[1], rights[2]))))
    out = []
    for value in inner:
        out += [value, across(value)]
    return out


def line_slots(z, x):
    table = jnp.array([[0, 1, 2, 3], [1, 0, 2, 3], [2, 3, 1, 0], [3, 2, 1, 0]], jnp.int32)[z]
    return jnp.stack([table * 2 + x, table * 2 + 1 - x], axis=1).reshape(8)


def line_order(z):
    return jnp.array([[3, 2, 1, 0], [3, 2, 0, 1], [0, 1, 3, 2], [0, 1, 2, 3]], jnp.int32)[z]


def line_reduce(keeps, sends, z):
    ready = [add(keep, across(send)) for keep, send in zip(keeps, sends)]
    low = lambda v: v.astype(bf16)
    right = along(low(ready[0]), True, (0,))
    left = along(low(ready[0]), False, (3,))
    right = along(low(jnp.where(z == 0, ready[1], ready[0]) + right.astype(f32)), True, (0, 1))
    left = along(low(jnp.where(z == 3, ready[1], ready[0]) + left.astype(f32)), False, (2, 3))
    right = along(low(jnp.where(z == 1, ready[1], ready[2]) + right.astype(f32)), True, (0, 1, 2))
    left = along(low(jnp.where(z == 2, ready[1], ready[2]) + left.astype(f32)), False, (1, 2, 3))
    return add(ready[3], right, left)


def whole_reduce(keep, send, z):
    near = swap(send, 1)
    far = swap(add(keep[1], near[1]).astype(bf16), 2)
    blocks = add(keep[0], near[0], far).astype(bf16)
    return line_reduce([blocks[2 * i] for i in range(4)], [blocks[2 * i + 1] for i in range(4)], z)


def total_all(vector):
    for move in (
        lambda v: swap(v, 1),
        lambda v: swap(v, 2),
        across,
        lambda v: lax.ppermute(v, "samp", [(i, i ^ 2) for i in range(8)]),
        lambda v: lax.ppermute(v, "samp", [(i, i ^ 4) for i in range(8)]),
    ):
        vector = vector + move(vector)
    return vector


def on_device(
    single,
    cond,
    pair,
    complex_length,
    sample_complex,
    cotangent,
    gain_one,
    w_scale_one,
    b_scale_one,
    w_shift_one,
    w_query,
    b_query,
    w_key,
    w_value,
    w_gate,
    w_out,
    w_pair,
    w_attn_cond,
    b_attn_cond,
    gain_two,
    w_scale_two,
    b_scale_two,
    w_shift_two,
    w_hidden_gate,
    w_hidden_up,
    w_hidden_down,
    w_tr_cond,
    b_tr_cond,
):
    groups = lax.axis_size("head")
    devices = lax.axis_size("samp")
    me = lax.axis_index("head")
    place = lax.axis_index("samp")
    core = me % 2
    part = me // 2
    samples, rows, width = single.shape
    cs = cond.shape[2]
    tokens = samples * rows
    length = rows * groups
    heads = w_pair.shape[1]
    few = heads // groups
    dim = width // heads
    wide = few * dim
    complexes, _, columns, _ = pair.shape
    chunks = 2 * groups
    chunk = length // chunks
    halves = range(groups // 2)
    fast = devices == 8 and groups == 4 and columns == chunk
    line = lambda v: v.reshape(1, -1)
    first = core == 0

    if fast:
        z, x = place // 2, place % 2
        order, slots = line_order(z), line_slots(z, x)
    else:
        z, x = place, jnp.zeros((), jnp.int32)
        order, slots = jnp.zeros((4,), jnp.int32), jnp.arange(chunks, dtype=jnp.int32)
    meta = jnp.concatenate([jnp.stack([me, x]).astype(jnp.int32), order, sample_complex, slots])
    pair_meta = jnp.stack([me, place]).astype(jnp.int32)

    group = 8
    sizes = dict(few=few, blocks=groups, group=group)
    pair_low, pair_inverse, pair_raw, *bias = pair_bias(pair_meta, complex_length, pair, blocked(w_pair, group), **sizes)
    biases = []
    for k in halves:
        own = jnp.concatenate([bias[k], swap(bias[groups // 2 + k], 1)], axis=-1)
        if fast:
            biases.append(line_gather(own, z))
            continue
        gathered = lax.all_gather(own, "samp", axis=0)
        moved = gathered.transpose(1, 2, 0, 3, 4).reshape(complexes, few, chunks, chunk, 2 * rows)
        biases.append([moved[:, :, i] for i in range(chunks)])

    single_t = single.reshape(tokens, width)
    cond_t = cond.reshape(tokens, cs)
    cot_t = cotangent.reshape(tokens, width)
    x_one = adapt(single_t, cond_t, line(gain_one), w_scale_one, line(b_scale_one), w_shift_one)
    x_far = swap(x_one, 2)
    x_near = swap(x_one, 1)
    x_cross = swap(x_far, 1)
    blocks = [v.reshape(samples, rows, width) for v in (x_one, x_near, x_far, x_cross)]

    def own_columns(w, k):
        return lax.dynamic_slice_in_dim(w, (2 * k + core) * wide, wide, w.ndim - 1)

    w_heads = [jnp.concatenate([own_columns(w, k).T for w in (w_query, w_key, w_value)], axis=0) for k in halves]
    b_heads = [own_columns(b_query.astype(f32), k)[:, None] for k in halves]
    kept = [attend(meta, blocks, w_heads[k], b_heads[k], biases[k], nh=few, hd=dim) for k in halves]
    atts = []
    for k in halves:
        out = kept[k][0]
        atts += [out[0].reshape(tokens, wide), swap(out[1], 1).reshape(tokens, wide)]

    block_out, d_mid, d_xg, da0, da1, da2, da3, s_ac, s_scale2, s_tc, s_gain2, *w_mid = middle(
        meta, x_one, single_t, cond_t, cot_t, atts,
        (w_gate, w_out, w_attn_cond, line(b_attn_cond), line(gain_two), w_scale_two, line(b_scale_two), w_shift_two,
         w_hidden_gate, w_hidden_up, w_hidden_down, w_tr_cond, line(b_tr_cond)),
        fast,
    )

    shape = (samples, rows, wide)
    d_x = None
    bias_sums, w_grads, q_grads = [], [], []
    for k, (own, sent) in enumerate(((da0, da1), (da2, da3))):
        out, probs, q, key, value, total = kept[k]
        d_x, *grads = attend_back(
            meta, blocks, w_heads[k], probs, q, key, value, total, out, own.reshape(shape), swap(sent, 1).reshape(shape),
            d_x, chunks, complexes, nh=few, hd=dim, fast=fast)
        if fast:
            gw, gb = grads[:2]
            bias_sums.append(line_reduce(grads[6:], grads[2:6], z).astype(bf16))
        else:
            db, gw, gb = grads
            moved = db.transpose(1, 2, 0, 3, 4).reshape(complexes, few, devices, columns, 2 * rows)
            bias_sums.append(lax.psum_scatter(moved, "samp", scatter_dimension=2, tiled=False))
        w_grads.append(gw)
        q_grads.append(gb)

    near = swap(d_x[3], 1)
    far = swap(add(d_x[2], near).astype(bf16), 2)
    near = swap(d_x[1], 1)
    flat = lambda v: v.reshape(tokens, width)
    grad_single, s_scale1, s_gain1, *w_last = last(
        meta, (flat(d_x[0]), flat(near), flat(far), d_xg), single_t, cond_t, d_mid,
        line(gain_one), w_scale_one, line(b_scale_one), w_shift_one, fast,
    )

    pair_grads = [v[..., :rows] for v in bias_sums] + [swap(v[..., rows:], 1) for v in bias_sums]
    grad_pair, grad_pair_weight = pair_back(pair_meta, pair_low, pair_inverse, pair_raw, w_pair, pair_grads, **sizes)

    keep = jnp.where(part == 0, w_grads[0], w_grads[1])
    send = jnp.where(part == 0, w_grads[1], w_grads[0])
    if fast:
        packed = add(keep, swap(send, 2)).astype(bf16)
        r_heads = line_reduce([packed[2 * i] for i in range(4)], [packed[2 * i + 1] for i in range(4)], z)
        packed = whole_reduce(*w_mid, z)

        def settle(block, tall=False):
            half = block.shape[1] // 2
            low, high = block[:, :half], block[:, half:]
            got = swap(jnp.where(first, high, low), 1)
            held = jnp.where(first, low, high)
            pair_of = (jnp.where(first, held, got), jnp.where(first, got, held))
            return jnp.concatenate(pair_of, axis=0) if tall else pair_of

        n, m = width // 8, cs // 8
        hidden = jnp.concatenate([packed[0:n], packed[n : 2 * n]], axis=1)
        r_hg, r_hu = settle(hidden)
        r_out, r_gate = settle(packed[2 * n : 3 * n])
        r_tc, r_ac = settle(packed[3 * n : 3 * n + m])
        r_scale2, r_shift2 = settle(packed[3 * n + m : 3 * n + 2 * m])
        r_down = settle(packed[3 * n + 2 * m :], tall=True)
        r_scale1, r_shift1 = settle(whole_reduce(*w_last, z))
    else:

        def total_of(stack):
            axis = stack.ndim - 1
            half = lax.psum_scatter(stack.astype(bf16), "head", scatter_dimension=axis, tiled=True).astype(f32)
            return lax.psum_scatter(half, "samp", scatter_dimension=axis - 1, tiled=True)

        r_heads = keep + swap(send.astype(bf16), 2).astype(f32)
        r_heads = lax.psum_scatter(r_heads.T, "samp", scatter_dimension=0, tiled=True)
        (r_hg, r_hu), (r_out, r_gate), (r_tc, r_ac), (r_scale2, r_shift2), r_down = [total_of(v) for v in w_mid]
        r_scale1, r_shift1 = total_of(w_last[0])

    zero = jnp.zeros((wide,), f32)
    q_full = []
    for k in halves:
        mine = q_grads[k][:, 0]
        q_full += [jnp.where(first, mine, zero), jnp.where(first, zero, mine)]
    column_sum = lambda v: jnp.sum(v, axis=0)
    early = jnp.concatenate([column_sum(s_gain2), *q_full, column_sum(s_ac), column_sum(s_scale2), column_sum(s_tc)])
    late = jnp.concatenate([grad_pair_weight.reshape(-1), column_sum(s_gain1), column_sum(s_scale1)])
    if fast:
        early, late = total_all(early), total_all(late)
    else:
        early, late = lax.psum((early, late), ("samp", "head"))
    cuts = [cs, cs + width, cs + 2 * width, cs + 3 * width]
    sum_gain2, sum_query, sum_ac, sum_scale2, sum_tc = jnp.split(early, cuts)
    across_pair = heads * w_pair.shape[0]
    sum_pair, sum_gain1, sum_scale1 = jnp.split(late, [across_pair, across_pair + cs])
    whole = (samples, rows, width)
    return (
        block_out.reshape(whole),
        grad_single.reshape(whole),
        grad_pair,
        sum_gain1,
        r_scale1,
        sum_scale1,
        r_shift1,
        r_heads[:, :wide],
        sum_query,
        r_heads[:, wide : 2 * wide],
        r_heads[:, 2 * wide :],
        r_gate,
        r_out,
        sum_pair.reshape(heads, -1).T,
        r_ac,
        sum_ac,
        sum_gain2,
        r_scale2,
        sum_scale2,
        r_shift2,
        r_hg,
        r_hu,
        r_down,
        r_tc,
        sum_tc,
    )


def solution(mesh):
    placed = (
        P("samp", "head", None),
        P("samp", "head", None),
        P(None, "head", "samp", None),
        P(),
        P("samp"),
        P("samp", "head", None),
        P(),
        P(),
        P(),
        P(),
        P(),
        P(),
        P(),
        P(),
        P(),
        P(),
        P(),
        P(),
        P(),
        P(),
        P(),
        P(),
        P(),
        P(),
        P(),
        P(),
        P(),
        P(),
    )
    return jax.shard_map(
        on_device,
        mesh=mesh,
        in_specs=placed,
        out_specs=(
            P("samp", "head", None),
            P("samp", "head", None),
            P(None, "head", "samp", None),
            P(),
            P("samp", "head"),
            P(),
            P("samp", "head"),
            P("samp", "head"),
            P(),
            P("samp", "head"),
            P("samp", "head"),
            P("samp", "head"),
            P("samp", "head"),
            P(),
            P("samp", "head"),
            P(),
            P(),
            P("samp", "head"),
            P(),
            P("samp", "head"),
            P("samp", "head"),
            P("samp", "head"),
            P("samp", "head"),
            P("samp", "head"),
            P(),
        ),
        check_vma=False,
    )
```

```python
import functools
import math

import jax
import jax.numpy as jnp
from jax import lax
from jax.experimental import pallas as pl
from jax.experimental.pallas import tpu as pltpu
from jax.sharding import PartitionSpec as P

f32, bf16 = jnp.float32, jnp.bfloat16
epsilon = 1e-05
fill_value = -1e30
LOG2E = math.log2(math.e)
VMEM_BYTES = 60 << 20
PAIR_LINES = (8, 16, 24, 32, 64)
NN, NT, TN = ((1,), (0,)), ((1,), (1,)), ((0,), (0,))


LIGHT = pl.CostEstimate(flops=1 << 20, bytes_accessed=1 << 20, transcendentals=0)


def dot(a, b, dims):
    return lax.dot_general(a, b, (dims, ((), ())), preferred_element_type=f32)


def norm_rows(inputs):
    mean_val = jnp.mean(inputs, axis=-1, keepdims=True)
    centered = inputs - mean_val
    variance = jnp.mean(centered * centered, axis=-1, keepdims=True)
    inverse = lax.rsqrt(variance + epsilon)
    return (centered * inverse, inverse)


def norm_back(normed, inverse, upstream):
    mean_grad = jnp.mean(upstream, axis=-1, keepdims=True)
    mean_dot = jnp.mean(upstream * normed, axis=-1, keepdims=True)
    return inverse * (upstream - mean_grad - normed * mean_dot)


def tile_of(tokens, sizes=(8, 16, 32, 64, 128, 256)):
    return max(t for t in sizes if tokens % t == 0)


def fixed(shape):
    return pl.BlockSpec(shape, lambda *_: (0,) * len(shape), pipeline_mode=pl.Buffered(1))


META = 6


def attend_kernel(meta, x0, x1, x2, x3, w_ref, bq_ref, *rest, which, nh, hd, rows, jc, nchunk, qscale):
    bias_hbm = rest[:nchunk]
    o_ref, far_ref, p_ref, q_ref, k_ref, v_ref, l_ref, xs, ks, ss, bias_ref, sems = rest[nchunk:]
    b = pl.program_id(0)
    g = meta[0]
    cplx = meta[META + b]
    per_block = nchunk // 4

    def copies():
        return [
            pltpu.make_async_copy(
                bias_hbm[i] if which[i] is None else bias_hbm[i].at[which[i]],
                bias_ref.at[meta[META + pl.num_programs(0) + i]],
                sems.at[i],
            )
            for i in range(nchunk)
        ]

    @pl.when(b == 0)
    def _():
        for copy in copies():
            copy.start()

    for r, x in enumerate((x0, x1, x2, x3)):
        xs[r * rows : (r + 1) * rows, :] = x[0]
    wch = nh * hd
    q = dot(w_ref[0:wch, :], xs[0 : 2 * rows, :], NT) + bq_ref[...]
    q_ref[0] = (q * qscale).astype(bf16)
    kv = dot(w_ref[wch : 3 * wch, :], xs[...], NT).astype(bf16)
    k_ref[0] = kv[0:wch]
    v_ref[0] = kv[wch:]

    @pl.when(b == 0)
    def _():
        for copy in copies():
            copy.wait()

    ones = jnp.ones((16, kv.shape[1]), bf16)
    outs = []
    sums = []
    for h in range(nh):
        ks[h % 2, :, :] = jnp.transpose(k_ref[0, h * hd : (h + 1) * hd, :])
        qT = q_ref[0, h * hd : (h + 1) * hd, :]
        m = None
        for t in range(nchunk):
            r, u = t // per_block, t % per_block
            s_idx = (r ^ g) * per_block + u
            s = dot(ks[h % 2, t * jc : (t + 1) * jc, :], qT, NN) + bias_ref[s_idx, cplx, h].astype(f32)
            ss[h % 2, t * jc : (t + 1) * jc, :] = s
            mt = jnp.max(s.reshape(jc // 8, 8, s.shape[1]), axis=0)
            m = mt if m is None else jnp.maximum(m, mt)
        m = jnp.max(m, axis=0, keepdims=True)
        for t in range(nchunk):
            part = slice(t * jc, (t + 1) * jc)
            p_ref[0, h, part, :] = jnp.exp2(ss[h % 2, part, :] - m).astype(bf16)
        va = jnp.concatenate([v_ref[0, h * hd : (h + 1) * hd, :], ones], axis=0)
        oT = dot(va, p_ref[0, h], NN)
        l = oT[hd : hd + 1, :]
        outs.append(oT[:hd] / l)
        sums.append(l)
    l_ref[0] = jnp.concatenate(sums, axis=0)
    o = jnp.transpose(jnp.concatenate(outs, axis=0)).astype(bf16)
    o_ref[0] = o[:rows]
    far_ref[0] = o[rows:]


def attend(meta, xb, wT, bq, biases, *, nh, hd):
    B, rows, C = xb[0].shape
    nchunk = len(biases)
    biases, which = zip(*biases)
    ncx, _, jc, qi = biases[0].shape[-4:]
    L = nchunk * jc
    wch = nh * hd
    kern = functools.partial(
        attend_kernel, which=which, nh=nh, hd=hd, rows=rows, jc=jc, nchunk=nchunk, qscale=LOG2E / math.sqrt(hd)
    )
    xspec = pl.BlockSpec((1, rows, C), lambda b, m: (b, 0, 0))
    per = lambda shape: pl.BlockSpec((1,) + shape, lambda b, m: (b,) + (0,) * len(shape))
    return pl.pallas_call(
        kern,
        grid_spec=pltpu.PrefetchScalarGridSpec(
            num_scalar_prefetch=1,
            grid=(B,),
            in_specs=[xspec] * 4
            + [fixed(wT.shape), fixed(bq.shape)]
            + [pl.BlockSpec(memory_space=pl.ANY)] * nchunk,
            out_specs=[
                per((rows, wch)),
                per((rows, wch)),
                per((nh, L, qi)),
                per((wch, qi)),
                per((wch, L)),
                per((wch, L)),
                per((nh, qi)),
            ],
            scratch_shapes=[
                pltpu.VMEM((L, C), bf16),
                pltpu.VMEM((2, L, hd), bf16),
                pltpu.VMEM((2, L, qi), f32),
                pltpu.VMEM((nchunk, ncx, nh, jc, qi), bf16),
                pltpu.SemaphoreType.DMA((nchunk,)),
            ],
        ),
        out_shape=[
            jax.ShapeDtypeStruct((B, rows, wch), bf16),
            jax.ShapeDtypeStruct((B, rows, wch), bf16),
            jax.ShapeDtypeStruct((B, nh, L, qi), bf16),
            jax.ShapeDtypeStruct((B, wch, qi), bf16),
            jax.ShapeDtypeStruct((B, wch, L), bf16),
            jax.ShapeDtypeStruct((B, wch, L), bf16),
            jax.ShapeDtypeStruct((B, nh, qi), f32),
        ],
        compiler_params=pltpu.CompilerParams(vmem_limit_bytes=VMEM_BYTES),
        cost_estimate=LIGHT,
        name="attend",
    )(meta, *xb, wT, bq, *biases)


def attend_back_kernel(
    meta, p_ref, q_ref, k_ref, v_ref, l_ref, o0, o1, do0, do1, *rest, base, nh, hd, jc, nchunk, scale, fast
):
    dq_ref, dkv_ref = rest[:2]
    vs, ds, acc = rest[-3:]
    b = pl.program_id(0)
    g = meta[0]
    cplx = meta[META + b]
    per_block = nchunk // 4
    wch = nh * hd
    L = nchunk * jc

    @pl.when(b == 0)
    def _():
        acc[...] = jnp.zeros_like(acc)

    dO = jnp.transpose(jnp.concatenate([do0[0], do1[0]], axis=0).astype(f32))
    O = jnp.transpose(jnp.concatenate([o0[0], o1[0]], axis=0).astype(f32))
    prod = dO * O
    qi = dO.shape[1]
    row = lax.broadcasted_iota(jnp.int32, (16, qi), 0)
    ones = jnp.ones((16, L), bf16)
    for h in range(nh):
        hs = slice(h * hd, (h + 1) * hd)
        his = slice((base + h) * hd, (base + h + 1) * hd)
        linv = 1.0 / l_ref[0, base + h : base + h + 1, :]
        dOh = (dO[his] * linv).astype(bf16)
        delta = jnp.sum(prod[his], axis=0, keepdims=True) * linv
        hi = delta.astype(bf16).astype(f32)
        extra = jnp.where(row == 0, -hi, jnp.where(row == 1, hi - delta, 0.0)).astype(bf16)
        dOa = jnp.concatenate([dOh, extra], axis=0)
        vs[h % 2] = jnp.transpose(jnp.concatenate([v_ref[0, hs, :], ones], axis=0))
        for t in range(nchunk):
            r, u = t // per_block, t % per_block
            s_idx = (r ^ g) * per_block + u
            ts = slice(t * jc, (t + 1) * jc)
            d = dot(vs[h % 2, ts, :], dOa, NN) * p_ref[0, h, ts, :].astype(f32)
            acc[s_idx, cplx, h] += d
            ds[h % 2, ts, :] = d.astype(bf16)
        dq_ref[0, hs, :] = (dot(k_ref[0, hs, :], ds[h % 2], NN) * scale).astype(bf16)
        dkv_ref[0, hs, :] = (dot(q_ref[0, hs, :], ds[h % 2], NT) * (1.0 / LOG2E)).astype(bf16)
        dkv_ref[0, wch + h * hd : wch + (h + 1) * hd, :] = dot(dOh, p_ref[0, h], NT).astype(bf16)

    @pl.when(b == pl.num_programs(0) - 1)
    def _():
        if fast:
            ncx = acc.shape[1]
            for c in range(ncx):
                for i in range(4):
                    place = meta[2 + i] * 2
                    rest[2 + c][i] = acc[place + meta[1], c].astype(bf16)
                    rest[2 + ncx + c][i] = acc[place + 1 - meta[1], c].astype(bf16)
        else:
            rest[2][...] = acc[...].astype(bf16)


def attend_back(meta, p, q, k, v, l, o0, o1, do0, do1, nchunk, ncx, *, base, nh, hd, fast):
    B, held, L, qi = p.shape
    rows = o0.shape[1]
    jc = L // nchunk
    wch = nh * hd
    kern = functools.partial(
        attend_back_kernel, base=base, nh=nh, hd=hd, jc=jc, nchunk=nchunk, scale=1.0 / math.sqrt(hd), fast=fast
    )
    per = lambda shape: pl.BlockSpec((1,) + shape, lambda b, m: (b,) + (0,) * len(shape))
    some = lambda shape: pl.BlockSpec((1,) + shape, lambda b, m: (b, base // nh) + (0,) * (len(shape) - 1))
    db = (nchunk, ncx, nh, jc, qi)
    outs = [((4,) + db[2:], bf16)] * (2 * ncx) if fast else [(db, bf16)]
    return pl.pallas_call(
        kern,
        grid_spec=pltpu.PrefetchScalarGridSpec(
            num_scalar_prefetch=1,
            grid=(B,),
            in_specs=[some((nh, L, qi)), some((wch, qi)), some((wch, L)), some((wch, L)), per((held, qi))]
            + [per((rows, held * hd))] * 4,
            out_specs=[per((wch, qi)), per((2 * wch, L))] + [fixed(s) for s, _ in outs],
            scratch_shapes=[
                pltpu.VMEM((2, L, hd + 16), bf16),
                pltpu.VMEM((2, L, qi), bf16),
                pltpu.VMEM(db, f32),
            ],
        ),
        out_shape=[jax.ShapeDtypeStruct((B, wch, qi), bf16), jax.ShapeDtypeStruct((B, 2 * wch, L), bf16)]
        + [jax.ShapeDtypeStruct(s, d) for s, d in outs],
        compiler_params=pltpu.CompilerParams(vmem_limit_bytes=VMEM_BYTES),
        cost_estimate=LIGHT,
        name="attend_back",
    )(meta, p, q, k, v, l, o0, o1, do0, do1)


def heads_back_kernel(meta, x0, x1, x2, x3, wq_ref, wkv_ref, *rest, parts, rows, wch, fast):
    n = len(parts)
    dqs, dkvs = rest[:n], rest[n : 2 * n]
    near_ref, cross_ref, far_ref, own_ref, gb_ref = rest[2 * n : 2 * n + 5]
    if fast:
        keep_ref, send_ref, xs, dq, dkv, gq, gkv, gt = rest[2 * n + 5 :]
    else:
        gq, gkv, xs, dq, dkv = rest[2 * n + 5 :]
    b = pl.program_id(0)

    @pl.when(b == 0)
    def _():
        gq[...] = jnp.zeros_like(gq)
        gkv[...] = jnp.zeros_like(gkv)
        gb_ref[...] = jnp.zeros_like(gb_ref)

    for r, x in enumerate((x0, x1, x2, x3)):
        xs[r * rows : (r + 1) * rows, :] = x[0]
    for (chunk, at, size), q, kv in zip(parts, dqs, dkvs):
        start = chunk * wch + at
        dq[start : start + size, :] = q[0]
        start = 2 * chunk * wch + at
        dkv[start : start + size, :] = kv[0, :size]
        dkv[start + wch : start + wch + size, :] = kv[0, size:]
    q, kv = dq[...], dkv[...]
    gb_ref[...] += jnp.sum(q.astype(f32), axis=1, keepdims=True)
    gq[...] += dot(q, xs[0 : 2 * rows, :], NN)
    gkv[...] += dot(kv, xs[...], NN)
    kv = jnp.transpose(kv)
    q = jnp.transpose(q)
    for r, ref in ((3, cross_ref), (2, far_ref), (1, near_ref), (0, own_ref)):
        rs = slice(r * rows, (r + 1) * rows)
        dx = dot(kv[rs], wkv_ref[...], NN)
        if r < 2:
            dx += dot(q[rs], wq_ref[...], NN)
        ref[0] = dx.astype(bf16)

    if fast:

        @pl.when(b == pl.num_programs(0) - 1)
        def _():
            for e, ref in enumerate((keep_ref, send_ref)):
                chunk = (meta[0] // 2) ^ e
                half = pl.ds(pl.multiple_of(chunk * wch, wch), wch)
                gt[:, 0:wch] = jnp.transpose(gq[half, :])
                both = pl.ds(pl.multiple_of(chunk * 2 * wch, wch), 2 * wch)
                gt[:, wch:] = jnp.transpose(gkv[both, :])
                count = gt.shape[0] // 8
                for i in range(8):
                    ref[i] = gt[emit_rows(meta, i, count), :].astype(bf16)


def heads_back(meta, xb, wq, wkv, grads, parts, *, wch, fast):
    B, rows, C = xb[0].shape
    L = 4 * rows
    total = wq.shape[0]
    row = pl.BlockSpec((1, rows, C), lambda b, m: (b, 0, 0))
    per = lambda shape: pl.BlockSpec((1,) + shape, lambda b, m: (b,) + (0,) * len(shape))
    dqs, dkvs = [g[0] for g in grads], [g[1] for g in grads]
    sums = [((total, C), f32), ((2 * total, C), f32)]
    held = [pltpu.VMEM((L, C), bf16), pltpu.VMEM((total, 2 * rows), bf16), pltpu.VMEM((2 * total, L), bf16)]
    if fast:
        outs = [((8, C // 8, 3 * wch), bf16)] * 2
        held += [pltpu.VMEM(s, d) for s, d in sums] + [pltpu.VMEM((C, 3 * wch), f32)]
    else:
        outs = sums
    outs = [((total, 1), f32)] + outs
    return pl.pallas_call(
        functools.partial(heads_back_kernel, parts=parts, rows=rows, wch=wch, fast=fast),
        grid_spec=pltpu.PrefetchScalarGridSpec(
            num_scalar_prefetch=1,
            grid=(B,),
            in_specs=[row] * 4
            + [fixed(wq.shape), fixed(wkv.shape)]
            + [per(v.shape[1:]) for v in dqs + dkvs],
            out_specs=[row] * 4 + [fixed(s) for s, _ in outs],
            scratch_shapes=held,
        ),
        out_shape=[jax.ShapeDtypeStruct((B, rows, C), bf16)] * 4 + [jax.ShapeDtypeStruct(s, d) for s, d in outs],
        compiler_params=pltpu.CompilerParams(vmem_limit_bytes=VMEM_BYTES),
        cost_estimate=LIGHT,
        name="heads_back",
    )(meta, *xb, wq, wkv, *dqs, *dkvs)


def blocked(w, count):
    across, heads = w.shape
    wide = jnp.tile(jnp.transpose(w), (count, count))
    row = lax.broadcasted_iota(jnp.int32, wide.shape, 0) // heads
    column = lax.broadcasted_iota(jnp.int32, wide.shape, 1) // across
    return jnp.where(row == column, wide, jnp.zeros_like(wide))


def pair_bias_kernel(meta, lens, pair_ref, wb_ref, low_ref, inv_ref, raw_ref, *rest, few, blocks, group):
    outs, scr = rest[:-1], rest[-1]
    c, t = pl.program_id(0), pl.program_id(1)
    lines, columns, cz = pair_ref.shape[1:]
    heads = few * blocks
    per = lines // group
    mean = jnp.full((cz, cz), 1.0 / cz, bf16)
    lane = lax.broadcasted_iota(jnp.int32, (columns, group * heads), 1) // heads
    table = []
    for n in range(per):
        x = [pair_ref[0, n * group + i] for i in range(group)]
        flat = columns % 16 == 0
        if flat:
            x = [jnp.concatenate(x, axis=0)]
        lows, inverses = [], []
        for v in x:
            centered = v.astype(f32) - dot(v, mean, NN)
            inverse = lax.rsqrt(dot((centered * centered).astype(bf16), mean, NN) + epsilon)
            lows.append((centered * inverse).astype(bf16))
            inverses.append(inverse)
        if flat:
            lows = [lows[0][i * columns : (i + 1) * columns] for i in range(group)]
            inverses = [inverses[0][i * columns : (i + 1) * columns] for i in range(group)]
        spread = inverses[0][:, : group * heads]
        for i in range(1, group):
            spread = jnp.where(lane == i, inverses[i][:, : group * heads], spread)
        inv_ref[0, n] = spread
        for i in range(group):
            low_ref[0, n * group + i] = lows[i]
        table.append(jnp.concatenate(lows, axis=1))
    out = dot(jnp.concatenate(table, axis=0), wb_ref[...], NT)
    for n in range(per):
        part = out[n * columns : (n + 1) * columns]
        raw_ref[0, n] = part
        start = pl.multiple_of((t * per + n) * group * heads, group * heads)
        scr[pl.ds(start, group * heads), :] = jnp.transpose(part)

    @pl.when(t == pl.num_programs(1) - 1)
    def _():
        core = meta[0] % 2
        rows = scr.shape[0] // heads
        place = lax.broadcasted_iota(jnp.int32, (columns, rows), 0) + meta[1] * columns
        valid = place < lens[c]
        half = len(outs) // 2
        for k in range(half):
            for f in range(few):
                for e in range(2):
                    h = (2 * k + (core ^ e)) * few + f
                    v = jnp.transpose(scr[pl.ds(h, rows, stride=heads), :])
                    outs[e * half + k][0, f] = jnp.where(valid, v * LOG2E, fill_value).astype(bf16)


def pair_specs(pair, heads, group):
    lines = tile_of(pair.shape[1], PAIR_LINES)
    columns, cz = pair.shape[2:]
    return (
        lines,
        pl.BlockSpec((1, lines, columns, cz), lambda c, t, *_: (c, t, 0, 0)),
        pl.BlockSpec((1, lines // group, columns, group * heads), lambda c, t, *_: (c, t, 0, 0)),
        jax.ShapeDtypeStruct((pair.shape[0], pair.shape[1] // group, columns, group * heads), f32),
    )


def pair_bias(meta, lens, pair, wb, *, few, blocks, group):
    ncx, rows, columns, cz = pair.shape
    heads = few * blocks
    lines, spec, thin, thin_shape = pair_specs(pair, heads, group)
    out = jax.ShapeDtypeStruct((ncx, few, columns, rows), bf16)
    return pl.pallas_call(
        functools.partial(pair_bias_kernel, few=few, blocks=blocks, group=group),
        grid_spec=pltpu.PrefetchScalarGridSpec(
            num_scalar_prefetch=2,
            grid=(ncx, rows // lines),
            in_specs=[spec, fixed(wb.shape)],
            out_specs=[spec, thin, thin]
            + [pl.BlockSpec((1, few, columns, rows), lambda c, t, *_: (c, 0, 0, 0))] * blocks,
            scratch_shapes=[pltpu.VMEM((rows * heads, columns), f32)],
        ),
        out_shape=[jax.ShapeDtypeStruct(pair.shape, bf16), thin_shape, thin_shape] + [out] * blocks,
        compiler_params=pltpu.CompilerParams(vmem_limit_bytes=VMEM_BYTES),
        cost_estimate=LIGHT,
        name="pair_bias",
    )(meta, lens, pair, wb)


def pair_back_kernel(meta, low_ref, inv_ref, raw_ref, w2_ref, mean_ref, *rest, few, blocks, group):
    grads = rest[:blocks]
    out_ref, gw_ref, scr, acc = rest[blocks:]
    c, t = pl.program_id(0), pl.program_id(1)
    lines, columns, cz = low_ref.shape[1:]
    heads = few * blocks
    per = lines // group

    @pl.when((c == 0) & (t == 0))
    def _():
        acc[...] = jnp.zeros_like(acc)

    @pl.when(t == 0)
    def _():
        core = meta[0] % 2
        rows = scr.shape[0] // heads
        half = blocks // 2
        for k in range(half):
            for f in range(few):
                for e in range(2):
                    h = (2 * k + (core ^ e)) * few + f
                    scr[pl.ds(h, rows, stride=heads), :] = jnp.transpose(grads[e * half + k][0, f].astype(f32))

    ds, prods, xs = [], [], []
    for n in range(per):
        start = pl.multiple_of((t * per + n) * group * heads, group * heads)
        x = jnp.transpose(scr[pl.ds(start, group * heads), :])
        d = x * inv_ref[0, n]
        prod = d * raw_ref[0, n]
        hi = prod.astype(bf16)
        d = d.astype(bf16)
        xs.append(x.astype(bf16))
        ds.append(jnp.concatenate([d, d], axis=1))
        prods.append(jnp.concatenate([hi, (prod - hi.astype(f32)).astype(bf16)], axis=1))
    upstream = dot(jnp.concatenate(ds, axis=0), w2_ref[...], NN)
    along = dot(jnp.concatenate(prods, axis=0), mean_ref[...], NN)
    table = []
    for n in range(per):
        lows = [low_ref[0, n * group + i] for i in range(group)]
        ns = slice(n * columns, (n + 1) * columns)
        for i in range(group):
            zs = slice(i * cz, (i + 1) * cz)
            out_ref[0, n * group + i] = upstream[ns, zs] - lows[i].astype(f32) * along[ns, zs]
        table.append(jnp.concatenate(lows, axis=1))
    acc[...] += dot(jnp.concatenate(xs, axis=0), jnp.concatenate(table, axis=0), TN)

    @pl.when((c == pl.num_programs(0) - 1) & (t == pl.num_programs(1) - 1))
    def _():
        total = acc[0:heads, 0:cz]
        for i in range(1, group):
            total += acc[i * heads : (i + 1) * heads, i * cz : (i + 1) * cz]
        gw_ref[...] = total


def pair_back(meta, low, inv, raw, w, grads, *, few, blocks, group):
    ncx, rows, columns, cz = low.shape
    heads = few * blocks
    lines, spec, thin, _ = pair_specs(low, heads, group)
    mean = jnp.mean(w.astype(f32), axis=0, keepdims=True)
    w2 = jnp.concatenate([blocked(w, group), blocked(jnp.broadcast_to(-mean, w.shape).astype(bf16), group)], axis=0)
    ones = blocked(jnp.full(w.shape, 1.0 / cz, bf16), group)
    ones = jnp.concatenate([ones, ones], axis=0)
    return pl.pallas_call(
        functools.partial(pair_back_kernel, few=few, blocks=blocks, group=group),
        grid_spec=pltpu.PrefetchScalarGridSpec(
            num_scalar_prefetch=1,
            grid=(ncx, rows // lines),
            in_specs=[spec, thin, thin, fixed(w2.shape), fixed(ones.shape)]
            + [pl.BlockSpec((1, few, columns, rows), lambda c, t, *_: (c, 0, 0, 0))] * blocks,
            out_specs=[spec, fixed((heads, cz))],
            scratch_shapes=[pltpu.VMEM((rows * heads, columns), f32), pltpu.VMEM((group * heads, group * cz), f32)],
        ),
        out_shape=[jax.ShapeDtypeStruct(low.shape, f32), jax.ShapeDtypeStruct((heads, cz), f32)],
        compiler_params=pltpu.CompilerParams(vmem_limit_bytes=VMEM_BYTES),
        cost_estimate=LIGHT,
        name="pair_back",
    )(meta, low, inv, raw, w2, ones, *grads)


def column_sum(v):
    return jnp.sum(v, axis=0, keepdims=True)


def tiled(rows, width, steps):
    return pl.BlockSpec((rows, width), lambda t, *_: (jnp.minimum(t, steps - 1), 0))


def adapt_kernel(single_ref, cond_ref, gain, w_scale, b_scale, w_shift, x_ref):
    normed, _ = norm_rows(single_ref[...].astype(f32))
    cond_hat, _ = norm_rows(cond_ref[...].astype(f32))
    cond_low = (cond_hat * gain[...].astype(f32)).astype(bf16)
    gate = jax.nn.sigmoid(dot(cond_low, w_scale[...], NN) + b_scale[...].astype(f32))
    x_ref[...] = (gate * normed + dot(cond_low, w_shift[...], NN)).astype(bf16)


def adapt(single, cond, gain, w_scale, b_scale, w_shift):
    tokens, width = single.shape
    tile = tile_of(tokens)
    steps = tokens // tile
    return pl.pallas_call(
        adapt_kernel,
        grid=(steps,),
        in_specs=[tiled(tile, width, steps), tiled(tile, cond.shape[1], steps)]
        + [fixed(v.shape) for v in (gain, w_scale, b_scale, w_shift)],
        out_specs=tiled(tile, width, steps),
        out_shape=jax.ShapeDtypeStruct((tokens, width), bf16),
        compiler_params=pltpu.CompilerParams(vmem_limit_bytes=VMEM_BYTES),
        cost_estimate=LIGHT,
        name="adapt",
    )(single, cond, gain, w_scale, b_scale, w_shift)


def emit_rows(meta, step, count):
    place = meta[2 + step % 4] * 2 + (meta[1] ^ (step // 4))
    return pl.ds(pl.multiple_of(place * count, count), count)


def middle_kernel(
    meta, x_ref, single_ref, cond_ref, cot_ref, a0, a1, a2, a3,
    w_gate, w_out, w_ac, b_ac, gain, w_scale, b_scale, w_shift, w_hg, w_hu, w_dn, w_tc, b_tc,
    out_ref, dmid_ref, dxg_ref, da0, da1, da2, da3, s_ac, s_scale, s_tc, s_gain, *rest, tiles, fast,
):
    core = meta[0] % 2
    step = pl.program_id(0)
    if fast:
        keep_ref, send_ref, g_hidden, g_square, g_cond, g_norm, g_dn = rest
    else:
        g_hidden, g_square, g_cond, g_norm, g_dn = rest

    @pl.when(step == 0)
    def _():
        for ref in (g_hidden, g_square, g_cond, g_norm, g_dn, s_ac, s_scale, s_tc, s_gain):
            ref[...] = jnp.zeros_like(ref)

    @pl.when(step < tiles)
    def _():
        x_one = x_ref[...]
        cond = cond_ref[...]
        gate = jax.nn.sigmoid(dot(x_one, w_gate[...], NN))
        first = core == 0
        att = jnp.concatenate(
            [
                jnp.where(first, a0[...], a1[...]),
                jnp.where(first, a1[...], a0[...]),
                jnp.where(first, a2[...], a3[...]),
                jnp.where(first, a3[...], a2[...]),
            ],
            axis=1,
        ).astype(f32)
        gated = (att * gate).astype(bf16)
        branch = dot(gated, w_out[...], NN)
        acond = jax.nn.sigmoid(dot(cond, w_ac[...], NN) + b_ac[...].astype(f32))
        mid = single_ref[...].astype(f32) + acond * branch
        cond_hat, _ = norm_rows(cond.astype(f32))
        cond_low = (cond_hat * gain[...].astype(f32)).astype(bf16)
        scale = jax.nn.sigmoid(dot(cond_low, w_scale[...], NN) + b_scale[...].astype(f32))
        normed, inverse = norm_rows(mid)
        x_two = (scale * normed + dot(cond_low, w_shift[...], NN)).astype(bf16)
        hgate = dot(x_two, w_hg[...], NN)
        hup = dot(x_two, w_hu[...], NN)
        sig = jax.nn.sigmoid(hgate)
        silu = hgate * sig
        hidden = (silu * hup).astype(bf16)
        tr_branch = dot(hidden, w_dn[...], NN)
        tcond = jax.nn.sigmoid(dot(cond, w_tc[...], NN) + b_tc[...].astype(f32))
        out_ref[...] = (mid + tcond * tr_branch).astype(bf16)
        dy = cot_ref[...].astype(f32)
        d_tr = (tcond * dy).astype(bf16)
        d_trc = dy * tr_branch * tcond * (1.0 - tcond)
        s_tc[...] += column_sum(d_trc)
        g_cond[0] += dot(cond, d_trc.astype(bf16), TN)
        g_dn[...] += dot(hidden, d_tr, TN)
        d_hidden = dot(d_tr, w_dn[...], NT)
        d_hg = (d_hidden * hup * sig * (1.0 + hgate * (1.0 - sig))).astype(bf16)
        d_hu = (d_hidden * silu).astype(bf16)
        g_hidden[0] += dot(x_two, d_hg, TN)
        g_hidden[1] += dot(x_two, d_hu, TN)
        g_two = dot(d_hg, w_hg[...], NT) + dot(d_hu, w_hu[...], NT)
        d_scale = g_two * normed * scale * (1.0 - scale)
        s_scale[...] += column_sum(d_scale)
        d_scale = d_scale.astype(bf16)
        d_shift = g_two.astype(bf16)
        g_norm[0] += dot(cond_low, d_scale, TN)
        g_norm[1] += dot(cond_low, d_shift, TN)
        d_cond = dot(d_scale, w_scale[...], NT) + dot(d_shift, w_shift[...], NT)
        s_gain[...] += column_sum(d_cond * cond_hat)
        d_mid = dy + norm_back(normed, inverse, g_two * scale)
        dmid_ref[...] = d_mid
        d_attn = (acond * d_mid).astype(bf16)
        d_ac = d_mid * branch * acond * (1.0 - acond)
        s_ac[...] += column_sum(d_ac)
        g_cond[1] += dot(cond, d_ac.astype(bf16), TN)
        g_square[0] += dot(gated, d_attn, TN)
        d_gated = dot(d_attn, w_out[...], NT)
        d_att = (d_gated * gate).astype(bf16)
        d_gate = (d_gated * att * gate * (1.0 - gate)).astype(bf16)
        g_square[1] += dot(x_one, d_gate, TN)
        dxg_ref[...] = dot(d_gate, w_gate[...], NT).astype(bf16)
        q = d_att.shape[1] // 4
        parts = [d_att[:, i * q : (i + 1) * q] for i in range(4)]
        da0[...] = jnp.where(first, parts[0], parts[1])
        da1[...] = jnp.where(first, parts[1], parts[0])
        da2[...] = jnp.where(first, parts[2], parts[3])
        da3[...] = jnp.where(first, parts[3], parts[2])

    if fast:

        @pl.when(step >= tiles)
        def _():
            emit = step - tiles
            for e, ref in enumerate((keep_ref, send_ref)):
                c = core ^ e
                for p in range(2):
                    side = (meta[0] // 2) ^ p
                    at = 0
                    for src, pieces in ((g_hidden, 2), (g_square, 1), (g_cond, 1), (g_norm, 1), (g_dn, 1)):
                        n = src.shape[-2] // 8
                        if src is g_dn:
                            place = meta[2 + emit % 4] * 2 + (meta[1] ^ (emit // 4))
                            rows = pl.ds(pl.multiple_of(place * n + c * (n // 2), n // 2), n // 2)
                            n = n // 2
                        else:
                            rows = emit_rows(meta, emit, n)
                        wide = src.shape[-1] // 2 // pieces
                        for piece in range(pieces):
                            lanes = pl.ds(pl.multiple_of((side * pieces + piece) * wide, wide), wide)
                            part = src[rows, lanes] if src is g_dn else src[c, rows, lanes]
                            ref[p, 0, at : at + n, :] = part.astype(bf16)
                            at += n


def middle(meta, x_one, single, cond, cot, atts, weights, fast):
    tokens, width = single.shape
    tile = tile_of(tokens)
    tiles = tokens // tile
    cs = cond.shape[1]
    quarter = atts[0].shape[1]
    w_gate, w_out, w_ac, b_ac, gain, w_scale, b_scale, w_shift, w_hg, w_hu, w_dn, w_tc, b_tc = weights
    fold = lambda n: jax.ShapeDtypeStruct((1, n), f32)
    sums = [fold(width), fold(width), fold(width), fold(cs)]
    grads = [(2,) + w_hg.shape, (2,) + w_out.shape, (2,) + w_ac.shape, (2,) + w_scale.shape, w_dn.shape]
    row_out = [(width, bf16), (width, f32), (width, bf16)] + [(quarter, bf16)] * 4
    macs = sum(w.size for w in weights if w.shape[0] > 1)
    if fast:
        lanes = width // 2
        rows = sum(w.size for w in weights if w.shape[0] > 1) // (8 * 4 * lanes)
        packed = pl.BlockSpec((2, 1, rows, lanes), lambda t, *_: (0, jnp.maximum(t - tiles, 0), 0, 0))
        more_specs = [packed] * 2
        more = [jax.ShapeDtypeStruct((2, 8, rows, lanes), bf16)] * 2
        scratch = [pltpu.VMEM(g, f32) for g in grads]
    else:
        more_specs = [fixed(g) for g in grads]
        more = [jax.ShapeDtypeStruct(g, f32) for g in grads]
        scratch = []
    return pl.pallas_call(
        functools.partial(middle_kernel, tiles=tiles, fast=fast),
        grid_spec=pltpu.PrefetchScalarGridSpec(
            num_scalar_prefetch=1,
            grid=(tiles + 8 * fast,),
            in_specs=[tiled(tile, w, tiles) for w in (width, width, cs, width)]
            + [tiled(tile, quarter, tiles)] * 4
            + [fixed(w.shape) for w in weights],
            out_specs=[tiled(tile, w, tiles) for w, _ in row_out] + [fixed(g.shape) for g in sums] + more_specs,
            scratch_shapes=scratch,
        ),
        out_shape=[jax.ShapeDtypeStruct((tokens, w), d) for w, d in row_out] + sums + more,
        compiler_params=pltpu.CompilerParams(vmem_limit_bytes=VMEM_BYTES),
        cost_estimate=LIGHT,
        name="middle",
    )(meta, x_one, single, cond, cot, *atts, *weights)


def last_kernel(
    meta, d0, d1, d2, d3, single_ref, cond_ref, dmid_ref, gain, w_scale, b_scale, w_shift,
    out_ref, s_scale, s_gain, *rest, fast,
):
    if fast:
        keep_ref, send_ref, g_norm = rest
    else:
        (g_norm,) = rest

    @pl.when(pl.program_id(0) == 0)
    def _():
        for ref in (g_norm, s_scale, s_gain):
            ref[...] = jnp.zeros_like(ref)

    g_one = d0[...].astype(f32) + d1[...].astype(f32) + d2[...].astype(f32) + d3[...].astype(f32)
    normed, inverse = norm_rows(single_ref[...].astype(f32))
    cond_hat, _ = norm_rows(cond_ref[...].astype(f32))
    cond_low = (cond_hat * gain[...].astype(f32)).astype(bf16)
    scale = jax.nn.sigmoid(dot(cond_low, w_scale[...], NN) + b_scale[...].astype(f32))
    d_scale = g_one * normed * scale * (1.0 - scale)
    s_scale[...] += column_sum(d_scale)
    d_scale = d_scale.astype(bf16)
    d_shift = g_one.astype(bf16)
    g_norm[0] += dot(cond_low, d_scale, TN)
    g_norm[1] += dot(cond_low, d_shift, TN)
    d_cond = dot(d_scale, w_scale[...], NT) + dot(d_shift, w_shift[...], NT)
    s_gain[...] += column_sum(d_cond * cond_hat)
    out_ref[...] = dmid_ref[...] + norm_back(normed, inverse, g_one * scale)

    if fast:

        @pl.when(pl.program_id(0) == pl.num_programs(0) - 1)
        def _():
            n, wide = g_norm.shape[1] // 8, g_norm.shape[2] // 2
            for e, ref in enumerate((keep_ref, send_ref)):
                for p in range(2):
                    lanes = pl.ds(pl.multiple_of(((meta[0] // 2) ^ p) * wide, wide), wide)
                    for i in range(8):
                        ref[p, i] = g_norm[(meta[0] % 2) ^ e, emit_rows(meta, i, n), lanes].astype(bf16)


def last(meta, ds, single, cond, dmid, gain, w_scale, b_scale, w_shift, fast):
    tokens, width = single.shape
    tile = tile_of(tokens)
    steps = tokens // tile
    cs = cond.shape[1]
    grads = (2,) + w_scale.shape
    if fast:
        more = [jax.ShapeDtypeStruct((2, 8, cs // 8, width // 2), bf16)] * 2
        scratch = [pltpu.VMEM(grads, f32)]
    else:
        more = [jax.ShapeDtypeStruct(grads, f32)]
        scratch = []
    more = [jax.ShapeDtypeStruct((1, width), f32), jax.ShapeDtypeStruct((1, cs), f32)] + more
    row = tiled(tile, width, steps)
    return pl.pallas_call(
        functools.partial(last_kernel, fast=fast),
        grid_spec=pltpu.PrefetchScalarGridSpec(
            num_scalar_prefetch=1,
            grid=(steps,),
            in_specs=[row] * 5
            + [tiled(tile, cs, steps), row]
            + [fixed(w.shape) for w in (gain, w_scale, b_scale, w_shift)],
            out_specs=[row] + [fixed(g.shape) for g in more],
            scratch_shapes=scratch,
        ),
        out_shape=[jax.ShapeDtypeStruct((tokens, width), f32)] + more,
        compiler_params=pltpu.CompilerParams(vmem_limit_bytes=VMEM_BYTES),
        cost_estimate=LIGHT,
        name="last",
    )(meta, *ds, single, cond, dmid, gain, w_scale, b_scale, w_shift)


def swap(value, bit):
    return lax.ppermute(value, "head", [(i, i ^ bit) for i in range(lax.axis_size("head"))])


def across(value):
    return lax.ppermute(value, "samp", [(i, i ^ 1) for i in range(8)])


def slot(value, bit):
    return lax.ppermute(value, "samp", [(i, i ^ (2 * bit)) for i in range(8)])


def add(*terms):
    total = terms[0].astype(f32)
    for term in terms[1:]:
        total = total + term.astype(f32)
    return total


def tie(value, *others):
    return lax.optimization_barrier((value,) + others)[0]


def low(*terms):
    return add(*terms).astype(bf16)


Z_ORDER = (0, 2, 1, 3)


def x_step(block):
    return block[:4], across(block[4:])


def z_first(keep, got):
    return slot(low(keep[2:], got[2:]), 1)


def z_second(keep, got, z_got):
    return slot(low(keep[1], got[1], z_got[1]), 2)


def z_total(keep, got, z_got, last_got):
    return add(keep[0], got[0], z_got[0], last_got)


def fence(*values):
    return lax.optimization_barrier(values)


def total_step(vector, step):
    if step < 2:
        return vector + swap(vector, 1 << step)
    if step == 2:
        return vector + across(vector)
    return vector + slot(vector, step - 2)


def pack_w(w_heads, wide):
    return (
        jnp.concatenate([w[:wide] for w in w_heads], axis=0),
        jnp.concatenate([w[wide:] for w in w_heads], axis=0),
    )


def on_device(
    single,
    cond,
    pair,
    complex_length,
    sample_complex,
    cotangent,
    gain_one,
    w_scale_one,
    b_scale_one,
    w_shift_one,
    w_query,
    b_query,
    w_key,
    w_value,
    w_gate,
    w_out,
    w_pair,
    w_attn_cond,
    b_attn_cond,
    gain_two,
    w_scale_two,
    b_scale_two,
    w_shift_two,
    w_hidden_gate,
    w_hidden_up,
    w_hidden_down,
    w_tr_cond,
    b_tr_cond,
):
    groups = lax.axis_size("head")
    devices = lax.axis_size("samp")
    me = lax.axis_index("head")
    place = lax.axis_index("samp")
    core = me % 2
    part = me // 2
    samples, rows, width = single.shape
    cs = cond.shape[2]
    tokens = samples * rows
    length = rows * groups
    heads = w_pair.shape[1]
    few = heads // groups
    dim = width // heads
    wide = few * dim
    complexes, _, columns, _ = pair.shape
    chunks = 2 * groups
    chunk = length // chunks
    halves = range(groups // 2)
    fast = devices == 8 and groups == 4 and columns == chunk
    line = lambda v: v.reshape(1, -1)
    flat = lambda v: v.reshape(tokens, width)
    first = core == 0

    if fast:
        z, x = place // 2, place % 2
        order = z ^ jnp.array(Z_ORDER, jnp.int32)
        slots = jnp.stack([order * 2 + x, order * 2 + 1 - x], axis=1).reshape(8)
    else:
        x = jnp.zeros((), jnp.int32)
        order, slots = jnp.zeros((4,), jnp.int32), jnp.arange(chunks, dtype=jnp.int32)
    meta = jnp.concatenate([jnp.stack([me, x]).astype(jnp.int32), order, sample_complex, slots])
    pair_meta = jnp.stack([me, place]).astype(jnp.int32)
    group = 8
    sizes = dict(few=few, blocks=groups, group=group)
    single_t, cond_t, cot_t = flat(single), cond.reshape(tokens, cs), flat(cotangent)
    weights_one = (line(gain_one), w_scale_one, line(b_scale_one), w_shift_one)
    weights_two = (
        w_gate, w_out, w_attn_cond, line(b_attn_cond), line(gain_two), w_scale_two, line(b_scale_two), w_shift_two,
        w_hidden_gate, w_hidden_up, w_hidden_down, w_tr_cond, line(b_tr_cond),
    )

    def own_columns(w, k):
        return lax.dynamic_slice_in_dim(w, (2 * k + core) * wide, wide, w.ndim - 1)

    w_heads = [jnp.concatenate([own_columns(w, k).T for w in (w_query, w_key, w_value)], axis=0) for k in halves]
    b_heads = [own_columns(b_query.astype(f32), k)[:, None] for k in halves]
    w_q, w_kv = pack_w(w_heads, wide)
    parts = [(k, 0, wide) for k in halves]
    by_sample = lambda v: v.reshape(samples, rows, -1)
    by_token = lambda v: v.reshape(tokens, -1)
    attend_one = lambda k, blocks, biases: attend(meta, blocks, w_heads[k], b_heads[k], biases, nh=few, hd=dim)
    middle_one = lambda x_one, atts: middle(meta, x_one, single_t, cond_t, cot_t, atts, weights_two, fast)
    back_one = lambda kept, own, near: attend_back(
        meta, *kept[2:], *kept[:2], own, near, chunks, complexes, base=0, nh=few, hd=dim, fast=fast
    )

    def q_sums(gb):
        zero = jnp.zeros((wide,), f32)
        out = []
        for k in halves:
            mine = gb[k * wide : (k + 1) * wide, 0]
            out += [jnp.where(first, mine, zero), jnp.where(first, zero, mine)]
        return out

    w_blocked = blocked(w_pair, group)
    pair_low, pair_inverse, pair_raw, *bias = pair_bias(pair_meta, complex_length, pair, w_blocked, **sizes)
    near_bias = [swap(v, 1) for v in bias[groups // 2 :]]
    owns = [jnp.concatenate([bias[k], near_bias[k]], axis=-1) for k in halves]

    if fast:
        owns, single_t = fence(owns, single_t)
        far_0, own_0 = slot(owns[0], 2), across(owns[0])
        x_one = adapt(single_t, cond_t, *weights_one)
        far_0, own_0, x_one, owns = fence(far_0, own_0, x_one, owns)
        x_far = swap(x_one, 2)
        x_near = swap(x_one, 1)
        z_0 = [slot(owns[0], 1), slot(far_0, 1)]
        x_0 = [own_0, across(far_0)]
        far_1, own_1 = slot(owns[1], 2), across(owns[1])
        z_0, x_0, far_1, own_1, owns, x_near = fence(z_0, x_0, far_1, own_1, owns, x_near)
        x_0 += [across(v) for v in z_0]
        z_1 = [slot(owns[1], 1), slot(far_1, 1)]
        x_1 = [own_1, across(far_1)]
        x_far, z_0, x_0, z_1, x_1 = fence(x_far, z_0, x_0, z_1, x_1)
        x_1 += [across(v) for v in z_1]
        x_cross = swap(x_far, 1)
        blocks = [by_sample(v) for v in (x_one, x_near, x_far, x_cross)]
        pairs_of = lambda here, there: [(v, None) for both in zip(here, there) for v in both]
        kept = [attend_one(0, blocks, pairs_of([owns[0], far_0] + z_0, x_0))]
        kept, x_1, z_1 = fence(kept, x_1, z_1)
        near_atts = [swap(kept[0][1], 1)]
        kept.append(attend_one(1, blocks, pairs_of([owns[1], far_1] + z_1, x_1)))
        kept, near_atts = fence(kept, near_atts)
        near_atts.append(swap(kept[1][1], 1))
        atts = [by_token(v) for k in halves for v in (kept[k][0], near_atts[k])]

        block_out, d_mid, d_xg, da0, da1, da2, da3, s_ac, s_scale2, s_tc, s_gain2, keep_mid, send_mid = middle_one(x_one, atts)
        near_att = [swap(by_sample(v), 1) for v in (da1, da3)]
        near_att, keep_mid, send_mid = fence(near_att, keep_mid, send_mid)

        near_mid = swap(send_mid, 1)
        dq_0, dkv_0, *db_0 = back_one(kept[0], by_sample(da0), near_att[0])
        near_mid, dq_0, db_0, kept_1 = fence(near_mid, dq_0, db_0, kept[1])
        half_mid = low(keep_mid[1], near_mid[1])
        half_mid, db_0, kept_1 = fence(half_mid, db_0, kept_1)
        far_mid = swap(half_mid, 2)
        keep_0, got_0 = db_0[:complexes], [across(v) for v in db_0[complexes:]]
        dq_1, dkv_1, *db_1 = back_one(kept_1, by_sample(da2), near_att[1])
        dq_1, db_1 = fence(dq_1, db_1)
        keep_1, got_1 = db_1[:complexes], [across(v) for v in db_1[complexes:]]
        d_near, d_cross, d_far, d_own, gb, keep_w, send_w = heads_back(
            meta, blocks, w_q, w_kv, [(dq_0, dkv_0), (dq_1, dkv_1)], parts, wch=wide, fast=fast
        )
        d_near, d_cross, d_far, gb, send_w, got_0 = fence(d_near, d_cross, d_far, gb, send_w, got_0)

        d_cross, near_x = swap(d_cross, 1), swap(d_near, 1)
        early = jnp.concatenate([s_gain2[0], *q_sums(gb), s_ac[0], s_scale2[0], s_tc[0]])
        early = total_step(early, 0)
        zs_0 = [z_first(k, g) for k, g in zip(keep_0, got_0)]
        d_cross, near_x, far_mid, early = fence(d_cross, near_x, far_mid, early)
        d_half = low(d_far, d_cross)
        far_x = swap(d_half, 2)
        zs_0, far_mid, d_half, got_1[0], early = fence(zs_0, far_mid, d_half, got_1[0], early)
        mid = low(keep_mid[0], near_mid[0], far_mid)
        far_w = swap(send_w, 2)
        last_0 = [z_second(*v) for v in zip(keep_0, got_0, zs_0)]
        zs_1 = [z_first(keep_1[0], got_1[0])]
        early = total_step(early, 2)
        last_0, zs_1, mid, got_1[1], early = fence(last_0, zs_1, mid, got_1[1], early)
        keep_m, got_m = x_step(mid)
        sum_0 = [z_total(*v).astype(bf16) for v in zip(keep_0, got_0, zs_0, last_0)]
        far_rows = [[swap(v[..., rows:], 1) for v in sum_0]]
        last_1 = [z_second(keep_1[0], got_1[0], zs_1[0])]
        zs_1.append(z_first(keep_1[1], got_1[1]))
        last_1, zs_1, far_w, sum_0 = fence(last_1, zs_1, far_w, sum_0)
        last_1.append(z_second(keep_1[1], got_1[1], zs_1[1]))
        grad_w = low(keep_w, far_w)
        keep_h, got_h = x_step(grad_w)
        last_1, got_m, got_h, early = fence(last_1, got_m, got_h, early)
        sum_1 = [z_total(*v).astype(bf16) for v in zip(keep_1, got_1, zs_1, last_1)]
        far_rows.append([swap(v[..., rows:], 1) for v in sum_1])
        far_rows, far_x = fence(far_rows, far_x)
        z_m, z_h = z_first(keep_m, got_m), z_first(keep_h, got_h)
        early = total_step(early, 1)
        grad_single, s_scale1, s_gain1, keep_l, send_l = last(
            meta, (flat(d_own), flat(near_x), far_x.reshape(tokens, width), d_xg), single_t, cond_t, d_mid, *weights_one, fast
        )
        z_m, z_h, keep_l, send_l, far_rows = fence(z_m, z_h, keep_l, send_l, far_rows)
        near_l = swap(send_l, 1)
        e_m, e_h = z_second(keep_m, got_m, z_m), z_second(keep_h, got_h, z_h)
        stacked = lambda v: jnp.stack(v)
        pair_grads = [stacked([v[..., :rows] for v in s]) for s in (sum_0, sum_1)] + [stacked(v) for v in far_rows]
        grad_pair, grad_pair_weight = pair_back(pair_meta, pair_low, pair_inverse, pair_raw, w_pair, pair_grads, **sizes)
        near_l, e_m, e_h, grad_pair_weight = fence(near_l, e_m, e_h, grad_pair_weight)
        r_heads = z_total(keep_h, got_h, z_h, e_h)
        packed = z_total(keep_m, got_m, z_m, e_m)
        far_l = swap(low(keep_l[1], near_l[1]), 2)
        late = total_step(jnp.concatenate([grad_pair_weight.reshape(-1), s_gain1[0], s_scale1[0]]), 0)

        def settle(block, tall=False):
            half = block.shape[1] // 2
            left, right = block[:, :half], block[:, half:]
            got = swap(jnp.where(first, right, left), 1)
            held = jnp.where(first, left, right)
            pair_of = (jnp.where(first, held, got), jnp.where(first, got, held))
            return jnp.concatenate(pair_of, axis=0) if tall else pair_of

        n, m = width // 8, cs // 8
        hidden = jnp.concatenate([packed[0:n], packed[n : 2 * n]], axis=1)
        r_hg, r_hu = settle(hidden)
        r_out, r_gate = settle(packed[2 * n : 3 * n])
        r_tc, r_ac = settle(packed[3 * n : 3 * n + m])
        r_scale2, r_shift2 = settle(packed[3 * n + m : 3 * n + 2 * m])
        r_down = settle(packed[3 * n + 2 * m :], tall=True)
        far_l, late, early = fence(far_l, late, early)
        keep_l, got_l = x_step(low(keep_l[0], near_l[0], far_l))
        late, early = total_step(late, 1), total_step(early, 3)
        got_l, late, early = fence(got_l, late, early)
        z_l = z_first(keep_l, got_l)
        late, early = total_step(late, 2), total_step(early, 4)
        z_l, late, early = fence(z_l, late, early)
        e_l = z_second(keep_l, got_l, z_l)
        late = total_step(late, 3)
        e_l, late = fence(e_l, late)
        r_scale1, r_shift1 = settle(z_total(keep_l, got_l, z_l, e_l))
        late = total_step(late, 4)
    else:
        biases = []
        for own in owns:
            gathered = lax.all_gather(own, "samp", axis=0)
            moved = gathered.transpose(1, 2, 0, 3, 4).reshape(complexes, few, chunks, chunk, 2 * rows)
            biases.append([(moved[:, :, i], None) for i in range(chunks)])
        x_one = adapt(single_t, cond_t, *weights_one)
        x_far = swap(x_one, 2)
        blocks = [by_sample(v) for v in (x_one, swap(x_one, 1), x_far, swap(x_far, 1))]
        kept = [attend_one(k, blocks, biases[k]) for k in halves]
        atts = [by_token(v) for k in halves for v in (kept[k][0], swap(kept[k][1], 1))]
        block_out, d_mid, d_xg, da0, da1, da2, da3, s_ac, s_scale2, s_tc, s_gain2, *w_mid = middle_one(x_one, atts)
        head_grads, sums = [], []
        for k, (own, sent) in enumerate(((da0, da1), (da2, da3))):
            dq, dkv, db = back_one(kept[k], by_sample(own), swap(by_sample(sent), 1))
            head_grads.append((dq, dkv))
            moved = db.transpose(1, 2, 0, 3, 4).reshape(complexes, few, devices, columns, 2 * rows)
            sums.append(lax.psum_scatter(moved, "samp", scatter_dimension=2, tiled=False))
        d_near, d_cross, d_far, d_own, gb, gq, gkv = heads_back(
            meta, blocks, w_q, w_kv, head_grads, parts, wch=wide, fast=fast
        )
        far_x = swap(low(d_far, swap(d_cross, 1)), 2)
        grad_single, s_scale1, s_gain1, w_last = last(
            meta, (flat(d_own), flat(swap(d_near, 1)), flat(far_x), d_xg), single_t, cond_t, d_mid, *weights_one, fast
        )
        pair_grads = [v[..., :rows] for v in sums] + [swap(v[..., rows:], 1) for v in sums]
        grad_pair, grad_pair_weight = pair_back(pair_meta, pair_low, pair_inverse, pair_raw, w_pair, pair_grads, **sizes)

        def total_of(stack):
            axis = stack.ndim - 1
            half = lax.psum_scatter(stack.astype(bf16), "head", scatter_dimension=axis, tiled=True).astype(f32)
            return lax.psum_scatter(half, "samp", scatter_dimension=axis - 1, tiled=True)

        grads = [
            jnp.concatenate([gq[k * wide : (k + 1) * wide], gkv[2 * k * wide : 2 * (k + 1) * wide]], axis=0) for k in halves
        ]
        held = jnp.where(part == 0, grads[0], grads[1])
        sent = jnp.where(part == 0, grads[1], grads[0])
        r_heads = add(held, swap(sent.astype(bf16), 2))
        r_heads = lax.psum_scatter(r_heads.T, "samp", scatter_dimension=0, tiled=True)
        (r_hg, r_hu), (r_out, r_gate), (r_tc, r_ac), (r_scale2, r_shift2), r_down = [total_of(v) for v in w_mid]
        r_scale1, r_shift1 = total_of(w_last)
        early = jnp.concatenate([s_gain2[0], *q_sums(gb), s_ac[0], s_scale2[0], s_tc[0]])
        late = jnp.concatenate([grad_pair_weight.reshape(-1), s_gain1[0], s_scale1[0]])
        early, late = lax.psum((early, late), ("samp", "head"))

    cuts = [cs, cs + width, cs + 2 * width, cs + 3 * width]
    sum_gain2, sum_query, sum_ac, sum_scale2, sum_tc = jnp.split(early, cuts)
    pair_size = heads * w_pair.shape[0]
    sum_pair, sum_gain1, sum_scale1 = jnp.split(late, [pair_size, pair_size + cs])
    whole = (samples, rows, width)
    return (
        block_out.reshape(whole),
        grad_single.reshape(whole),
        grad_pair,
        sum_gain1,
        r_scale1,
        sum_scale1,
        r_shift1,
        r_heads[:, :wide],
        sum_query,
        r_heads[:, wide : 2 * wide],
        r_heads[:, 2 * wide :],
        r_gate,
        r_out,
        sum_pair.reshape(heads, -1).T,
        r_ac,
        sum_ac,
        sum_gain2,
        r_scale2,
        sum_scale2,
        r_shift2,
        r_hg,
        r_hu,
        r_down,
        r_tc,
        sum_tc,
    )


def solution(mesh):
    placed = (
        P("samp", "head", None),
        P("samp", "head", None),
        P(None, "head", "samp", None),
        P(),
        P("samp"),
        P("samp", "head", None),
        P(),
        P(),
        P(),
        P(),
        P(),
        P(),
        P(),
        P(),
        P(),
        P(),
        P(),
        P(),
        P(),
        P(),
        P(),
        P(),
        P(),
        P(),
        P(),
        P(),
        P(),
        P(),
    )
    return jax.shard_map(
        on_device,
        mesh=mesh,
        in_specs=placed,
        out_specs=(
            P("samp", "head", None),
            P("samp", "head", None),
            P(None, "head", "samp", None),
            P(),
            P("samp", "head"),
            P(),
            P("samp", "head"),
            P("samp", "head"),
            P(),
            P("samp", "head"),
            P("samp", "head"),
            P("samp", "head"),
            P("samp", "head"),
            P(),
            P("samp", "head"),
            P(),
            P(),
            P("samp", "head"),
            P(),
            P("samp", "head"),
            P("samp", "head"),
            P("samp", "head"),
            P("samp", "head"),
            P("samp", "head"),
            P(),
        ),
        check_vma=False,
    )
```

```python
import functools
import math

import jax
import jax.numpy as jnp
from jax import lax
from jax.experimental import pallas as pl
from jax.experimental.pallas import tpu as pltpu
from jax.sharding import PartitionSpec as P

f32, bf16 = jnp.float32, jnp.bfloat16
epsilon = 1e-05
fill_value = -1e30
LOG2E = math.log2(math.e)
VMEM_BYTES = 60 << 20
PAIR_LINES = (8, 16, 24, 32, 64)
NN, NT, TN = ((1,), (0,)), ((1,), (1,)), ((0,), (0,))


LIGHT = pl.CostEstimate(flops=1 << 20, bytes_accessed=1 << 20, transcendentals=0)


def dot(a, b, dims):
    return lax.dot_general(a, b, (dims, ((), ())), preferred_element_type=f32)


def norm_rows(inputs):
    mean_val = jnp.mean(inputs, axis=-1, keepdims=True)
    centered = inputs - mean_val
    variance = jnp.mean(centered * centered, axis=-1, keepdims=True)
    inverse = lax.rsqrt(variance + epsilon)
    return (centered * inverse, inverse)


def norm_back(normed, inverse, upstream):
    mean_grad = jnp.mean(upstream, axis=-1, keepdims=True)
    mean_dot = jnp.mean(upstream * normed, axis=-1, keepdims=True)
    return inverse * (upstream - mean_grad - normed * mean_dot)


def tile_of(tokens, sizes=(8, 16, 32, 64, 128, 256)):
    return max(t for t in sizes if tokens % t == 0)


def fixed(shape):
    return pl.BlockSpec(shape, lambda *_: (0,) * len(shape), pipeline_mode=pl.Buffered(1))


META = 6


def attend_kernel(meta, x0, x1, x2, x3, w_ref, bq_ref, *rest, which, nh, hd, rows, jc, nchunk, qscale):
    bias_hbm = rest[:nchunk]
    o_ref, far_ref, p_ref, q_ref, k_ref, v_ref, l_ref, xs, ks, ss, bias_ref, sems = rest[nchunk:]
    b = pl.program_id(0)
    g = meta[0]
    cplx = meta[META + b]
    per_block = nchunk // 4

    def copies():
        return [
            pltpu.make_async_copy(
                bias_hbm[i] if which[i] is None else bias_hbm[i].at[which[i]],
                bias_ref.at[meta[META + pl.num_programs(0) + i]],
                sems.at[i],
            )
            for i in range(nchunk)
        ]

    @pl.when(b == 0)
    def _():
        for copy in copies():
            copy.start()

    for r, x in enumerate((x0, x1, x2, x3)):
        xs[r * rows : (r + 1) * rows, :] = x[0]
    wch = nh * hd
    q = dot(w_ref[0:wch, :], xs[0 : 2 * rows, :], NT) + bq_ref[...]
    q_ref[0] = (q * qscale).astype(bf16)
    kv = dot(w_ref[wch : 3 * wch, :], xs[...], NT).astype(bf16)
    k_ref[0] = kv[0:wch]
    v_ref[0] = kv[wch:]

    @pl.when(b == 0)
    def _():
        for copy in copies():
            copy.wait()

    ones = jnp.ones((16, kv.shape[1]), bf16)
    outs = []
    sums = []
    before = None
    for h in range(nh + 1):
        if h < nh:
            ks[h % 2, :, :] = jnp.transpose(k_ref[0, h * hd : (h + 1) * hd, :])
            qT = q_ref[0, h * hd : (h + 1) * hd, :]
        m = None
        for t in range(nchunk):
            part = slice(t * jc, (t + 1) * jc)
            if h < nh:
                s_idx = ((t // per_block) ^ g) * per_block + t % per_block
                s = dot(ks[h % 2, part, :], qT, NN) + bias_ref[s_idx, cplx, h].astype(f32)
                ss[h % 2, part, :] = s
                mt = jnp.max(s.reshape(jc // 8, 8, s.shape[1]), axis=0)
                m = mt if m is None else jnp.maximum(m, mt)
            if h > 0:
                p_ref[0, h - 1, part, :] = jnp.exp2(ss[(h - 1) % 2, part, :] - before).astype(bf16)
        if h < nh:
            m = jnp.max(m, axis=0, keepdims=True)
        if h > 0:
            va = jnp.concatenate([v_ref[0, (h - 1) * hd : h * hd, :], ones], axis=0)
            oT = dot(va, p_ref[0, h - 1], NN)
            l = oT[hd : hd + 1, :]
            outs.append(oT[:hd] / l)
            sums.append(l)
        before = m
    l_ref[0] = jnp.concatenate(sums, axis=0)
    o = jnp.transpose(jnp.concatenate(outs, axis=0)).astype(bf16)
    o_ref[0] = o[:rows]
    far_ref[0] = o[rows:]


def attend(meta, xb, wT, bq, biases, *, nh, hd):
    B, rows, C = xb[0].shape
    nchunk = len(biases)
    biases, which = zip(*biases)
    ncx, _, jc, qi = biases[0].shape[-4:]
    L = nchunk * jc
    wch = nh * hd
    kern = functools.partial(
        attend_kernel, which=which, nh=nh, hd=hd, rows=rows, jc=jc, nchunk=nchunk, qscale=LOG2E / math.sqrt(hd)
    )
    xspec = pl.BlockSpec((1, rows, C), lambda b, m: (b, 0, 0))
    per = lambda shape: pl.BlockSpec((1,) + shape, lambda b, m: (b,) + (0,) * len(shape))
    return pl.pallas_call(
        kern,
        grid_spec=pltpu.PrefetchScalarGridSpec(
            num_scalar_prefetch=1,
            grid=(B,),
            in_specs=[xspec] * 4
            + [fixed(wT.shape), fixed(bq.shape)]
            + [pl.BlockSpec(memory_space=pl.ANY)] * nchunk,
            out_specs=[
                per((rows, wch)),
                per((rows, wch)),
                per((nh, L, qi)),
                per((wch, qi)),
                per((wch, L)),
                per((wch, L)),
                per((nh, qi)),
            ],
            scratch_shapes=[
                pltpu.VMEM((L, C), bf16),
                pltpu.VMEM((2, L, hd), bf16),
                pltpu.VMEM((2, L, qi), f32),
                pltpu.VMEM((nchunk, ncx, nh, jc, qi), bf16),
                pltpu.SemaphoreType.DMA((nchunk,)),
            ],
        ),
        out_shape=[
            jax.ShapeDtypeStruct((B, rows, wch), bf16),
            jax.ShapeDtypeStruct((B, rows, wch), bf16),
            jax.ShapeDtypeStruct((B, nh, L, qi), bf16),
            jax.ShapeDtypeStruct((B, wch, qi), bf16),
            jax.ShapeDtypeStruct((B, wch, L), bf16),
            jax.ShapeDtypeStruct((B, wch, L), bf16),
            jax.ShapeDtypeStruct((B, nh, qi), f32),
        ],
        compiler_params=pltpu.CompilerParams(vmem_limit_bytes=VMEM_BYTES),
        cost_estimate=LIGHT,
        name="attend",
    )(meta, *xb, wT, bq, *biases)


def attend_back_kernel(
    meta, p_ref, q_ref, k_ref, v_ref, l_ref, o0, o1, do0, do1, *rest, base, nh, hd, jc, nchunk, scale, fast
):
    dq_ref, dkv_ref = rest[:2]
    vs, ds, acc = rest[-3:]
    b = pl.program_id(0)
    g = meta[0]
    cplx = meta[META + b]
    per_block = nchunk // 4
    wch = nh * hd
    L = nchunk * jc

    @pl.when(b == 0)
    def _():
        acc[...] = jnp.zeros_like(acc)

    dO = jnp.transpose(jnp.concatenate([do0[0], do1[0]], axis=0).astype(f32))
    O = jnp.transpose(jnp.concatenate([o0[0], o1[0]], axis=0).astype(f32))
    prod = dO * O
    qi = dO.shape[1]
    row = lax.broadcasted_iota(jnp.int32, (16, qi), 0)
    ones = jnp.ones((16, L), bf16)
    for h in range(nh + 1):
        if h < nh:
            hs = slice(h * hd, (h + 1) * hd)
            his = slice((base + h) * hd, (base + h + 1) * hd)
            linv = 1.0 / l_ref[0, base + h : base + h + 1, :]
            dOh = (dO[his] * linv).astype(bf16)
            delta = jnp.sum(prod[his], axis=0, keepdims=True) * linv
            hi = delta.astype(bf16).astype(f32)
            extra = jnp.where(row == 0, -hi, jnp.where(row == 1, hi - delta, 0.0)).astype(bf16)
            dOa = jnp.concatenate([dOh, extra], axis=0)
            vs[h % 2] = jnp.transpose(jnp.concatenate([v_ref[0, hs, :], ones], axis=0))
        if h > 0:
            ps = slice((h - 1) * hd, h * hd)
            dk_parts, dv_parts = [], []
            kk, qq = k_ref[0, ps, :], q_ref[0, ps, :]
        for t in range(nchunk):
            r, u = t // per_block, t % per_block
            s_idx = (r ^ g) * per_block + u
            ts = slice(t * jc, (t + 1) * jc)
            if h < nh:
                d = dot(vs[h % 2, ts, :], dOa, NN) * p_ref[0, h, ts, :].astype(f32)
                acc[s_idx, cplx, h] += d
                ds[h % 2, ts, :] = d.astype(bf16)
            if h > 0:
                dk_parts.append(dot(ds[(h - 1) % 2, ts, :], qq, NT))
                dv_parts.append(dot(p_ref[0, h - 1, ts, :], dO_before, NT))
        if h > 0:
            dq_ref[0, ps, :] = (dot(kk, ds[(h - 1) % 2], NN) * scale).astype(bf16)
            dk = jnp.transpose(jnp.concatenate(dk_parts, axis=0)) * (1.0 / LOG2E)
            dkv_ref[0, ps, :] = dk.astype(bf16)
            dv = jnp.transpose(jnp.concatenate(dv_parts, axis=0))
            dkv_ref[0, wch + (h - 1) * hd : wch + h * hd, :] = dv.astype(bf16)
        if h < nh:
            dO_before = dOh

    @pl.when(b == pl.num_programs(0) - 1)
    def _():
        if fast:
            for i in range(4):
                for e in range(2):
                    block = acc[meta[2 + i] * 2 + (meta[1] ^ e)].astype(bf16)
                    for c in range(block.shape[0]):
                        rest[2 + 2 * c + e][i] = block[c]
        else:
            rest[2][...] = acc[...].astype(bf16)


def attend_back(meta, p, q, k, v, l, o0, o1, do0, do1, nchunk, ncx, *, base, nh, hd, fast):
    B, held, L, qi = p.shape
    rows = o0.shape[1]
    jc = L // nchunk
    wch = nh * hd
    kern = functools.partial(
        attend_back_kernel, base=base, nh=nh, hd=hd, jc=jc, nchunk=nchunk, scale=1.0 / math.sqrt(hd), fast=fast
    )
    per = lambda shape: pl.BlockSpec((1,) + shape, lambda b, m: (b,) + (0,) * len(shape))
    some = lambda shape: pl.BlockSpec((1,) + shape, lambda b, m: (b, base // nh) + (0,) * (len(shape) - 1))
    db = (nchunk, ncx, nh, jc, qi)
    outs = [((4,) + db[2:], bf16)] * (2 * ncx) if fast else [(db, bf16)]
    return pl.pallas_call(
        kern,
        grid_spec=pltpu.PrefetchScalarGridSpec(
            num_scalar_prefetch=1,
            grid=(B,),
            in_specs=[some((nh, L, qi)), some((wch, qi)), some((wch, L)), some((wch, L)), per((held, qi))]
            + [per((rows, held * hd))] * 4,
            out_specs=[per((wch, qi)), per((2 * wch, L))] + [fixed(s) for s, _ in outs],
            scratch_shapes=[
                pltpu.VMEM((2, L, hd + 16), bf16),
                pltpu.VMEM((2, L, qi), bf16),
                pltpu.VMEM(db, f32),
            ],
        ),
        out_shape=[jax.ShapeDtypeStruct((B, wch, qi), bf16), jax.ShapeDtypeStruct((B, 2 * wch, L), bf16)]
        + [jax.ShapeDtypeStruct(s, d) for s, d in outs],
        compiler_params=pltpu.CompilerParams(vmem_limit_bytes=VMEM_BYTES),
        cost_estimate=LIGHT,
        name="attend_back",
    )(meta, p, q, k, v, l, o0, o1, do0, do1)


def heads_back_kernel(meta, x0, x1, x2, x3, wq_ref, wkv_ref, *rest, parts, rows, wch, fast):
    n = len(parts)
    dqs, dkvs = rest[:n], rest[n : 2 * n]
    near_ref, cross_ref, far_ref, own_ref, gb_ref = rest[2 * n : 2 * n + 5]
    if fast:
        keep_ref, send_ref, xs, dq, dkv, gq, gkv, gt = rest[2 * n + 5 :]
    else:
        gq, gkv, xs, dq, dkv = rest[2 * n + 5 :]
    b = pl.program_id(0)

    @pl.when(b == 0)
    def _():
        gq[...] = jnp.zeros_like(gq)
        gkv[...] = jnp.zeros_like(gkv)
        gb_ref[...] = jnp.zeros_like(gb_ref)

    for r, x in enumerate((x0, x1, x2, x3)):
        xs[r * rows : (r + 1) * rows, :] = x[0]
    for (chunk, at, size), q, kv in zip(parts, dqs, dkvs):
        start = chunk * wch + at
        dq[start : start + size, :] = q[0]
        start = 2 * chunk * wch + at
        dkv[start : start + size, :] = kv[0, :size]
        dkv[start + wch : start + wch + size, :] = kv[0, size:]
    q, kv = dq[...], dkv[...]
    gb_ref[...] += jnp.sum(q.astype(f32), axis=1, keepdims=True)
    gq[...] += dot(q, xs[0 : 2 * rows, :], NN)
    gkv[...] += dot(kv, xs[...], NN)
    kv = jnp.transpose(kv)
    q = jnp.transpose(q)
    dx = dot(kv[2 * rows :], wkv_ref[...], NN).astype(bf16)
    far_ref[0] = dx[:rows]
    cross_ref[0] = dx[rows:]
    dx = (dot(kv[: 2 * rows], wkv_ref[...], NN) + dot(q, wq_ref[...], NN)).astype(bf16)
    own_ref[0] = dx[:rows]
    near_ref[0] = dx[rows:]

    if fast:

        @pl.when(b == pl.num_programs(0) - 1)
        def _():
            for e, ref in enumerate((keep_ref, send_ref)):
                chunk = (meta[0] // 2) ^ e
                half = pl.ds(pl.multiple_of(chunk * wch, wch), wch)
                gt[:, 0:wch] = jnp.transpose(gq[half, :])
                both = pl.ds(pl.multiple_of(chunk * 2 * wch, wch), 2 * wch)
                gt[:, wch:] = jnp.transpose(gkv[both, :])
                count = gt.shape[0] // 8
                for i in range(8):
                    ref[i] = gt[emit_rows(meta, i, count), :].astype(bf16)


def heads_back(meta, xb, wq, wkv, grads, parts, *, wch, fast):
    B, rows, C = xb[0].shape
    L = 4 * rows
    total = wq.shape[0]
    row = pl.BlockSpec((1, rows, C), lambda b, m: (b, 0, 0))
    per = lambda shape: pl.BlockSpec((1,) + shape, lambda b, m: (b,) + (0,) * len(shape))
    dqs, dkvs = [g[0] for g in grads], [g[1] for g in grads]
    sums = [((total, C), f32), ((2 * total, C), f32)]
    held = [pltpu.VMEM((L, C), bf16), pltpu.VMEM((total, 2 * rows), bf16), pltpu.VMEM((2 * total, L), bf16)]
    if fast:
        outs = [((8, C // 8, 3 * wch), bf16)] * 2
        held += [pltpu.VMEM(s, d) for s, d in sums] + [pltpu.VMEM((C, 3 * wch), f32)]
    else:
        outs = sums
    outs = [((total, 1), f32)] + outs
    return pl.pallas_call(
        functools.partial(heads_back_kernel, parts=parts, rows=rows, wch=wch, fast=fast),
        grid_spec=pltpu.PrefetchScalarGridSpec(
            num_scalar_prefetch=1,
            grid=(B,),
            in_specs=[row] * 4
            + [fixed(wq.shape), fixed(wkv.shape)]
            + [per(v.shape[1:]) for v in dqs + dkvs],
            out_specs=[row] * 4 + [fixed(s) for s, _ in outs],
            scratch_shapes=held,
        ),
        out_shape=[jax.ShapeDtypeStruct((B, rows, C), bf16)] * 4 + [jax.ShapeDtypeStruct(s, d) for s, d in outs],
        compiler_params=pltpu.CompilerParams(vmem_limit_bytes=VMEM_BYTES),
        cost_estimate=LIGHT,
        name="heads_back",
    )(meta, *xb, wq, wkv, *dqs, *dkvs)


def blocked(w, count):
    across, heads = w.shape
    wide = jnp.tile(jnp.transpose(w), (count, count))
    row = lax.broadcasted_iota(jnp.int32, wide.shape, 0) // heads
    column = lax.broadcasted_iota(jnp.int32, wide.shape, 1) // across
    return jnp.where(row == column, wide, jnp.zeros_like(wide))


def pair_bias_kernel(meta, lens, pair_ref, wb_ref, low_ref, inv_ref, raw_ref, *rest, few, blocks, group):
    outs, scr = rest[:-1], rest[-1]
    c, t = pl.program_id(0), pl.program_id(1)
    lines, columns, cz = pair_ref.shape[1:]
    heads = few * blocks
    per = lines // group
    mean = jnp.full((cz, cz), 1.0 / cz, bf16)
    lane = lax.broadcasted_iota(jnp.int32, (columns, group * heads), 1) // heads
    table = []
    for n in range(per):
        x = [pair_ref[0, n * group + i] for i in range(group)]
        flat = columns % 16 == 0
        if flat:
            x = [jnp.concatenate(x, axis=0)]
        lows, inverses = [], []
        for v in x:
            centered = v.astype(f32) - dot(v, mean, NN)
            inverse = lax.rsqrt(dot((centered * centered).astype(bf16), mean, NN) + epsilon)
            lows.append((centered * inverse).astype(bf16))
            inverses.append(inverse)
        if flat:
            lows = [lows[0][i * columns : (i + 1) * columns] for i in range(group)]
            inverses = [inverses[0][i * columns : (i + 1) * columns] for i in range(group)]
        spread = inverses[0][:, : group * heads]
        for i in range(1, group):
            spread = jnp.where(lane == i, inverses[i][:, : group * heads], spread)
        inv_ref[0, n] = spread
        for i in range(group):
            low_ref[0, n * group + i] = lows[i]
        table.append(jnp.concatenate(lows, axis=1))
    out = dot(jnp.concatenate(table, axis=0), wb_ref[...], NT)
    for n in range(per):
        part = out[n * columns : (n + 1) * columns]
        raw_ref[0, n] = part
        start = pl.multiple_of((t * per + n) * group * heads, group * heads)
        scr[pl.ds(start, group * heads), :] = jnp.transpose(part)

    @pl.when(t == pl.num_programs(1) - 1)
    def _():
        core = meta[0] % 2
        rows = scr.shape[0] // heads
        place = lax.broadcasted_iota(jnp.int32, (columns, rows), 0) + meta[1] * columns
        valid = place < lens[c]
        half = len(outs) // 2
        for k in range(half):
            for f in range(few):
                for e in range(2):
                    h = (2 * k + (core ^ e)) * few + f
                    v = jnp.transpose(scr[pl.ds(h, rows, stride=heads), :])
                    outs[e * half + k][0, f] = jnp.where(valid, v * LOG2E, fill_value).astype(bf16)


def pair_specs(pair, heads, group):
    lines = tile_of(pair.shape[1], PAIR_LINES)
    columns, cz = pair.shape[2:]
    return (
        lines,
        pl.BlockSpec((1, lines, columns, cz), lambda c, t, *_: (c, t, 0, 0)),
        pl.BlockSpec((1, lines // group, columns, group * heads), lambda c, t, *_: (c, t, 0, 0)),
        jax.ShapeDtypeStruct((pair.shape[0], pair.shape[1] // group, columns, group * heads), f32),
    )


def pair_bias(meta, lens, pair, wb, *, few, blocks, group):
    ncx, rows, columns, cz = pair.shape
    heads = few * blocks
    lines, spec, thin, thin_shape = pair_specs(pair, heads, group)
    out = jax.ShapeDtypeStruct((ncx, few, columns, rows), bf16)
    return pl.pallas_call(
        functools.partial(pair_bias_kernel, few=few, blocks=blocks, group=group),
        grid_spec=pltpu.PrefetchScalarGridSpec(
            num_scalar_prefetch=2,
            grid=(ncx, rows // lines),
            in_specs=[spec, fixed(wb.shape)],
            out_specs=[spec, thin, thin]
            + [pl.BlockSpec((1, few, columns, rows), lambda c, t, *_: (c, 0, 0, 0))] * blocks,
            scratch_shapes=[pltpu.VMEM((rows * heads, columns), f32)],
        ),
        out_shape=[jax.ShapeDtypeStruct(pair.shape, bf16), thin_shape, thin_shape] + [out] * blocks,
        compiler_params=pltpu.CompilerParams(vmem_limit_bytes=VMEM_BYTES),
        cost_estimate=LIGHT,
        name="pair_bias",
    )(meta, lens, pair, wb)


def pair_back_kernel(meta, low_ref, inv_ref, raw_ref, w2_ref, mean_ref, *rest, few, blocks, group):
    grads = rest[:blocks]
    out_ref, gw_ref, scr, acc = rest[blocks:]
    c, t = pl.program_id(0), pl.program_id(1)
    lines, columns, cz = low_ref.shape[1:]
    heads = few * blocks
    per = lines // group

    @pl.when((c == 0) & (t == 0))
    def _():
        acc[...] = jnp.zeros_like(acc)

    @pl.when(t == 0)
    def _():
        core = meta[0] % 2
        rows = scr.shape[0] // heads
        half = blocks // 2
        for k in range(half):
            for f in range(few):
                for e in range(2):
                    h = (2 * k + (core ^ e)) * few + f
                    scr[pl.ds(h, rows, stride=heads), :] = jnp.transpose(grads[e * half + k][0, f].astype(f32))

    ds, prods, xs = [], [], []
    for n in range(per):
        start = pl.multiple_of((t * per + n) * group * heads, group * heads)
        x = jnp.transpose(scr[pl.ds(start, group * heads), :])
        d = x * inv_ref[0, n]
        prod = d * raw_ref[0, n]
        hi = prod.astype(bf16)
        d = d.astype(bf16)
        xs.append(x.astype(bf16))
        ds.append(jnp.concatenate([d, d], axis=1))
        prods.append(jnp.concatenate([hi, (prod - hi.astype(f32)).astype(bf16)], axis=1))
    upstream = dot(jnp.concatenate(ds, axis=0), w2_ref[...], NN)
    along = dot(jnp.concatenate(prods, axis=0), mean_ref[...], NN)
    table = []
    for n in range(per):
        lows = [low_ref[0, n * group + i] for i in range(group)]
        ns = slice(n * columns, (n + 1) * columns)
        for i in range(group):
            zs = slice(i * cz, (i + 1) * cz)
            out_ref[0, n * group + i] = upstream[ns, zs] - lows[i].astype(f32) * along[ns, zs]
        table.append(jnp.concatenate(lows, axis=1))
    acc[...] += dot(jnp.concatenate(xs, axis=0), jnp.concatenate(table, axis=0), TN)

    @pl.when((c == pl.num_programs(0) - 1) & (t == pl.num_programs(1) - 1))
    def _():
        total = acc[0:heads, 0:cz]
        for i in range(1, group):
            total += acc[i * heads : (i + 1) * heads, i * cz : (i + 1) * cz]
        gw_ref[...] = total


def pair_back(meta, low, inv, raw, w, grads, *, few, blocks, group):
    ncx, rows, columns, cz = low.shape
    heads = few * blocks
    lines, spec, thin, _ = pair_specs(low, heads, group)
    mean = jnp.mean(w.astype(f32), axis=0, keepdims=True)
    w2 = jnp.concatenate([blocked(w, group), blocked(jnp.broadcast_to(-mean, w.shape).astype(bf16), group)], axis=0)
    ones = blocked(jnp.full(w.shape, 1.0 / cz, bf16), group)
    ones = jnp.concatenate([ones, ones], axis=0)
    return pl.pallas_call(
        functools.partial(pair_back_kernel, few=few, blocks=blocks, group=group),
        grid_spec=pltpu.PrefetchScalarGridSpec(
            num_scalar_prefetch=1,
            grid=(ncx, rows // lines),
            in_specs=[spec, thin, thin, fixed(w2.shape), fixed(ones.shape)]
            + [pl.BlockSpec((1, few, columns, rows), lambda c, t, *_: (c, 0, 0, 0))] * blocks,
            out_specs=[spec, fixed((heads, cz))],
            scratch_shapes=[pltpu.VMEM((rows * heads, columns), f32), pltpu.VMEM((group * heads, group * cz), f32)],
        ),
        out_shape=[jax.ShapeDtypeStruct(low.shape, f32), jax.ShapeDtypeStruct((heads, cz), f32)],
        compiler_params=pltpu.CompilerParams(vmem_limit_bytes=VMEM_BYTES),
        cost_estimate=LIGHT,
        name="pair_back",
    )(meta, low, inv, raw, w2, ones, *grads)


def column_sum(v):
    return jnp.sum(v, axis=0, keepdims=True)


def tiled(rows, width, steps):
    return pl.BlockSpec((rows, width), lambda t, *_: (jnp.minimum(t, steps - 1), 0))


def adapt_kernel(single_ref, cond_ref, gain, w_scale, b_scale, w_shift, x_ref):
    normed, _ = norm_rows(single_ref[...].astype(f32))
    cond_hat, _ = norm_rows(cond_ref[...].astype(f32))
    cond_low = (cond_hat * gain[...].astype(f32)).astype(bf16)
    gate = jax.nn.sigmoid(dot(cond_low, w_scale[...], NN) + b_scale[...].astype(f32))
    x_ref[...] = (gate * normed + dot(cond_low, w_shift[...], NN)).astype(bf16)


def adapt(single, cond, gain, w_scale, b_scale, w_shift):
    tokens, width = single.shape
    tile = tile_of(tokens)
    steps = tokens // tile
    return pl.pallas_call(
        adapt_kernel,
        grid=(steps,),
        in_specs=[tiled(tile, width, steps), tiled(tile, cond.shape[1], steps)]
        + [fixed(v.shape) for v in (gain, w_scale, b_scale, w_shift)],
        out_specs=tiled(tile, width, steps),
        out_shape=jax.ShapeDtypeStruct((tokens, width), bf16),
        compiler_params=pltpu.CompilerParams(vmem_limit_bytes=VMEM_BYTES),
        cost_estimate=LIGHT,
        name="adapt",
    )(single, cond, gain, w_scale, b_scale, w_shift)


def emit_rows(meta, step, count):
    place = meta[2 + step % 4] * 2 + (meta[1] ^ (step // 4))
    return pl.ds(pl.multiple_of(place * count, count), count)


def before_kernel(
    x_ref, cond_ref, cot_ref, w_gate, w_ac, b_ac, gain, w_scale, b_scale, w_shift, w_dn, w_tc, b_tc,
    gate_ref, acond_ref, tcond_ref, scale_ref, shift_ref, dh_ref,
):
    cond = cond_ref[...]
    tcond = jax.nn.sigmoid(dot(cond, w_tc[...], NN) + b_tc[...].astype(f32))
    tcond_ref[...] = tcond.astype(tcond_ref.dtype)
    d_tr = (tcond * cot_ref[...].astype(f32)).astype(bf16)
    dh_ref[...] = dot(d_tr, w_dn[...], NT).astype(dh_ref.dtype)
    acond_ref[...] = jax.nn.sigmoid(dot(cond, w_ac[...], NN) + b_ac[...].astype(f32)).astype(acond_ref.dtype)
    cond_hat, _ = norm_rows(cond.astype(f32))
    cond_low = (cond_hat * gain[...].astype(f32)).astype(bf16)
    scale = jax.nn.sigmoid(dot(cond_low, w_scale[...], NN) + b_scale[...].astype(f32))
    scale_ref[...] = scale.astype(scale_ref.dtype)
    shift_ref[...] = dot(cond_low, w_shift[...], NN).astype(shift_ref.dtype)
    gate_ref[...] = jax.nn.sigmoid(dot(x_ref[...], w_gate[...], NN)).astype(gate_ref.dtype)


def before(x_one, cond, cot, weights):
    w_gate, w_out, w_ac, b_ac, gain, w_scale, b_scale, w_shift, w_hg, w_hu, w_dn, w_tc, b_tc = weights
    used = (w_gate, w_ac, b_ac, gain, w_scale, b_scale, w_shift, w_dn, w_tc, b_tc)
    tokens, width = x_one.shape
    tile = tile_of(tokens)
    steps = tokens // tile
    outs = [(width, f32)] * 4 + [(width, bf16), (w_dn.shape[0], bf16)]
    return pl.pallas_call(
        before_kernel,
        grid=(steps,),
        in_specs=[tiled(tile, w, steps) for w in (width, cond.shape[1], width)] + [fixed(w.shape) for w in used],
        out_specs=[tiled(tile, w, steps) for w, _ in outs],
        out_shape=[jax.ShapeDtypeStruct((tokens, w), d) for w, d in outs],
        compiler_params=pltpu.CompilerParams(vmem_limit_bytes=VMEM_BYTES),
        cost_estimate=LIGHT,
        name="before",
    )(x_one, cond, cot, *used)


def middle_kernel(
    meta, x_ref, single_ref, cond_ref, cot_ref, gate_ref, acond_ref, tcond_ref, scale_ref, shift_ref, dh_ref,
    a0, a1, a2, a3, w_gate, w_out, gain, w_scale, w_shift, w_hg, w_hu, w_dn,
    out_ref, dmid_ref, dxg_ref, da0, da1, da2, da3, s_ac, s_scale, s_tc, s_gain, *rest, tiles, fast,
):
    core = meta[0] % 2
    step = pl.program_id(0)
    if fast:
        out_w, g_hidden, g_square, g_cond, g_norm, g_dn = rest
    else:
        g_hidden, g_square, g_cond, g_norm, g_dn = rest

    @pl.when(step == 0)
    def _():
        for ref in (g_hidden, g_square, g_cond, g_norm, g_dn, s_ac, s_scale, s_tc, s_gain):
            ref[...] = jnp.zeros_like(ref)

    @pl.when(step < tiles)
    def _():
        cond = cond_ref[...]
        first = core == 0

        def attended():
            return jnp.concatenate(
                [
                    jnp.where(first, a0[...], a1[...]),
                    jnp.where(first, a1[...], a0[...]),
                    jnp.where(first, a2[...], a3[...]),
                    jnp.where(first, a3[...], a2[...]),
                ],
                axis=1,
            ).astype(f32)

        gated = (attended() * gate_ref[...]).astype(bf16)
        branch = dot(gated, w_out[...], NN)
        mid = single_ref[...].astype(f32) + acond_ref[...] * branch
        normed, inverse = norm_rows(mid)
        x_two = (scale_ref[...] * normed + shift_ref[...].astype(f32)).astype(bf16)
        hgate = dot(x_two, w_hg[...], NN)
        hup = dot(x_two, w_hu[...], NN)
        sig = jax.nn.sigmoid(hgate)
        silu = hgate * sig
        hidden = (silu * hup).astype(bf16)
        d_hidden = dh_ref[...].astype(f32)
        d_hg = (d_hidden * hup * sig * (1.0 + hgate * (1.0 - sig))).astype(bf16)
        d_hu = (d_hidden * silu).astype(bf16)
        tcond = tcond_ref[...]
        dy = cot_ref[...].astype(f32)
        tr_branch = dot(hidden, w_dn[...], NN)
        out_ref[...] = (mid + tcond * tr_branch).astype(bf16)
        d_trc = dy * tr_branch * tcond * (1.0 - tcond)
        s_tc[...] += column_sum(d_trc)
        g_cond[0] += dot(cond, d_trc.astype(bf16), TN)
        g_dn[...] += dot(hidden, (tcond * dy).astype(bf16), TN)
        g_hidden[0] += dot(x_two, d_hg, TN)
        g_hidden[1] += dot(x_two, d_hu, TN)
        g_two = dot(d_hg, w_hg[...], NT) + dot(d_hu, w_hu[...], NT)
        scale = scale_ref[...]
        cond_hat, _ = norm_rows(cond.astype(f32))
        cond_low = (cond_hat * gain[...].astype(f32)).astype(bf16)
        d_scale = g_two * normed * scale * (1.0 - scale)
        s_scale[...] += column_sum(d_scale)
        d_scale = d_scale.astype(bf16)
        d_shift = g_two.astype(bf16)
        g_norm[0] += dot(cond_low, d_scale, TN)
        g_norm[1] += dot(cond_low, d_shift, TN)
        d_cond = dot(d_scale, w_scale[...], NT) + dot(d_shift, w_shift[...], NT)
        s_gain[...] += column_sum(d_cond * cond_hat)
        d_mid = dy + norm_back(normed, inverse, g_two * scale)
        dmid_ref[...] = d_mid
        acond = acond_ref[...]
        d_attn = (acond * d_mid).astype(bf16)
        d_ac = d_mid * branch * acond * (1.0 - acond)
        s_ac[...] += column_sum(d_ac)
        g_cond[1] += dot(cond, d_ac.astype(bf16), TN)
        g_square[0] += dot(gated, d_attn, TN)
        d_gated = dot(d_attn, w_out[...], NT)
        gate = gate_ref[...]
        d_att = (d_gated * gate).astype(bf16)
        d_gate = (d_gated * attended() * gate * (1.0 - gate)).astype(bf16)
        g_square[1] += dot(x_ref[...], d_gate, TN)
        dxg_ref[...] = dot(d_gate, w_gate[...], NT).astype(bf16)
        q = d_att.shape[1] // 4
        parts = [d_att[:, i * q : (i + 1) * q] for i in range(4)]
        da0[...] = jnp.where(first, parts[0], parts[1])
        da1[...] = jnp.where(first, parts[1], parts[0])
        da2[...] = jnp.where(first, parts[2], parts[3])
        da3[...] = jnp.where(first, parts[3], parts[2])

    if fast:

        @pl.when(step >= tiles)
        def _():
            emit = step - tiles
            place = meta[2 + emit % 4] * 2 + (meta[1] ^ (emit // 4))
            for g in range(4):
                at = 0
                for one, two, count in (
                    (g_hidden.at[0], None, 8),
                    (g_hidden.at[1], None, 8),
                    (g_square.at[0], g_square.at[1], 8),
                    (g_cond.at[0], g_cond.at[1], 8),
                    (g_norm.at[0], g_norm.at[1], 8),
                    (g_dn, g_dn, 16),
                ):
                    n, lanes = one.shape[0] // count, one.shape[1] // 4
                    take = lambda ref, row: ref[pl.ds(pl.multiple_of(row, n), n), g * lanes : (g + 1) * lanes]
                    if two is None:
                        part = take(one, place * n)
                    elif one is two:
                        part = jnp.concatenate([take(one, 2 * place * n), take(one, (2 * place + 1) * n)], axis=1)
                    else:
                        part = jnp.concatenate([take(one, place * n), take(two, place * n)], axis=1)
                    out_w[g, 0, at : at + n, :] = part.astype(bf16)
                    at += n


def middle(meta, x_one, single, cond, cot, gates, atts, weights, fast):
    tokens, width = single.shape
    tile = tile_of(tokens)
    tiles = tokens // tile
    cs = cond.shape[1]
    quarter = atts[0].shape[1]
    w_gate, w_out, w_ac, b_ac, gain, w_scale, b_scale, w_shift, w_hg, w_hu, w_dn, w_tc, b_tc = weights
    fold = lambda n: jax.ShapeDtypeStruct((1, n), f32)
    sums = [fold(width), fold(width), fold(width), fold(cs)]
    grads = [(2,) + w_hg.shape, (2,) + w_out.shape, (2,) + w_ac.shape, (2,) + w_scale.shape, w_dn.shape]
    row_out = [(width, bf16), (width, f32), (width, bf16)] + [(quarter, bf16)] * 4
    used = (w_gate, w_out, gain, w_scale, w_shift, w_hg, w_hu, w_dn)
    if fast:
        lanes = width // 2
        rows = sum(w.size for w in weights if w.shape[0] > 1) // (8 * 4 * lanes)
        more_specs = [pl.BlockSpec((4, 1, rows, lanes), lambda t, *_: (0, jnp.maximum(t - tiles, 0), 0, 0))]
        more = [jax.ShapeDtypeStruct((4, 8, rows, lanes), bf16)]
        scratch = [pltpu.VMEM(g, f32) for g in grads]
    else:
        more_specs = [fixed(g) for g in grads]
        more = [jax.ShapeDtypeStruct(g, f32) for g in grads]
        scratch = []
    return pl.pallas_call(
        functools.partial(middle_kernel, tiles=tiles, fast=fast),
        grid_spec=pltpu.PrefetchScalarGridSpec(
            num_scalar_prefetch=1,
            grid=(tiles + 8 * fast,),
            in_specs=[tiled(tile, w, tiles) for w in (width, width, cs, width)]
            + [tiled(tile, v.shape[1], tiles) for v in gates]
            + [tiled(tile, quarter, tiles)] * 4
            + [fixed(w.shape) for w in used],
            out_specs=[tiled(tile, w, tiles) for w, _ in row_out] + [fixed(g.shape) for g in sums] + more_specs,
            scratch_shapes=scratch,
        ),
        out_shape=[jax.ShapeDtypeStruct((tokens, w), d) for w, d in row_out] + sums + more,
        compiler_params=pltpu.CompilerParams(vmem_limit_bytes=VMEM_BYTES),
        cost_estimate=LIGHT,
        name="middle",
    )(meta, x_one, single, cond, cot, *gates, *atts, *used)


def last_kernel(
    meta, d0, d1, d2, d3, d4, single_ref, cond_ref, dmid_ref, gain, w_scale, b_scale, w_shift,
    out_ref, s_scale, s_gain, *rest, fast,
):
    if fast:
        keep_ref, send_ref, g_norm = rest
    else:
        (g_norm,) = rest

    @pl.when(pl.program_id(0) == 0)
    def _():
        for ref in (g_norm, s_scale, s_gain):
            ref[...] = jnp.zeros_like(ref)

    late_half = pl.program_id(0) >= pl.num_programs(0) // 2
    far = jnp.where(late_half, d3[...], d2[...]).astype(f32)
    g_one = d0[...].astype(f32) + d1[...].astype(f32) + far + d4[...].astype(f32)
    normed, inverse = norm_rows(single_ref[...].astype(f32))
    cond_hat, _ = norm_rows(cond_ref[...].astype(f32))
    cond_low = (cond_hat * gain[...].astype(f32)).astype(bf16)
    scale = jax.nn.sigmoid(dot(cond_low, w_scale[...], NN) + b_scale[...].astype(f32))
    d_scale = g_one * normed * scale * (1.0 - scale)
    s_scale[...] += column_sum(d_scale)
    d_scale = d_scale.astype(bf16)
    d_shift = g_one.astype(bf16)
    g_norm[0] += dot(cond_low, d_scale, TN)
    g_norm[1] += dot(cond_low, d_shift, TN)
    d_cond = dot(d_scale, w_scale[...], NT) + dot(d_shift, w_shift[...], NT)
    s_gain[...] += column_sum(d_cond * cond_hat)
    out_ref[...] = dmid_ref[...] + norm_back(normed, inverse, g_one * scale)

    if fast:

        @pl.when(pl.program_id(0) == pl.num_programs(0) - 1)
        def _():
            n, wide = g_norm.shape[1] // 8, g_norm.shape[2] // 2
            for e, ref in enumerate((keep_ref, send_ref)):
                for p in range(2):
                    lanes = pl.ds(pl.multiple_of(((meta[0] // 2) ^ p) * wide, wide), wide)
                    for i in range(8):
                        ref[p, i] = g_norm[(meta[0] % 2) ^ e, emit_rows(meta, i, n), lanes].astype(bf16)


def last(meta, ds, single, cond, dmid, gain, w_scale, b_scale, w_shift, fast):
    tokens, width = single.shape
    tile = tile_of(tokens)
    steps = tokens // tile
    cs = cond.shape[1]
    grads = (2,) + w_scale.shape
    if fast:
        more = [jax.ShapeDtypeStruct((2, 8, cs // 8, width // 2), bf16)] * 2
        scratch = [pltpu.VMEM(grads, f32)]
    else:
        more = [jax.ShapeDtypeStruct(grads, f32)]
        scratch = []
    more = [jax.ShapeDtypeStruct((1, width), f32), jax.ShapeDtypeStruct((1, cs), f32)] + more
    row = tiled(tile, width, steps)
    half = steps // 2
    early_row = pl.BlockSpec((tile, width), lambda t, *_: (jnp.minimum(t, half - 1), 0))
    late_row = pl.BlockSpec((tile, width), lambda t, *_: (jnp.maximum(t - half, 0), 0))
    return pl.pallas_call(
        functools.partial(last_kernel, fast=fast),
        grid_spec=pltpu.PrefetchScalarGridSpec(
            num_scalar_prefetch=1,
            grid=(steps,),
            in_specs=[row, row, early_row, late_row, row, row]
            + [tiled(tile, cs, steps), row]
            + [fixed(w.shape) for w in (gain, w_scale, b_scale, w_shift)],
            out_specs=[row] + [fixed(g.shape) for g in more],
            scratch_shapes=scratch,
        ),
        out_shape=[jax.ShapeDtypeStruct((tokens, width), f32)] + more,
        compiler_params=pltpu.CompilerParams(vmem_limit_bytes=VMEM_BYTES),
        cost_estimate=LIGHT,
        name="last",
    )(meta, *ds, single, cond, dmid, gain, w_scale, b_scale, w_shift)


def swap(value, bit):
    return lax.ppermute(value, "head", [(i, i ^ bit) for i in range(lax.axis_size("head"))])


def across(value):
    return lax.ppermute(value, "samp", [(i, i ^ 1) for i in range(8)])


def slot(value, bit):
    return lax.ppermute(value, "samp", [(i, i ^ (2 * bit)) for i in range(8)])


def add(*terms):
    total = terms[0].astype(f32)
    for term in terms[1:]:
        total = total + term.astype(f32)
    return total


def tie(value, *others):
    return lax.optimization_barrier((value,) + others)[0]


def low(*terms):
    return add(*terms).astype(bf16)


Z_ORDER = (0, 2, 1, 3)


def x_step(block):
    return block[:4], across(block[4:])


def z_first(keep, got):
    return slot(low(keep[2:], got[2:]), 1)


def z_second(keep, got, z_got):
    return slot(low(keep[1], got[1], z_got[1]), 2)


def z_total(keep, got, z_got, last_got):
    return add(keep[0], got[0], z_got[0], last_got)


def fence(*values):
    return lax.optimization_barrier(values)


def total_step(vector, step):
    if step < 2:
        return vector + swap(vector, 1 << step)
    if step == 2:
        return vector + across(vector)
    return vector + slot(vector, step - 2)


def pack_w(w_heads, wide):
    return (
        jnp.concatenate([w[:wide] for w in w_heads], axis=0),
        jnp.concatenate([w[wide:] for w in w_heads], axis=0),
    )


def on_device(
    single,
    cond,
    pair,
    complex_length,
    sample_complex,
    cotangent,
    gain_one,
    w_scale_one,
    b_scale_one,
    w_shift_one,
    w_query,
    b_query,
    w_key,
    w_value,
    w_gate,
    w_out,
    w_pair,
    w_attn_cond,
    b_attn_cond,
    gain_two,
    w_scale_two,
    b_scale_two,
    w_shift_two,
    w_hidden_gate,
    w_hidden_up,
    w_hidden_down,
    w_tr_cond,
    b_tr_cond,
):
    groups = lax.axis_size("head")
    devices = lax.axis_size("samp")
    me = lax.axis_index("head")
    place = lax.axis_index("samp")
    core = me % 2
    part = me // 2
    samples, rows, width = single.shape
    cs = cond.shape[2]
    tokens = samples * rows
    length = rows * groups
    heads = w_pair.shape[1]
    few = heads // groups
    dim = width // heads
    wide = few * dim
    complexes, _, columns, _ = pair.shape
    chunks = 2 * groups
    chunk = length // chunks
    halves = range(groups // 2)
    fast = devices == 8 and groups == 4 and columns == chunk
    line = lambda v: v.reshape(1, -1)
    flat = lambda v: v.reshape(tokens, width)
    first = core == 0

    if fast:
        z, x = place // 2, place % 2
        order = z ^ jnp.array(Z_ORDER, jnp.int32)
        slots = jnp.stack([order * 2 + x, order * 2 + 1 - x], axis=1).reshape(8)
    else:
        x = jnp.zeros((), jnp.int32)
        order, slots = jnp.zeros((4,), jnp.int32), jnp.arange(chunks, dtype=jnp.int32)
    meta = jnp.concatenate([jnp.stack([me, x]).astype(jnp.int32), order, sample_complex, slots])
    pair_meta = jnp.stack([me, place]).astype(jnp.int32)
    group = 8
    sizes = dict(few=few, blocks=groups, group=group)
    single_t, cond_t, cot_t = flat(single), cond.reshape(tokens, cs), flat(cotangent)
    weights_one = (line(gain_one), w_scale_one, line(b_scale_one), w_shift_one)
    weights_two = (
        w_gate, w_out, w_attn_cond, line(b_attn_cond), line(gain_two), w_scale_two, line(b_scale_two), w_shift_two,
        w_hidden_gate, w_hidden_up, w_hidden_down, w_tr_cond, line(b_tr_cond),
    )

    def own_heads(*weights):
        columns_of = lambda w, k: lax.dynamic_slice_in_dim(w, (2 * k + core) * wide, wide, w.ndim - 1)
        w_heads = [jnp.concatenate([columns_of(w, k).T for w in weights[:3]], axis=0) for k in halves]
        b_heads = [columns_of(weights[3].astype(f32), k)[:, None] for k in halves]
        return w_heads, b_heads, *pack_w(w_heads, wide)

    parts = [(k, 0, wide) for k in halves]
    by_sample = lambda v: v.reshape(samples, rows, -1)
    by_token = lambda v: v.reshape(-1, v.shape[-1])
    attend_one = lambda k, blocks, biases: attend(meta, blocks, w_heads[k], b_heads[k], biases, nh=few, hd=dim)
    middle_one = lambda x_one, gates, atts: middle(meta, x_one, single_t, cond_t, cot_t, gates, atts, weights_two, fast)
    back_one = lambda kept, own, near: attend_back(
        meta, *kept[2:], *kept[:2], own, near, chunks, complexes, base=0, nh=few, hd=dim, fast=fast
    )

    def q_sums(gb):
        zero = jnp.zeros((wide,), f32)
        out = []
        for k in halves:
            mine = gb[k * wide : (k + 1) * wide].reshape(-1)
            out += [jnp.where(first, mine, zero), jnp.where(first, zero, mine)]
        return out

    w_blocked = blocked(w_pair, group)
    pair_low, pair_inverse, pair_raw, *bias = pair_bias(pair_meta, complex_length, pair, w_blocked, **sizes)
    near_bias = [swap(v, 1) for v in bias[groups // 2 :]]
    owns = [jnp.concatenate([bias[k], near_bias[k]], axis=-1) for k in halves]

    if fast:
        both_owns = jnp.stack(owns)
        owns, both_owns, single_t = fence(owns, both_owns, single_t)
        far_0, z_0, x_own = slot(owns[0], 2), [slot(owns[0], 1)], across(both_owns)
        x_one = adapt(single_t, cond_t, *weights_one)
        far_0, z_0, x_own, x_one, owns = fence(far_0, z_0, x_own, x_one, owns)
        x_far = swap(x_one, 2)
        far_1 = slot(owns[1], 2)
        z_0.append(slot(far_0, 1))
        x_0 = [across(far_0), across(z_0[0])]
        far_1, z_0, x_0, owns, x_mid, qkv = fence(far_1, z_0, x_0, owns, x_one, (w_query, w_key, w_value, b_query))
        w_heads, b_heads, w_q, w_kv = own_heads(*qkv)
        x_0.append(across(z_0[1]))
        x_1 = [across(far_1)]
        z_1 = [slot(owns[1], 1), slot(far_1, 1)]
        gates = before(x_mid, cond_t, cot_t, weights_two)
        x_far, x_0, x_1, z_1, gates, x_mid, w_heads, b_heads, w_q, w_kv = fence(
            x_far, x_0, x_1, z_1, gates, x_mid, w_heads, b_heads, w_q, w_kv
        )
        x_cross, x_near = swap(x_far, 1), swap(x_mid, 1)
        x_1 += [across(v) for v in z_1]
        blocks = [by_sample(v) for v in (x_one, x_near, x_far, x_cross)]
        pairs_of = lambda k, here, there: [
            pair_of for v, w in zip(here, [(x_own, k)] + [(u, None) for u in there]) for pair_of in ((v, None), w)
        ]
        kept = [attend_one(0, blocks, pairs_of(0, [owns[0], far_0] + z_0, x_0))]
        kept, x_1 = fence(kept, x_1)
        near_atts = [swap(kept[0][1], 1)]
        kept.append(attend_one(1, blocks, pairs_of(1, [owns[1], far_1] + z_1, x_1)))
        kept, near_atts = fence(kept, near_atts)
        near_atts.append(swap(kept[1][1], 1))
        atts = [by_token(v) for k in halves for v in (kept[k][0], near_atts[k])]

        block_out, d_mid, d_xg, da0, da1, da2, da3, s_ac, s_scale2, s_tc, s_gain2, w_mid = middle_one(x_one, gates, atts)
        near_att = [swap(by_sample(v), 1) for v in (da1, da3)]
        near_att, w_mid = fence(near_att, w_mid)
        mid = lax.psum_scatter(w_mid, "head", scatter_dimension=0, tiled=True)[0]

        dq_0, dkv_0, *db_0 = back_one(kept[0], by_sample(da0), near_att[0])
        db_0, kept_1 = fence(db_0, kept[1])
        keep_a, got_a, keep_b, got_b = db_0[0], across(db_0[1]), db_0[2], across(db_0[3])
        dq_1, dkv_1, *db_1 = back_one(kept_1, by_sample(da2), near_att[1])
        dq_1, db_1, got_a = fence(dq_1, db_1, got_a)
        keep_c, got_c, keep_d = db_1[0], across(db_1[1]), db_1[2]
        zs_a = z_first(keep_a, got_a)
        d_near, d_cross, d_far, d_own, gb, keep_w, send_w = heads_back(
            meta, blocks, w_q, w_kv, [(dq_0, dkv_0), (dq_1, dkv_1)], parts, wch=wide, fast=fast
        )
        d_near, d_cross, d_far, gb, send_w, got_b, got_c, zs_a, send_d = fence(
            d_near, d_cross, d_far, gb, send_w, got_b, got_c, zs_a, db_1[3]
        )
        d_cross, near_x, got_d = swap(d_cross, 1), swap(d_near, 1), across(send_d)
        zs_b, zs_c = z_first(keep_b, got_b), z_first(keep_c, got_c)
        d_cross, d_far, near_x = fence(d_cross, d_far, near_x)
        cut = samples // 2
        far_x = [swap(low(d_far[:cut], d_cross[:cut]), 2)]
        last_a = z_second(keep_a, got_a, zs_a)
        far_x[0], zs_b, zs_c, got_d, last_a, d_far, d_cross = fence(far_x[0], zs_b, zs_c, got_d, last_a, d_far, d_cross)
        far_x.append(swap(low(d_far[cut:], d_cross[cut:]), 2))
        zs_d = z_first(keep_d, got_d)
        last_b, last_c = z_second(keep_b, got_b, zs_b), z_second(keep_c, got_c, zs_c)
        keep_m, got_m = x_step(mid)
        far_x[1], zs_d, last_b, last_c, send_w = fence(far_x[1], zs_d, last_b, last_c, send_w)
        last_d = z_second(keep_d, got_d, zs_d)
        sums = [
            low(z_total(keep_a, got_a, zs_a, last_a)),
            low(z_total(keep_b, got_b, zs_b, last_b)),
            low(z_total(keep_c, got_c, zs_c, last_c)),
        ]
        far_rows = [swap(jnp.stack([v[..., rows:] for v in sums]), 1)]
        far_w = swap(send_w, 2)
        grad_single, s_scale1, s_gain1, keep_l, send_l = last(
            meta, (flat(d_own), flat(near_x), *(by_token(v) for v in far_x), d_xg),
            single_t, cond_t, d_mid, *weights_one, fast,
        )
        far_rows, far_w, keep_l, send_l, last_d, got_m, s_gain1, s_scale1 = fence(
            far_rows, far_w, keep_l, send_l, last_d, got_m, s_gain1, s_scale1
        )
        sums.append(low(z_total(keep_d, got_d, zs_d, last_d)))
        far_rows.append(swap(sums[3][..., rows:], 1))
        near_l = swap(send_l, 1)
        z_m = z_first(keep_m, got_m)
        keep_h, got_h = x_step(low(keep_w, far_w))
        others = jnp.concatenate(
            [v.reshape(-1) for v in (s_gain1, s_scale1, *q_sums(gb), s_gain2, s_ac, s_scale2, s_tc)]
        )
        far_rows, near_l, others = fence(far_rows, near_l, others)
        far_l = swap(low(keep_l[1], near_l[1]), 2)
        pair_grads = [jnp.stack([v[..., :rows] for v in sums[2 * k : 2 * k + 2]]) for k in halves]
        pair_grads += [far_rows[0][:2], jnp.stack([far_rows[0][2], far_rows[1]])]
        grad_pair, grad_pair_weight = pair_back(pair_meta, pair_low, pair_inverse, pair_raw, w_pair, pair_grads, **sizes)
        far_l, got_h, z_m, grad_pair_weight = fence(far_l, got_h, z_m, grad_pair_weight)
        keep_l, got_l = x_step(low(keep_l[0], near_l[0], far_l))
        late = total_step(jnp.concatenate([grad_pair_weight.reshape(-1), others]), 0)
        z_h = z_first(keep_h, got_h)
        e_m = z_second(keep_m, got_m, z_m)
        got_l, late, z_h, e_m = fence(got_l, late, z_h, e_m)

        def settle(block):
            size = block.shape[1] // 2
            left, right = block[:, :size], block[:, size:]
            got = swap(jnp.where(first, right, left), 1)
            held = jnp.where(first, left, right)
            return jnp.where(first, held, got), jnp.where(first, got, held)

        late = total_step(late, 1)
        e_h = z_second(keep_h, got_h, z_h)
        z_l = z_first(keep_l, got_l)
        z_l, late, e_h = fence(z_l, late, e_h)
        e_l = z_second(keep_l, got_l, z_l)
        late = total_step(late, 2)
        e_l, late = fence(e_l, late)
        r_scale1, r_shift1 = settle(z_total(keep_l, got_l, z_l, e_l))
        late = total_step(late, 3)
        r_heads = z_total(keep_h, got_h, z_h, e_h)
        n, m, half = width // 8, cs // 8, width // 4
        r_mid = z_total(keep_m, got_m, z_m, e_m)
        r_hg, r_hu = r_mid[:n], r_mid[n : 2 * n]
        r_out, r_gate = r_mid[2 * n : 3 * n, :half], r_mid[2 * n : 3 * n, half:]
        r_tc, r_ac = r_mid[3 * n : 3 * n + m, :half], r_mid[3 * n : 3 * n + m, half:]
        r_scale2, r_shift2 = r_mid[3 * n + m : 3 * n + 2 * m, :half], r_mid[3 * n + m : 3 * n + 2 * m, half:]
        r_down = jnp.concatenate([r_mid[3 * n + 2 * m :, :half], r_mid[3 * n + 2 * m :, half:]], axis=0)
        r_scale1, r_shift1, late = fence(r_scale1, r_shift1, late)
        late = total_step(late, 4)
    else:
        w_heads, b_heads, w_q, w_kv = own_heads(w_query, w_key, w_value, b_query)
        biases = []
        for own in owns:
            gathered = lax.all_gather(own, "samp", axis=0)
            moved = gathered.transpose(1, 2, 0, 3, 4).reshape(complexes, few, chunks, chunk, 2 * rows)
            biases.append([(moved[:, :, i], None) for i in range(chunks)])
        x_one = adapt(single_t, cond_t, *weights_one)
        x_far = swap(x_one, 2)
        blocks = [by_sample(v) for v in (x_one, swap(x_one, 1), x_far, swap(x_far, 1))]
        kept = [attend_one(k, blocks, biases[k]) for k in halves]
        atts = [by_token(v) for k in halves for v in (kept[k][0], swap(kept[k][1], 1))]
        block_out, d_mid, d_xg, da0, da1, da2, da3, s_ac, s_scale2, s_tc, s_gain2, *w_mid = middle_one(x_one, before(x_one, cond_t, cot_t, weights_two), atts)
        head_grads, sums = [], []
        for k, (own, sent) in enumerate(((da0, da1), (da2, da3))):
            dq, dkv, db = back_one(kept[k], by_sample(own), swap(by_sample(sent), 1))
            head_grads.append((dq, dkv))
            moved = db.transpose(1, 2, 0, 3, 4).reshape(complexes, few, devices, columns, 2 * rows)
            sums.append(lax.psum_scatter(moved, "samp", scatter_dimension=2, tiled=False))
        d_near, d_cross, d_far, d_own, gb, gq, gkv = heads_back(
            meta, blocks, w_q, w_kv, head_grads, parts, wch=wide, fast=fast
        )
        far_x = swap(low(d_far, swap(d_cross, 1)), 2)
        grad_single, s_scale1, s_gain1, w_last = last(
            meta, (flat(d_own), flat(swap(d_near, 1)), *jnp.split(flat(far_x), 2), d_xg), single_t, cond_t, d_mid,
            *weights_one, fast,
        )
        pair_grads = [v[..., :rows] for v in sums] + [swap(v[..., rows:], 1) for v in sums]
        grad_pair, grad_pair_weight = pair_back(pair_meta, pair_low, pair_inverse, pair_raw, w_pair, pair_grads, **sizes)

        def total_of(stack):
            axis = stack.ndim - 1
            half = lax.psum_scatter(stack.astype(bf16), "head", scatter_dimension=axis, tiled=True).astype(f32)
            return lax.psum_scatter(half, "samp", scatter_dimension=axis - 1, tiled=True)

        grads = [
            jnp.concatenate([gq[k * wide : (k + 1) * wide], gkv[2 * k * wide : 2 * (k + 1) * wide]], axis=0) for k in halves
        ]
        held = jnp.where(part == 0, grads[0], grads[1])
        sent = jnp.where(part == 0, grads[1], grads[0])
        r_heads = add(held, swap(sent.astype(bf16), 2))
        r_heads = lax.psum_scatter(r_heads.T, "samp", scatter_dimension=0, tiled=True)
        (r_hg, r_hu), (r_out, r_gate), (r_tc, r_ac), (r_scale2, r_shift2), r_down = [total_of(v) for v in w_mid]
        r_scale1, r_shift1 = total_of(w_last)
        late = jnp.concatenate(
            [v.reshape(-1) for v in (grad_pair_weight, s_gain1, s_scale1, *q_sums(gb), s_gain2, s_ac, s_scale2, s_tc)]
        )
        late = lax.psum(late, ("samp", "head"))

    cuts = [heads * w_pair.shape[0]]
    for size in (cs, width, width, cs, width, width):
        cuts.append(cuts[-1] + size)
    sum_pair, sum_gain1, sum_scale1, sum_query, sum_gain2, sum_ac, sum_scale2, sum_tc = jnp.split(late, cuts)
    whole = (samples, rows, width)
    return (
        block_out.reshape(whole),
        grad_single.reshape(whole),
        grad_pair,
        sum_gain1,
        r_scale1,
        sum_scale1,
        r_shift1,
        r_heads[:, :wide],
        sum_query,
        r_heads[:, wide : 2 * wide],
        r_heads[:, 2 * wide :],
        r_gate,
        r_out,
        sum_pair.reshape(heads, -1).T,
        r_ac,
        sum_ac,
        sum_gain2,
        r_scale2,
        sum_scale2,
        r_shift2,
        r_hg,
        r_hu,
        r_down,
        r_tc,
        sum_tc,
    )


def solution(mesh):
    placed = (
        P("samp", "head", None),
        P("samp", "head", None),
        P(None, "head", "samp", None),
        P(),
        P("samp"),
        P("samp", "head", None),
        P(),
        P(),
        P(),
        P(),
        P(),
        P(),
        P(),
        P(),
        P(),
        P(),
        P(),
        P(),
        P(),
        P(),
        P(),
        P(),
        P(),
        P(),
        P(),
        P(),
        P(),
        P(),
    )
    return jax.shard_map(
        on_device,
        mesh=mesh,
        in_specs=placed,
        out_specs=(
            P("samp", "head", None),
            P("samp", "head", None),
            P(None, "head", "samp", None),
            P(),
            P("samp", "head"),
            P(),
            P("samp", "head"),
            P("samp", "head"),
            P(),
            P("samp", "head"),
            P("samp", "head"),
            P("samp", "head"),
            P("samp", "head"),
            P(),
            P("samp", "head"),
            P(),
            P(),
            P("samp", "head"),
            P(),
            P("samp", "head"),
            P("samp", "head"),
            P("samp", "head"),
            P("samp", "head"),
            P("samp", "head"),
            P(),
        ),
        check_vma=False,
    )
```

```python
import functools
import math

import jax
import jax.numpy as jnp
from jax import lax
from jax.experimental import pallas as pl
from jax.experimental.pallas import tpu as pltpu
from jax.sharding import PartitionSpec as P

f32, bf16 = jnp.float32, jnp.bfloat16
epsilon = 1e-05
fill_value = -1e30
LOG2E = math.log2(math.e)
VMEM_BYTES = 60 << 20
PAIR_LINES = (8, 16, 24, 32, 64)
NN, NT, TN = ((1,), (0,)), ((1,), (1,)), ((0,), (0,))


LIGHT = pl.CostEstimate(flops=1 << 20, bytes_accessed=1 << 20, transcendentals=0)


def dot(a, b, dims):
    return lax.dot_general(a, b, (dims, ((), ())), preferred_element_type=f32)


def norm_rows(inputs):
    mean_val = jnp.mean(inputs, axis=-1, keepdims=True)
    centered = inputs - mean_val
    variance = jnp.mean(centered * centered, axis=-1, keepdims=True)
    inverse = lax.rsqrt(variance + epsilon)
    return (centered * inverse, inverse)


def norm_back(normed, inverse, upstream):
    mean_grad = jnp.mean(upstream, axis=-1, keepdims=True)
    mean_dot = jnp.mean(upstream * normed, axis=-1, keepdims=True)
    return inverse * (upstream - mean_grad - normed * mean_dot)


def tile_of(tokens, sizes=(8, 16, 32, 64, 128, 256)):
    return max(t for t in sizes if tokens % t == 0)


def fixed(shape):
    return pl.BlockSpec(shape, lambda *_: (0,) * len(shape), pipeline_mode=pl.Buffered(1))


META = 6


def attend_kernel(meta, x0, x1, x2, x3, w_ref, bq_ref, *rest, which, nh, hd, rows, jc, nchunk, qscale):
    bias_hbm = rest[:nchunk]
    o_ref, far_ref, p_ref, q_ref, k_ref, v_ref, l_ref, xs, ks, ss, bias_ref, sems = rest[nchunk:]
    b = pl.program_id(0)
    g = meta[0]
    cplx = meta[META + b]
    per_block = nchunk // 4

    def copies():
        return [
            pltpu.make_async_copy(
                bias_hbm[i] if which[i] is None else bias_hbm[i].at[which[i]],
                bias_ref.at[meta[META + pl.num_programs(0) + i]],
                sems.at[i],
            )
            for i in range(nchunk)
        ]

    @pl.when(b == 0)
    def _():
        for copy in copies():
            copy.start()

    for r, x in enumerate((x0, x1, x2, x3)):
        xs[r * rows : (r + 1) * rows, :] = x[0]
    wch = nh * hd
    q = dot(w_ref[0:wch, :], xs[0 : 2 * rows, :], NT) + bq_ref[...]
    q_ref[0] = (q * qscale).astype(bf16)
    kv = dot(w_ref[wch : 3 * wch, :], xs[...], NT).astype(bf16)
    k_ref[0] = kv[0:wch]
    v_ref[0] = kv[wch:]

    @pl.when(b == 0)
    def _():
        for copy in copies():
            copy.wait()

    ones = jnp.ones((16, kv.shape[1]), bf16)
    outs = []
    sums = []
    before = None
    for h in range(nh + 1):
        if h < nh:
            ks[h % 2, :, :] = jnp.transpose(k_ref[0, h * hd : (h + 1) * hd, :])
            qT = q_ref[0, h * hd : (h + 1) * hd, :]
        m = None
        for t in range(nchunk):
            part = slice(t * jc, (t + 1) * jc)
            if h < nh:
                s_idx = ((t // per_block) ^ g) * per_block + t % per_block
                s = dot(ks[h % 2, part, :], qT, NN) + bias_ref[s_idx, cplx, h].astype(f32)
                ss[h % 2, part, :] = s
                mt = jnp.max(s.reshape(jc // 8, 8, s.shape[1]), axis=0)
                m = mt if m is None else jnp.maximum(m, mt)
            if h > 0:
                p_ref[0, h - 1, part, :] = jnp.exp2(ss[(h - 1) % 2, part, :] - before).astype(bf16)
        if h < nh:
            m = jnp.max(m, axis=0, keepdims=True)
        if h > 0:
            va = jnp.concatenate([v_ref[0, (h - 1) * hd : h * hd, :], ones], axis=0)
            oT = dot(va, p_ref[0, h - 1], NN)
            l = oT[hd : hd + 1, :]
            outs.append(oT[:hd] / l)
            sums.append(l)
        before = m
    l_ref[0] = jnp.concatenate(sums, axis=0)
    o = jnp.transpose(jnp.concatenate(outs, axis=0)).astype(bf16)
    o_ref[0] = o[:rows]
    far_ref[0] = o[rows:]


def attend(meta, xb, wT, bq, biases, *, nh, hd):
    B, rows, C = xb[0].shape
    nchunk = len(biases)
    biases, which = zip(*biases)
    ncx, _, jc, qi = biases[0].shape[-4:]
    L = nchunk * jc
    wch = nh * hd
    kern = functools.partial(
        attend_kernel, which=which, nh=nh, hd=hd, rows=rows, jc=jc, nchunk=nchunk, qscale=LOG2E / math.sqrt(hd)
    )
    xspec = pl.BlockSpec((1, rows, C), lambda b, m: (b, 0, 0))
    per = lambda shape: pl.BlockSpec((1,) + shape, lambda b, m: (b,) + (0,) * len(shape))
    return pl.pallas_call(
        kern,
        grid_spec=pltpu.PrefetchScalarGridSpec(
            num_scalar_prefetch=1,
            grid=(B,),
            in_specs=[xspec] * 4
            + [fixed(wT.shape), fixed(bq.shape)]
            + [pl.BlockSpec(memory_space=pl.ANY)] * nchunk,
            out_specs=[
                per((rows, wch)),
                per((rows, wch)),
                per((nh, L, qi)),
                per((wch, qi)),
                per((wch, L)),
                per((wch, L)),
                per((nh, qi)),
            ],
            scratch_shapes=[
                pltpu.VMEM((L, C), bf16),
                pltpu.VMEM((2, L, hd), bf16),
                pltpu.VMEM((2, L, qi), f32),
                pltpu.VMEM((nchunk, ncx, nh, jc, qi), bf16),
                pltpu.SemaphoreType.DMA((nchunk,)),
            ],
        ),
        out_shape=[
            jax.ShapeDtypeStruct((B, rows, wch), bf16),
            jax.ShapeDtypeStruct((B, rows, wch), bf16),
            jax.ShapeDtypeStruct((B, nh, L, qi), bf16),
            jax.ShapeDtypeStruct((B, wch, qi), bf16),
            jax.ShapeDtypeStruct((B, wch, L), bf16),
            jax.ShapeDtypeStruct((B, wch, L), bf16),
            jax.ShapeDtypeStruct((B, nh, qi), f32),
        ],
        compiler_params=pltpu.CompilerParams(vmem_limit_bytes=VMEM_BYTES),
        cost_estimate=LIGHT,
        name="attend",
    )(meta, *xb, wT, bq, *biases)


def attend_back_kernel(
    meta, p_ref, q_ref, k_ref, v_ref, l_ref, o0, o1, do0, do1, *rest, base, nh, hd, jc, nchunk, scale, fast
):
    dq_ref, dkv_ref = rest[:2]
    vs, ds, acc = rest[-3:]
    b = pl.program_id(0)
    g = meta[0]
    cplx = meta[META + b]
    per_block = nchunk // 4
    wch = nh * hd
    L = nchunk * jc

    @pl.when(b == 0)
    def _():
        acc[...] = jnp.zeros_like(acc)

    dO = jnp.transpose(jnp.concatenate([do0[0], do1[0]], axis=0).astype(f32))
    O = jnp.transpose(jnp.concatenate([o0[0], o1[0]], axis=0).astype(f32))
    prod = dO * O
    qi = dO.shape[1]
    row = lax.broadcasted_iota(jnp.int32, (16, qi), 0)
    ones = jnp.ones((16, L), bf16)
    for h in range(nh + 1):
        if h < nh:
            hs = slice(h * hd, (h + 1) * hd)
            his = slice((base + h) * hd, (base + h + 1) * hd)
            linv = 1.0 / l_ref[0, base + h : base + h + 1, :]
            dOh = (dO[his] * linv).astype(bf16)
            delta = jnp.sum(prod[his], axis=0, keepdims=True) * linv
            hi = delta.astype(bf16).astype(f32)
            extra = jnp.where(row == 0, -hi, jnp.where(row == 1, hi - delta, 0.0)).astype(bf16)
            dOa = jnp.concatenate([dOh, extra], axis=0)
            vs[h % 2] = jnp.transpose(jnp.concatenate([v_ref[0, hs, :], ones], axis=0))
        if h > 0:
            ps = slice((h - 1) * hd, h * hd)
            dk_parts, dv_parts = [], []
            kk, qq = k_ref[0, ps, :], q_ref[0, ps, :]
        for t in range(nchunk):
            r, u = t // per_block, t % per_block
            s_idx = (r ^ g) * per_block + u
            ts = slice(t * jc, (t + 1) * jc)
            if h < nh:
                d = dot(vs[h % 2, ts, :], dOa, NN) * p_ref[0, h, ts, :].astype(f32)
                acc[s_idx, cplx, h] += d
                ds[h % 2, ts, :] = d.astype(bf16)
            if h > 0:
                dk_parts.append(dot(ds[(h - 1) % 2, ts, :], qq, NT))
                dv_parts.append(dot(p_ref[0, h - 1, ts, :], dO_before, NT))
        if h > 0:
            dq_ref[0, ps, :] = (dot(kk, ds[(h - 1) % 2], NN) * scale).astype(bf16)
            dk = jnp.transpose(jnp.concatenate(dk_parts, axis=0)) * (1.0 / LOG2E)
            dkv_ref[0, ps, :] = dk.astype(bf16)
            dv = jnp.transpose(jnp.concatenate(dv_parts, axis=0))
            dkv_ref[0, wch + (h - 1) * hd : wch + h * hd, :] = dv.astype(bf16)
        if h < nh:
            dO_before = dOh

    @pl.when(b == pl.num_programs(0) - 1)
    def _():
        if fast:
            for i in range(4):
                for e in range(2):
                    block = acc[meta[2 + i] * 2 + (meta[1] ^ e)].astype(bf16)
                    for c in range(block.shape[0]):
                        rest[2 + 2 * c + e][i] = block[c]
        else:
            rest[2][...] = acc[...].astype(bf16)


def attend_back(meta, p, q, k, v, l, o0, o1, do0, do1, nchunk, ncx, *, base, nh, hd, fast):
    B, held, L, qi = p.shape
    rows = o0.shape[1]
    jc = L // nchunk
    wch = nh * hd
    kern = functools.partial(
        attend_back_kernel, base=base, nh=nh, hd=hd, jc=jc, nchunk=nchunk, scale=1.0 / math.sqrt(hd), fast=fast
    )
    per = lambda shape: pl.BlockSpec((1,) + shape, lambda b, m: (b,) + (0,) * len(shape))
    some = lambda shape: pl.BlockSpec((1,) + shape, lambda b, m: (b, base // nh) + (0,) * (len(shape) - 1))
    db = (nchunk, ncx, nh, jc, qi)
    outs = [((4,) + db[2:], bf16)] * (2 * ncx) if fast else [(db, bf16)]
    return pl.pallas_call(
        kern,
        grid_spec=pltpu.PrefetchScalarGridSpec(
            num_scalar_prefetch=1,
            grid=(B,),
            in_specs=[some((nh, L, qi)), some((wch, qi)), some((wch, L)), some((wch, L)), per((held, qi))]
            + [per((rows, held * hd))] * 4,
            out_specs=[per((wch, qi)), per((2 * wch, L))] + [fixed(s) for s, _ in outs],
            scratch_shapes=[
                pltpu.VMEM((2, L, hd + 16), bf16),
                pltpu.VMEM((2, L, qi), bf16),
                pltpu.VMEM(db, f32),
            ],
        ),
        out_shape=[jax.ShapeDtypeStruct((B, wch, qi), bf16), jax.ShapeDtypeStruct((B, 2 * wch, L), bf16)]
        + [jax.ShapeDtypeStruct(s, d) for s, d in outs],
        compiler_params=pltpu.CompilerParams(vmem_limit_bytes=VMEM_BYTES),
        cost_estimate=LIGHT,
        name="attend_back",
    )(meta, p, q, k, v, l, o0, o1, do0, do1)


def heads_back_kernel(meta, x0, x1, x2, x3, wq_ref, wkv_ref, *rest, parts, rows, wch, fast, chained):
    n = len(parts)
    dqs, dkvs, rest = rest[:n], rest[n : 2 * n], rest[2 * n :]
    if chained:
        start_b, start_q, start_kv = rest[:3]
        rest = rest[3:]
    near_ref, cross_ref, far_ref, own_ref, gb_ref = rest[:5]
    if fast:
        keep_ref, send_ref, xs, dq, dkv, gq, gkv, gt = rest[5:]
    else:
        gq, gkv, xs, dq, dkv = rest[5:]
    b = pl.program_id(0)

    @pl.when(b == 0)
    def _():
        gq[...] = start_q[...] if chained else jnp.zeros_like(gq)
        gkv[...] = start_kv[...] if chained else jnp.zeros_like(gkv)
        gb_ref[...] = start_b[...] if chained else jnp.zeros_like(gb_ref)

    for r, x in enumerate((x0, x1, x2, x3)):
        xs[r * rows : (r + 1) * rows, :] = x[0]
    for (chunk, at, size), q, kv in zip(parts, dqs, dkvs):
        start = chunk * wch + at
        dq[start : start + size, :] = q[0]
        start = 2 * chunk * wch + at
        dkv[start : start + size, :] = kv[0, :size]
        dkv[start + wch : start + wch + size, :] = kv[0, size:]
    q, kv = dq[...], dkv[...]
    gb_ref[...] += jnp.sum(q.astype(f32), axis=1, keepdims=True)
    gq[...] += dot(q, xs[0 : 2 * rows, :], NN)
    gkv[...] += dot(kv, xs[...], NN)
    kv = jnp.transpose(kv)
    q = jnp.transpose(q)
    dx = dot(kv[2 * rows :], wkv_ref[...], NN).astype(bf16)
    far_ref[0] = dx[:rows]
    cross_ref[0] = dx[rows:]
    dx = (dot(kv[: 2 * rows], wkv_ref[...], NN) + dot(q, wq_ref[...], NN)).astype(bf16)
    own_ref[0] = dx[:rows]
    near_ref[0] = dx[rows:]

    if fast:

        @pl.when(b == pl.num_programs(0) - 1)
        def _():
            for e, ref in enumerate((keep_ref, send_ref)):
                chunk = (meta[0] // 2) ^ e
                half = pl.ds(pl.multiple_of(chunk * wch, wch), wch)
                gt[:, 0:wch] = jnp.transpose(gq[half, :])
                both = pl.ds(pl.multiple_of(chunk * 2 * wch, wch), 2 * wch)
                gt[:, wch:] = jnp.transpose(gkv[both, :])
                count = gt.shape[0] // 8
                for i in range(8):
                    ref[i] = gt[emit_rows(meta, i, count), :].astype(bf16)


def heads_back(meta, xb, wq, wkv, grads, parts, *, wch, fast, span=None, start=()):
    rows, C = xb[0].shape[1:]
    off, B = span or (0, xb[0].shape[0])
    L = 4 * rows
    total = wq.shape[0]
    row = pl.BlockSpec((1, rows, C), lambda b, m: (b, 0, 0))
    row_in = pl.BlockSpec((1, rows, C), lambda b, m: (b + off, 0, 0))
    per = lambda shape: pl.BlockSpec((1,) + shape, lambda b, m: (b + off,) + (0,) * len(shape))
    dqs, dkvs = [g[0] for g in grads], [g[1] for g in grads]
    sums = [((total, C), f32), ((2 * total, C), f32)]
    held = [pltpu.VMEM((L, C), bf16), pltpu.VMEM((total, 2 * rows), bf16), pltpu.VMEM((2 * total, L), bf16)]
    if fast:
        outs = [((8, C // 8, 3 * wch), bf16)] * 2
        held += [pltpu.VMEM(s, d) for s, d in sums] + [pltpu.VMEM((C, 3 * wch), f32)]
    else:
        outs = sums
    outs = [((total, 1), f32)] + outs
    return pl.pallas_call(
        functools.partial(heads_back_kernel, parts=parts, rows=rows, wch=wch, fast=fast, chained=bool(start)),
        grid_spec=pltpu.PrefetchScalarGridSpec(
            num_scalar_prefetch=1,
            grid=(B,),
            in_specs=[row_in] * 4
            + [fixed(wq.shape), fixed(wkv.shape)]
            + [per(v.shape[1:]) for v in dqs + dkvs]
            + [fixed(v.shape) for v in start],
            out_specs=[row] * 4 + [fixed(s) for s, _ in outs],
            scratch_shapes=held,
        ),
        out_shape=[jax.ShapeDtypeStruct((B, rows, C), bf16)] * 4 + [jax.ShapeDtypeStruct(s, d) for s, d in outs],
        compiler_params=pltpu.CompilerParams(vmem_limit_bytes=VMEM_BYTES),
        cost_estimate=LIGHT,
        name="heads_back",
    )(meta, *xb, wq, wkv, *dqs, *dkvs, *start)


def blocked(w, count):
    across, heads = w.shape
    wide = jnp.tile(jnp.transpose(w), (count, count))
    row = lax.broadcasted_iota(jnp.int32, wide.shape, 0) // heads
    column = lax.broadcasted_iota(jnp.int32, wide.shape, 1) // across
    return jnp.where(row == column, wide, jnp.zeros_like(wide))


def pair_bias_kernel(meta, lens, pair_ref, wb_ref, low_ref, inv_ref, raw_ref, *rest, few, blocks, group):
    outs, scr = rest[:-1], rest[-1]
    c, t = pl.program_id(0), pl.program_id(1)
    lines, columns, cz = pair_ref.shape[1:]
    heads = few * blocks
    per = lines // group
    mean = jnp.full((cz, cz), 1.0 / cz, bf16)
    lane = lax.broadcasted_iota(jnp.int32, (columns, group * heads), 1) // heads
    table = []
    for n in range(per):
        x = [pair_ref[0, n * group + i] for i in range(group)]
        flat = columns % 16 == 0
        if flat:
            x = [jnp.concatenate(x, axis=0)]
        lows, inverses = [], []
        for v in x:
            centered = v.astype(f32) - dot(v, mean, NN)
            inverse = lax.rsqrt(dot((centered * centered).astype(bf16), mean, NN) + epsilon)
            lows.append((centered * inverse).astype(bf16))
            inverses.append(inverse)
        if flat:
            lows = [lows[0][i * columns : (i + 1) * columns] for i in range(group)]
            inverses = [inverses[0][i * columns : (i + 1) * columns] for i in range(group)]
        spread = inverses[0][:, : group * heads]
        for i in range(1, group):
            spread = jnp.where(lane == i, inverses[i][:, : group * heads], spread)
        inv_ref[0, n] = spread
        for i in range(group):
            low_ref[0, n * group + i] = lows[i]
        table.append(jnp.concatenate(lows, axis=1))
    out = dot(jnp.concatenate(table, axis=0), wb_ref[...], NT)
    for n in range(per):
        part = out[n * columns : (n + 1) * columns]
        raw_ref[0, n] = part
        start = pl.multiple_of((t * per + n) * group * heads, group * heads)
        scr[pl.ds(start, group * heads), :] = jnp.transpose(part)

    @pl.when(t == pl.num_programs(1) - 1)
    def _():
        core = meta[0] % 2
        rows = scr.shape[0] // heads
        place = lax.broadcasted_iota(jnp.int32, (columns, rows), 0) + meta[1] * columns
        valid = place < lens[c]
        half = len(outs) // 2
        for k in range(half):
            for f in range(few):
                for e in range(2):
                    h = (2 * k + (core ^ e)) * few + f
                    v = jnp.transpose(scr[pl.ds(h, rows, stride=heads), :])
                    outs[e * half + k][0, f] = jnp.where(valid, v * LOG2E, fill_value).astype(bf16)


def pair_specs(pair, heads, group):
    lines = tile_of(pair.shape[1], PAIR_LINES)
    columns, cz = pair.shape[2:]
    return (
        lines,
        pl.BlockSpec((1, lines, columns, cz), lambda c, t, *_: (c, t, 0, 0)),
        pl.BlockSpec((1, lines // group, columns, group * heads), lambda c, t, *_: (c, t, 0, 0)),
        jax.ShapeDtypeStruct((pair.shape[0], pair.shape[1] // group, columns, group * heads), f32),
    )


def pair_bias(meta, lens, pair, wb, *, few, blocks, group):
    ncx, rows, columns, cz = pair.shape
    heads = few * blocks
    lines, spec, thin, thin_shape = pair_specs(pair, heads, group)
    out = jax.ShapeDtypeStruct((ncx, few, columns, rows), bf16)
    return pl.pallas_call(
        functools.partial(pair_bias_kernel, few=few, blocks=blocks, group=group),
        grid_spec=pltpu.PrefetchScalarGridSpec(
            num_scalar_prefetch=2,
            grid=(ncx, rows // lines),
            in_specs=[spec, fixed(wb.shape)],
            out_specs=[spec, thin, thin]
            + [pl.BlockSpec((1, few, columns, rows), lambda c, t, *_: (c, 0, 0, 0))] * blocks,
            scratch_shapes=[pltpu.VMEM((rows * heads, columns), f32)],
        ),
        out_shape=[jax.ShapeDtypeStruct(pair.shape, bf16), thin_shape, thin_shape] + [out] * blocks,
        compiler_params=pltpu.CompilerParams(vmem_limit_bytes=VMEM_BYTES),
        cost_estimate=LIGHT,
        name="pair_bias",
    )(meta, lens, pair, wb)


def pair_back_kernel(meta, low_ref, inv_ref, raw_ref, w2_ref, mean_ref, *rest, few, blocks, group):
    grads = rest[:blocks]
    out_ref, gw_ref, scr, acc = rest[blocks:]
    c, t = pl.program_id(0), pl.program_id(1)
    lines, columns, cz = low_ref.shape[1:]
    heads = few * blocks
    per = lines // group

    @pl.when((c == 0) & (t == 0))
    def _():
        acc[...] = jnp.zeros_like(acc)

    @pl.when(t == 0)
    def _():
        core = meta[0] % 2
        rows = scr.shape[0] // heads
        half = blocks // 2
        for k in range(half):
            for f in range(few):
                for e in range(2):
                    h = (2 * k + (core ^ e)) * few + f
                    scr[pl.ds(h, rows, stride=heads), :] = jnp.transpose(grads[e * half + k][0, f].astype(f32))

    ds, prods, xs = [], [], []
    for n in range(per):
        start = pl.multiple_of((t * per + n) * group * heads, group * heads)
        x = jnp.transpose(scr[pl.ds(start, group * heads), :])
        d = x * inv_ref[0, n]
        prod = d * raw_ref[0, n]
        hi = prod.astype(bf16)
        d = d.astype(bf16)
        xs.append(x.astype(bf16))
        ds.append(jnp.concatenate([d, d], axis=1))
        prods.append(jnp.concatenate([hi, (prod - hi.astype(f32)).astype(bf16)], axis=1))
    upstream = dot(jnp.concatenate(ds, axis=0), w2_ref[...], NN)
    along = dot(jnp.concatenate(prods, axis=0), mean_ref[...], NN)
    table = []
    for n in range(per):
        lows = [low_ref[0, n * group + i] for i in range(group)]
        ns = slice(n * columns, (n + 1) * columns)
        for i in range(group):
            zs = slice(i * cz, (i + 1) * cz)
            out_ref[0, n * group + i] = upstream[ns, zs] - lows[i].astype(f32) * along[ns, zs]
        table.append(jnp.concatenate(lows, axis=1))
    acc[...] += dot(jnp.concatenate(xs, axis=0), jnp.concatenate(table, axis=0), TN)

    @pl.when((c == pl.num_programs(0) - 1) & (t == pl.num_programs(1) - 1))
    def _():
        total = acc[0:heads, 0:cz]
        for i in range(1, group):
            total += acc[i * heads : (i + 1) * heads, i * cz : (i + 1) * cz]
        gw_ref[...] = total


def pair_back(meta, low, inv, raw, w, grads, *, few, blocks, group):
    ncx, rows, columns, cz = low.shape
    heads = few * blocks
    lines, spec, thin, _ = pair_specs(low, heads, group)
    mean = jnp.mean(w.astype(f32), axis=0, keepdims=True)
    w2 = jnp.concatenate([blocked(w, group), blocked(jnp.broadcast_to(-mean, w.shape).astype(bf16), group)], axis=0)
    ones = blocked(jnp.full(w.shape, 1.0 / cz, bf16), group)
    ones = jnp.concatenate([ones, ones], axis=0)
    return pl.pallas_call(
        functools.partial(pair_back_kernel, few=few, blocks=blocks, group=group),
        grid_spec=pltpu.PrefetchScalarGridSpec(
            num_scalar_prefetch=1,
            grid=(ncx, rows // lines),
            in_specs=[spec, thin, thin, fixed(w2.shape), fixed(ones.shape)]
            + [pl.BlockSpec((1, few, columns, rows), lambda c, t, *_: (c, 0, 0, 0))] * blocks,
            out_specs=[spec, fixed((heads, cz))],
            scratch_shapes=[pltpu.VMEM((rows * heads, columns), f32), pltpu.VMEM((group * heads, group * cz), f32)],
        ),
        out_shape=[jax.ShapeDtypeStruct(low.shape, f32), jax.ShapeDtypeStruct((heads, cz), f32)],
        compiler_params=pltpu.CompilerParams(vmem_limit_bytes=VMEM_BYTES),
        cost_estimate=LIGHT,
        name="pair_back",
    )(meta, low, inv, raw, w2, ones, *grads)


def column_sum(v):
    return jnp.sum(v, axis=0, keepdims=True)


def tiled(rows, width, steps):
    return pl.BlockSpec((rows, width), lambda t, *_: (jnp.minimum(t, steps - 1), 0))


def adapt_kernel(single_ref, cond_ref, gain, w_scale, b_scale, w_shift, x_ref):
    normed, _ = norm_rows(single_ref[...].astype(f32))
    cond_hat, _ = norm_rows(cond_ref[...].astype(f32))
    cond_low = (cond_hat * gain[...].astype(f32)).astype(bf16)
    gate = jax.nn.sigmoid(dot(cond_low, w_scale[...], NN) + b_scale[...].astype(f32))
    x_ref[...] = (gate * normed + dot(cond_low, w_shift[...], NN)).astype(bf16)


def adapt(single, cond, gain, w_scale, b_scale, w_shift):
    tokens, width = single.shape
    tile = tile_of(tokens)
    steps = tokens // tile
    return pl.pallas_call(
        adapt_kernel,
        grid=(steps,),
        in_specs=[tiled(tile, width, steps), tiled(tile, cond.shape[1], steps)]
        + [fixed(v.shape) for v in (gain, w_scale, b_scale, w_shift)],
        out_specs=tiled(tile, width, steps),
        out_shape=jax.ShapeDtypeStruct((tokens, width), bf16),
        compiler_params=pltpu.CompilerParams(vmem_limit_bytes=VMEM_BYTES),
        cost_estimate=LIGHT,
        name="adapt",
    )(single, cond, gain, w_scale, b_scale, w_shift)


def emit_rows(meta, step, count):
    place = meta[2 + step % 4] * 2 + (meta[1] ^ (step // 4))
    return pl.ds(pl.multiple_of(place * count, count), count)


def before_kernel(
    x_ref, cond_ref, cot_ref, w_gate, w_ac, b_ac, gain, w_scale, b_scale, w_shift, w_dn, w_tc, b_tc,
    gate_ref, acond_ref, tcond_ref, scale_ref, shift_ref, dh_ref,
):
    cond = cond_ref[...]
    tcond = jax.nn.sigmoid(dot(cond, w_tc[...], NN) + b_tc[...].astype(f32))
    tcond_ref[...] = tcond.astype(tcond_ref.dtype)
    d_tr = (tcond * cot_ref[...].astype(f32)).astype(bf16)
    dh_ref[...] = dot(d_tr, w_dn[...], NT).astype(dh_ref.dtype)
    acond_ref[...] = jax.nn.sigmoid(dot(cond, w_ac[...], NN) + b_ac[...].astype(f32)).astype(acond_ref.dtype)
    cond_hat, _ = norm_rows(cond.astype(f32))
    cond_low = (cond_hat * gain[...].astype(f32)).astype(bf16)
    scale = jax.nn.sigmoid(dot(cond_low, w_scale[...], NN) + b_scale[...].astype(f32))
    scale_ref[...] = scale.astype(scale_ref.dtype)
    shift_ref[...] = dot(cond_low, w_shift[...], NN).astype(shift_ref.dtype)
    gate_ref[...] = jax.nn.sigmoid(dot(x_ref[...], w_gate[...], NN)).astype(gate_ref.dtype)


def before(x_one, cond, cot, weights):
    w_gate, w_out, w_ac, b_ac, gain, w_scale, b_scale, w_shift, w_hg, w_hu, w_dn, w_tc, b_tc = weights
    used = (w_gate, w_ac, b_ac, gain, w_scale, b_scale, w_shift, w_dn, w_tc, b_tc)
    tokens, width = x_one.shape
    tile = tile_of(tokens)
    steps = tokens // tile
    outs = [(width, f32)] * 4 + [(width, bf16), (w_dn.shape[0], bf16)]
    return pl.pallas_call(
        before_kernel,
        grid=(steps,),
        in_specs=[tiled(tile, w, steps) for w in (width, cond.shape[1], width)] + [fixed(w.shape) for w in used],
        out_specs=[tiled(tile, w, steps) for w, _ in outs],
        out_shape=[jax.ShapeDtypeStruct((tokens, w), d) for w, d in outs],
        compiler_params=pltpu.CompilerParams(vmem_limit_bytes=VMEM_BYTES),
        cost_estimate=LIGHT,
        name="before",
    )(x_one, cond, cot, *used)


def middle_kernel(
    meta, x_ref, single_ref, cond_ref, cot_ref, gate_ref, acond_ref, tcond_ref, scale_ref, shift_ref, dh_ref,
    a0, a1, a2, a3, w_gate, w_out, gain, w_scale, w_shift, w_hg, w_hu, w_dn,
    out_ref, dmid_ref, dxg_ref, da0, da1, da2, da3, s_ac, s_scale, s_tc, s_gain, *rest, tiles, fast,
):
    core = meta[0] % 2
    step = pl.program_id(0)
    if fast:
        out_w, g_hidden, g_square, g_cond, g_norm, g_dn = rest
    else:
        g_hidden, g_square, g_cond, g_norm, g_dn = rest

    @pl.when(step == 0)
    def _():
        for ref in (g_hidden, g_square, g_cond, g_norm, g_dn, s_ac, s_scale, s_tc, s_gain):
            ref[...] = jnp.zeros_like(ref)

    @pl.when(step < tiles)
    def _():
        cond = cond_ref[...]
        first = core == 0

        def attended():
            return jnp.concatenate(
                [
                    jnp.where(first, a0[...], a1[...]),
                    jnp.where(first, a1[...], a0[...]),
                    jnp.where(first, a2[...], a3[...]),
                    jnp.where(first, a3[...], a2[...]),
                ],
                axis=1,
            ).astype(f32)

        gated = (attended() * gate_ref[...]).astype(bf16)
        branch = dot(gated, w_out[...], NN)
        mid = single_ref[...].astype(f32) + acond_ref[...] * branch
        normed, inverse = norm_rows(mid)
        x_two = (scale_ref[...] * normed + shift_ref[...].astype(f32)).astype(bf16)
        hgate = dot(x_two, w_hg[...], NN)
        hup = dot(x_two, w_hu[...], NN)
        sig = jax.nn.sigmoid(hgate)
        silu = hgate * sig
        hidden = (silu * hup).astype(bf16)
        d_hidden = dh_ref[...].astype(f32)
        d_hg = (d_hidden * hup * sig * (1.0 + hgate * (1.0 - sig))).astype(bf16)
        d_hu = (d_hidden * silu).astype(bf16)
        tcond = tcond_ref[...]
        dy = cot_ref[...].astype(f32)
        tr_branch = dot(hidden, w_dn[...], NN)
        out_ref[...] = (mid + tcond * tr_branch).astype(bf16)
        d_trc = dy * tr_branch * tcond * (1.0 - tcond)
        s_tc[...] += column_sum(d_trc)
        g_cond[0] += dot(cond, d_trc.astype(bf16), TN)
        g_dn[...] += dot(hidden, (tcond * dy).astype(bf16), TN)
        g_hidden[0] += dot(x_two, d_hg, TN)
        g_hidden[1] += dot(x_two, d_hu, TN)
        g_two = dot(d_hg, w_hg[...], NT) + dot(d_hu, w_hu[...], NT)
        scale = scale_ref[...]
        cond_hat, _ = norm_rows(cond.astype(f32))
        cond_low = (cond_hat * gain[...].astype(f32)).astype(bf16)
        d_scale = g_two * normed * scale * (1.0 - scale)
        s_scale[...] += column_sum(d_scale)
        d_scale = d_scale.astype(bf16)
        d_shift = g_two.astype(bf16)
        g_norm[0] += dot(cond_low, d_scale, TN)
        g_norm[1] += dot(cond_low, d_shift, TN)
        d_cond = dot(d_scale, w_scale[...], NT) + dot(d_shift, w_shift[...], NT)
        s_gain[...] += column_sum(d_cond * cond_hat)
        d_mid = dy + norm_back(normed, inverse, g_two * scale)
        dmid_ref[...] = d_mid
        acond = acond_ref[...]
        d_attn = (acond * d_mid).astype(bf16)
        d_ac = d_mid * branch * acond * (1.0 - acond)
        s_ac[...] += column_sum(d_ac)
        g_cond[1] += dot(cond, d_ac.astype(bf16), TN)
        g_square[0] += dot(gated, d_attn, TN)
        d_gated = dot(d_attn, w_out[...], NT)
        gate = gate_ref[...]
        d_att = (d_gated * gate).astype(bf16)
        d_gate = (d_gated * attended() * gate * (1.0 - gate)).astype(bf16)
        g_square[1] += dot(x_ref[...], d_gate, TN)
        dxg_ref[...] = dot(d_gate, w_gate[...], NT).astype(bf16)
        q = d_att.shape[1] // 4
        parts = [d_att[:, i * q : (i + 1) * q] for i in range(4)]
        da0[...] = jnp.where(first, parts[0], parts[1])
        da1[...] = jnp.where(first, parts[1], parts[0])
        da2[...] = jnp.where(first, parts[2], parts[3])
        da3[...] = jnp.where(first, parts[3], parts[2])

    if fast:

        @pl.when(step >= tiles)
        def _():
            emit = step - tiles
            place = meta[2 + emit % 4] * 2 + (meta[1] ^ (emit // 4))
            for g in range(4):
                at = 0
                for one, two, count in (
                    (g_hidden.at[0], None, 8),
                    (g_hidden.at[1], None, 8),
                    (g_square.at[0], g_square.at[1], 8),
                    (g_cond.at[0], g_cond.at[1], 8),
                    (g_norm.at[0], g_norm.at[1], 8),
                    (g_dn, g_dn, 16),
                ):
                    n, lanes = one.shape[0] // count, one.shape[1] // 4
                    take = lambda ref, row: ref[pl.ds(pl.multiple_of(row, n), n), g * lanes : (g + 1) * lanes]
                    if two is None:
                        part = take(one, place * n)
                    elif one is two:
                        part = jnp.concatenate([take(one, 2 * place * n), take(one, (2 * place + 1) * n)], axis=1)
                    else:
                        part = jnp.concatenate([take(one, place * n), take(two, place * n)], axis=1)
                    out_w[g, 0, at : at + n, :] = part.astype(bf16)
                    at += n


def middle(meta, x_one, single, cond, cot, gates, atts, weights, fast):
    tokens, width = single.shape
    tile = tile_of(tokens)
    tiles = tokens // tile
    cs = cond.shape[1]
    quarter = atts[0].shape[1]
    w_gate, w_out, w_ac, b_ac, gain, w_scale, b_scale, w_shift, w_hg, w_hu, w_dn, w_tc, b_tc = weights
    fold = lambda n: jax.ShapeDtypeStruct((1, n), f32)
    sums = [fold(width), fold(width), fold(width), fold(cs)]
    grads = [(2,) + w_hg.shape, (2,) + w_out.shape, (2,) + w_ac.shape, (2,) + w_scale.shape, w_dn.shape]
    row_out = [(width, bf16), (width, f32), (width, bf16)] + [(quarter, bf16)] * 4
    used = (w_gate, w_out, gain, w_scale, w_shift, w_hg, w_hu, w_dn)
    if fast:
        lanes = width // 2
        rows = sum(w.size for w in weights if w.shape[0] > 1) // (8 * 4 * lanes)
        more_specs = [pl.BlockSpec((4, 1, rows, lanes), lambda t, *_: (0, jnp.maximum(t - tiles, 0), 0, 0))]
        more = [jax.ShapeDtypeStruct((4, 8, rows, lanes), bf16)]
        scratch = [pltpu.VMEM(g, f32) for g in grads]
    else:
        more_specs = [fixed(g) for g in grads]
        more = [jax.ShapeDtypeStruct(g, f32) for g in grads]
        scratch = []
    return pl.pallas_call(
        functools.partial(middle_kernel, tiles=tiles, fast=fast),
        grid_spec=pltpu.PrefetchScalarGridSpec(
            num_scalar_prefetch=1,
            grid=(tiles + 8 * fast,),
            in_specs=[tiled(tile, w, tiles) for w in (width, width, cs, width)]
            + [tiled(tile, v.shape[1], tiles) for v in gates]
            + [tiled(tile, quarter, tiles)] * 4
            + [fixed(w.shape) for w in used],
            out_specs=[tiled(tile, w, tiles) for w, _ in row_out] + [fixed(g.shape) for g in sums] + more_specs,
            scratch_shapes=scratch,
        ),
        out_shape=[jax.ShapeDtypeStruct((tokens, w), d) for w, d in row_out] + sums + more,
        compiler_params=pltpu.CompilerParams(vmem_limit_bytes=VMEM_BYTES),
        cost_estimate=LIGHT,
        name="middle",
    )(meta, x_one, single, cond, cot, *gates, *atts, *used)


def last_kernel(
    meta, d0, d1, d2, d3, d4, d5, d6, single_ref, cond_ref, dmid_ref, gain, w_scale, b_scale, w_shift,
    out_ref, s_scale, s_gain, *rest, fast,
):
    if fast:
        keep_ref, send_ref, g_norm = rest
    else:
        (g_norm,) = rest

    @pl.when(pl.program_id(0) == 0)
    def _():
        for ref in (g_norm, s_scale, s_gain):
            ref[...] = jnp.zeros_like(ref)

    late_half = pl.program_id(0) >= pl.num_programs(0) // 2
    g_one = d6[...].astype(f32)
    for one, two in ((d0, d1), (d2, d3), (d4, d5)):
        g_one += jnp.where(late_half, two[...], one[...]).astype(f32)
    normed, inverse = norm_rows(single_ref[...].astype(f32))
    cond_hat, _ = norm_rows(cond_ref[...].astype(f32))
    cond_low = (cond_hat * gain[...].astype(f32)).astype(bf16)
    scale = jax.nn.sigmoid(dot(cond_low, w_scale[...], NN) + b_scale[...].astype(f32))
    d_scale = g_one * normed * scale * (1.0 - scale)
    s_scale[...] += column_sum(d_scale)
    d_scale = d_scale.astype(bf16)
    d_shift = g_one.astype(bf16)
    g_norm[0] += dot(cond_low, d_scale, TN)
    g_norm[1] += dot(cond_low, d_shift, TN)
    d_cond = dot(d_scale, w_scale[...], NT) + dot(d_shift, w_shift[...], NT)
    s_gain[...] += column_sum(d_cond * cond_hat)
    out_ref[...] = dmid_ref[...] + norm_back(normed, inverse, g_one * scale)

    if fast:

        @pl.when(pl.program_id(0) == pl.num_programs(0) - 1)
        def _():
            n, wide = g_norm.shape[1] // 8, g_norm.shape[2] // 2
            for e, ref in enumerate((keep_ref, send_ref)):
                for p in range(2):
                    lanes = pl.ds(pl.multiple_of(((meta[0] // 2) ^ p) * wide, wide), wide)
                    for i in range(8):
                        ref[p, i] = g_norm[(meta[0] % 2) ^ e, emit_rows(meta, i, n), lanes].astype(bf16)


def last(meta, ds, single, cond, dmid, gain, w_scale, b_scale, w_shift, fast):
    tokens, width = single.shape
    tile = tile_of(tokens)
    steps = tokens // tile
    cs = cond.shape[1]
    grads = (2,) + w_scale.shape
    if fast:
        more = [jax.ShapeDtypeStruct((2, 8, cs // 8, width // 2), bf16)] * 2
        scratch = [pltpu.VMEM(grads, f32)]
    else:
        more = [jax.ShapeDtypeStruct(grads, f32)]
        scratch = []
    more = [jax.ShapeDtypeStruct((1, width), f32), jax.ShapeDtypeStruct((1, cs), f32)] + more
    row = tiled(tile, width, steps)
    half = steps // 2
    early_row = pl.BlockSpec((tile, width), lambda t, *_: (jnp.minimum(t, half - 1), 0))
    late_row = pl.BlockSpec((tile, width), lambda t, *_: (jnp.maximum(t - half, 0), 0))
    return pl.pallas_call(
        functools.partial(last_kernel, fast=fast),
        grid_spec=pltpu.PrefetchScalarGridSpec(
            num_scalar_prefetch=1,
            grid=(steps,),
            in_specs=[early_row, late_row] * 3
            + [row, row]
            + [tiled(tile, cs, steps), row]
            + [fixed(w.shape) for w in (gain, w_scale, b_scale, w_shift)],
            out_specs=[row] + [fixed(g.shape) for g in more],
            scratch_shapes=scratch,
        ),
        out_shape=[jax.ShapeDtypeStruct((tokens, width), f32)] + more,
        compiler_params=pltpu.CompilerParams(vmem_limit_bytes=VMEM_BYTES),
        cost_estimate=LIGHT,
        name="last",
    )(meta, *ds, single, cond, dmid, gain, w_scale, b_scale, w_shift)


def swap(value, bit):
    return lax.ppermute(value, "head", [(i, i ^ bit) for i in range(lax.axis_size("head"))])


def across(value):
    return lax.ppermute(value, "samp", [(i, i ^ 1) for i in range(8)])


def slot(value, bit):
    return lax.ppermute(value, "samp", [(i, i ^ (2 * bit)) for i in range(8)])


def add(*terms):
    total = terms[0].astype(f32)
    for term in terms[1:]:
        total = total + term.astype(f32)
    return total


def tie(value, *others):
    return lax.optimization_barrier((value,) + others)[0]


def low(*terms):
    return add(*terms).astype(bf16)


Z_ORDER = (0, 2, 1, 3)


def x_step(block):
    return block[:4], across(block[4:])


def z_first(keep, got):
    return slot(low(keep[2:], got[2:]), 1)


def z_second(keep, got, z_got):
    return slot(low(keep[1], got[1], z_got[1]), 2)


def z_total(keep, got, z_got, last_got):
    return add(keep[0], got[0], z_got[0], last_got)


def fence(*values):
    return lax.optimization_barrier(values)


def total_step(vector, step):
    if step < 2:
        return vector + swap(vector, 1 << step)
    if step == 2:
        return vector + across(vector)
    return vector + slot(vector, step - 2)


def pack_w(w_heads, wide):
    return (
        jnp.concatenate([w[:wide] for w in w_heads], axis=0),
        jnp.concatenate([w[wide:] for w in w_heads], axis=0),
    )


def on_device(
    single,
    cond,
    pair,
    complex_length,
    sample_complex,
    cotangent,
    gain_one,
    w_scale_one,
    b_scale_one,
    w_shift_one,
    w_query,
    b_query,
    w_key,
    w_value,
    w_gate,
    w_out,
    w_pair,
    w_attn_cond,
    b_attn_cond,
    gain_two,
    w_scale_two,
    b_scale_two,
    w_shift_two,
    w_hidden_gate,
    w_hidden_up,
    w_hidden_down,
    w_tr_cond,
    b_tr_cond,
):
    groups = lax.axis_size("head")
    devices = lax.axis_size("samp")
    me = lax.axis_index("head")
    place = lax.axis_index("samp")
    core = me % 2
    part = me // 2
    samples, rows, width = single.shape
    cs = cond.shape[2]
    tokens = samples * rows
    length = rows * groups
    heads = w_pair.shape[1]
    few = heads // groups
    dim = width // heads
    wide = few * dim
    complexes, _, columns, _ = pair.shape
    chunks = 2 * groups
    chunk = length // chunks
    halves = range(groups // 2)
    fast = devices == 8 and groups == 4 and columns == chunk
    line = lambda v: v.reshape(1, -1)
    flat = lambda v: v.reshape(tokens, width)
    first = core == 0

    if fast:
        z, x = place // 2, place % 2
        order = z ^ jnp.array(Z_ORDER, jnp.int32)
        slots = jnp.stack([order * 2 + x, order * 2 + 1 - x], axis=1).reshape(8)
    else:
        x = jnp.zeros((), jnp.int32)
        order, slots = jnp.zeros((4,), jnp.int32), jnp.arange(chunks, dtype=jnp.int32)
    meta = jnp.concatenate([jnp.stack([me, x]).astype(jnp.int32), order, sample_complex, slots])
    pair_meta = jnp.stack([me, place]).astype(jnp.int32)
    group = 8
    sizes = dict(few=few, blocks=groups, group=group)
    single_t, cond_t, cot_t = flat(single), cond.reshape(tokens, cs), flat(cotangent)
    weights_one = (line(gain_one), w_scale_one, line(b_scale_one), w_shift_one)
    weights_two = (
        w_gate, w_out, w_attn_cond, line(b_attn_cond), line(gain_two), w_scale_two, line(b_scale_two), w_shift_two,
        w_hidden_gate, w_hidden_up, w_hidden_down, w_tr_cond, line(b_tr_cond),
    )

    def own_heads(*weights):
        columns_of = lambda w, k: lax.dynamic_slice_in_dim(w, (2 * k + core) * wide, wide, w.ndim - 1)
        w_heads = [jnp.concatenate([columns_of(w, k).T for w in weights[:3]], axis=0) for k in halves]
        b_heads = [columns_of(weights[3].astype(f32), k)[:, None] for k in halves]
        return w_heads, b_heads, *pack_w(w_heads, wide)

    parts = [(k, 0, wide) for k in halves]
    by_sample = lambda v: v.reshape(samples, rows, -1)
    by_token = lambda v: v.reshape(-1, v.shape[-1])
    attend_one = lambda k, blocks, biases: attend(meta, blocks, w_heads[k], b_heads[k], biases, nh=few, hd=dim)
    middle_one = lambda x_one, gates, atts: middle(meta, x_one, single_t, cond_t, cot_t, gates, atts, weights_two, fast)
    back_one = lambda kept, own, near: attend_back(
        meta, *kept[2:], *kept[:2], own, near, chunks, complexes, base=0, nh=few, hd=dim, fast=fast
    )

    def q_sums(gb):
        zero = jnp.zeros((wide,), f32)
        out = []
        for k in halves:
            mine = gb[k * wide : (k + 1) * wide].reshape(-1)
            out += [jnp.where(first, mine, zero), jnp.where(first, zero, mine)]
        return out

    w_blocked = blocked(w_pair, group)
    pair_low, pair_inverse, pair_raw, *bias = pair_bias(pair_meta, complex_length, pair, w_blocked, **sizes)
    near_bias = [swap(v, 1) for v in bias[groups // 2 :]]
    owns = [jnp.concatenate([bias[k], near_bias[k]], axis=-1) for k in halves]

    if fast:
        both_owns = jnp.stack(owns)
        owns, both_owns, single_t = fence(owns, both_owns, single_t)
        far_0, z_0, x_own = slot(owns[0], 2), [slot(owns[0], 1)], across(both_owns)
        x_one = adapt(single_t, cond_t, *weights_one)
        far_0, z_0, x_own, x_one, owns = fence(far_0, z_0, x_own, x_one, owns)
        x_far = swap(x_one, 2)
        far_1 = slot(owns[1], 2)
        z_0.append(slot(far_0, 1))
        x_0 = [across(far_0), across(z_0[0])]
        far_1, z_0, x_0, owns, x_mid, qkv = fence(far_1, z_0, x_0, owns, x_one, (w_query, w_key, w_value, b_query))
        w_heads, b_heads, w_q, w_kv = own_heads(*qkv)
        x_0.append(across(z_0[1]))
        x_1 = [across(far_1)]
        z_1 = [slot(owns[1], 1), slot(far_1, 1)]
        gates = before(x_mid, cond_t, cot_t, weights_two)
        x_far, x_0, x_1, z_1, gates, x_mid, w_heads, b_heads, w_q, w_kv = fence(
            x_far, x_0, x_1, z_1, gates, x_mid, w_heads, b_heads, w_q, w_kv
        )
        x_cross, x_near = swap(x_far, 1), swap(x_mid, 1)
        x_1 += [across(v) for v in z_1]
        blocks = [by_sample(v) for v in (x_one, x_near, x_far, x_cross)]
        pairs_of = lambda k, here, there: [
            pair_of for v, w in zip(here, [(x_own, k)] + [(u, None) for u in there]) for pair_of in ((v, None), w)
        ]
        kept = [attend_one(0, blocks, pairs_of(0, [owns[0], far_0] + z_0, x_0))]
        kept, x_1 = fence(kept, x_1)
        near_atts = [swap(kept[0][1], 1)]
        kept.append(attend_one(1, blocks, pairs_of(1, [owns[1], far_1] + z_1, x_1)))
        kept, near_atts = fence(kept, near_atts)
        near_atts.append(swap(kept[1][1], 1))
        atts = [by_token(v) for k in halves for v in (kept[k][0], near_atts[k])]

        block_out, d_mid, d_xg, da0, da1, da2, da3, s_ac, s_scale2, s_tc, s_gain2, w_mid = middle_one(x_one, gates, atts)
        near_att = [swap(by_sample(v), 1) for v in (da1, da3)]
        near_att, w_mid = fence(near_att, w_mid)
        mid = lax.psum_scatter(w_mid, "head", scatter_dimension=0, tiled=False)

        dq_0, dkv_0, *db_0 = back_one(kept[0], by_sample(da0), near_att[0])
        db_0, kept_1 = fence(db_0, kept[1])
        keep_a, got_a, keep_b, got_b = db_0[0], across(db_0[1]), db_0[2], across(db_0[3])
        dq_1, dkv_1, *db_1 = back_one(kept_1, by_sample(da2), near_att[1])
        dq_1, db_1, got_a = fence(dq_1, db_1, got_a)
        keep_c, got_c, keep_d = db_1[0], across(db_1[1]), db_1[2]
        zs_a = z_first(keep_a, got_a)
        cut = samples // 2
        back_heads = lambda grads, span, start, full: heads_back(
            meta, blocks, w_q, w_kv, grads, parts, wch=wide, fast=full, span=span, start=start
        )
        near_1, cross_1, far_1, own_1, *start = back_heads([(dq_0, dkv_0), (dq_1, dkv_1)], (0, cut), (), False)
        near_1, cross_1, far_1, start, zs_a, dq_1 = fence(near_1, cross_1, far_1, start, zs_a, dq_1)
        cross_1 = swap(cross_1, 1)
        cross_1, dq_1, got_b = fence(cross_1, dq_1, got_b)
        half_1 = low(far_1, cross_1)
        half_1, dq_1 = fence(half_1, dq_1)
        far_x, near_x = [swap(half_1, 2)], [swap(near_1, 1)]
        zs_b, last_a = z_first(keep_b, got_b), z_second(keep_a, got_a, zs_a)
        near_2, cross_2, far_2, own_2, gb, keep_w, send_w = back_heads(
            [(dq_0, dkv_0), (dq_1, dkv_1)], (cut, samples - cut), start, True
        )
        near_2, cross_2, far_2, send_w, send_d, last_a, zs_b, far_x[0] = fence(
            near_2, cross_2, far_2, send_w, db_1[3], last_a, zs_b, far_x[0]
        )
        cross_2, got_d = swap(cross_2, 1), across(send_d)
        cross_2, got_c = fence(cross_2, got_c)
        far_x.append(swap(low(far_2, cross_2), 2))
        zs_c, last_b = z_first(keep_c, got_c), z_second(keep_b, got_b, zs_b)
        far_x[1], got_d, zs_c, last_b, send_w, mid, near_2 = fence(far_x[1], got_d, zs_c, last_b, send_w, mid, near_2)
        zs_d, last_c = z_first(keep_d, got_d), z_second(keep_c, got_c, zs_c)
        keep_m, got_m = x_step(mid)
        far_w = swap(send_w, 2)
        sums = [low(z_total(keep_a, got_a, zs_a, last_a)), low(z_total(keep_b, got_b, zs_b, last_b))]
        zs_d, last_c, sums, near_2 = fence(zs_d, last_c, sums, near_2)
        near_x.append(swap(near_2, 1))
        sums.append(low(z_total(keep_c, got_c, zs_c, last_c)))
        last_d = z_second(keep_d, got_d, zs_d)
        near_x, sums = fence(near_x, sums)
        grad_single, s_scale1, s_gain1, keep_l, send_l = last(
            meta, (*map(by_token, (own_1, own_2, *near_x, *far_x)), d_xg), single_t, cond_t, d_mid, *weights_one, fast
        )
        last_d, got_m, far_w, keep_l, send_l, s_gain1, s_scale1 = fence(
            last_d, got_m, far_w, keep_l, send_l, s_gain1, s_scale1
        )
        sums.append(low(z_total(keep_d, got_d, zs_d, last_d)))
        far_rows = swap(jnp.stack([v[..., rows:] for v in sums]), 1)
        near_l = swap(send_l, 1)
        z_m = z_first(keep_m, got_m)
        keep_h, got_h = x_step(low(keep_w, far_w))
        others = jnp.concatenate(
            [v.reshape(-1) for v in (s_gain1, s_scale1, *q_sums(gb), s_gain2, s_ac, s_scale2, s_tc)]
        )
        far_rows, near_l, others = fence(far_rows, near_l, others)
        far_l = swap(low(keep_l[1], near_l[1]), 2)
        pair_grads = [jnp.stack([v[..., :rows] for v in sums[2 * k : 2 * k + 2]]) for k in halves]
        pair_grads += [far_rows[:2], far_rows[2:]]
        grad_pair, grad_pair_weight = pair_back(pair_meta, pair_low, pair_inverse, pair_raw, w_pair, pair_grads, **sizes)
        far_l, got_h, z_m, grad_pair_weight = fence(far_l, got_h, z_m, grad_pair_weight)
        late = total_step(jnp.concatenate([grad_pair_weight.reshape(-1), others]), 0)
        keep_l, got_l = x_step(low(keep_l[0], near_l[0], far_l))
        e_m = z_second(keep_m, got_m, z_m)
        z_h = z_first(keep_h, got_h)
        late, got_l, e_m, z_h = fence(late, got_l, e_m, z_h)

        def settle(block):
            size = block.shape[1] // 2
            left, right = block[:, :size], block[:, size:]
            got = swap(jnp.where(first, right, left), 1)
            held = jnp.where(first, left, right)
            return jnp.where(first, held, got), jnp.where(first, got, held)

        late = total_step(late, 1)
        z_l = z_first(keep_l, got_l)
        e_h = z_second(keep_h, got_h, z_h)
        late, z_l, e_h = fence(late, z_l, e_h)
        late = total_step(late, 2)
        e_l = z_second(keep_l, got_l, z_l)
        late, e_l = fence(late, e_l)
        r_scale1, r_shift1 = settle(z_total(keep_l, got_l, z_l, e_l))
        r_heads = z_total(keep_h, got_h, z_h, e_h)
        n, m, half = width // 8, cs // 8, width // 4
        r_mid = z_total(keep_m, got_m, z_m, e_m)
        r_hg, r_hu = r_mid[:n], r_mid[n : 2 * n]
        r_out, r_gate = r_mid[2 * n : 3 * n, :half], r_mid[2 * n : 3 * n, half:]
        r_tc, r_ac = r_mid[3 * n : 3 * n + m, :half], r_mid[3 * n : 3 * n + m, half:]
        r_scale2, r_shift2 = r_mid[3 * n + m : 3 * n + 2 * m, :half], r_mid[3 * n + m : 3 * n + 2 * m, half:]
        r_down = jnp.concatenate([r_mid[3 * n + 2 * m :, :half], r_mid[3 * n + 2 * m :, half:]], axis=0)
        late = total_step(total_step(late, 3), 4)
    else:
        w_heads, b_heads, w_q, w_kv = own_heads(w_query, w_key, w_value, b_query)
        biases = []
        for own in owns:
            gathered = lax.all_gather(own, "samp", axis=0)
            moved = gathered.transpose(1, 2, 0, 3, 4).reshape(complexes, few, chunks, chunk, 2 * rows)
            biases.append([(moved[:, :, i], None) for i in range(chunks)])
        x_one = adapt(single_t, cond_t, *weights_one)
        x_far = swap(x_one, 2)
        blocks = [by_sample(v) for v in (x_one, swap(x_one, 1), x_far, swap(x_far, 1))]
        kept = [attend_one(k, blocks, biases[k]) for k in halves]
        atts = [by_token(v) for k in halves for v in (kept[k][0], swap(kept[k][1], 1))]
        block_out, d_mid, d_xg, da0, da1, da2, da3, s_ac, s_scale2, s_tc, s_gain2, *w_mid = middle_one(x_one, before(x_one, cond_t, cot_t, weights_two), atts)
        head_grads, sums = [], []
        for k, (own, sent) in enumerate(((da0, da1), (da2, da3))):
            dq, dkv, db = back_one(kept[k], by_sample(own), swap(by_sample(sent), 1))
            head_grads.append((dq, dkv))
            moved = db.transpose(1, 2, 0, 3, 4).reshape(complexes, few, devices, columns, 2 * rows)
            sums.append(lax.psum_scatter(moved, "samp", scatter_dimension=2, tiled=False))
        d_near, d_cross, d_far, d_own, gb, gq, gkv = heads_back(
            meta, blocks, w_q, w_kv, head_grads, parts, wch=wide, fast=fast
        )
        far_x = swap(low(d_far, swap(d_cross, 1)), 2)
        grad_single, s_scale1, s_gain1, w_last = last(
            meta, (*(u for v in (d_own, swap(d_near, 1), far_x) for u in jnp.split(flat(v), 2)), d_xg),
            single_t, cond_t, d_mid, *weights_one, fast,
        )
        pair_grads = [v[..., :rows] for v in sums] + [swap(v[..., rows:], 1) for v in sums]
        grad_pair, grad_pair_weight = pair_back(pair_meta, pair_low, pair_inverse, pair_raw, w_pair, pair_grads, **sizes)

        def total_of(stack):
            axis = stack.ndim - 1
            half = lax.psum_scatter(stack.astype(bf16), "head", scatter_dimension=axis, tiled=True).astype(f32)
            return lax.psum_scatter(half, "samp", scatter_dimension=axis - 1, tiled=True)

        grads = [
            jnp.concatenate([gq[k * wide : (k + 1) * wide], gkv[2 * k * wide : 2 * (k + 1) * wide]], axis=0) for k in halves
        ]
        held = jnp.where(part == 0, grads[0], grads[1])
        sent = jnp.where(part == 0, grads[1], grads[0])
        r_heads = add(held, swap(sent.astype(bf16), 2))
        r_heads = lax.psum_scatter(r_heads.T, "samp", scatter_dimension=0, tiled=True)
        (r_hg, r_hu), (r_out, r_gate), (r_tc, r_ac), (r_scale2, r_shift2), r_down = [total_of(v) for v in w_mid]
        r_scale1, r_shift1 = total_of(w_last)
        late = jnp.concatenate(
            [v.reshape(-1) for v in (grad_pair_weight, s_gain1, s_scale1, *q_sums(gb), s_gain2, s_ac, s_scale2, s_tc)]
        )
        late = lax.psum(late, ("samp", "head"))

    cuts = [heads * w_pair.shape[0]]
    for size in (cs, width, width, cs, width, width):
        cuts.append(cuts[-1] + size)
    sum_pair, sum_gain1, sum_scale1, sum_query, sum_gain2, sum_ac, sum_scale2, sum_tc = jnp.split(late, cuts)
    whole = (samples, rows, width)
    return (
        block_out.reshape(whole),
        grad_single.reshape(whole),
        grad_pair,
        sum_gain1,
        r_scale1,
        sum_scale1,
        r_shift1,
        r_heads[:, :wide],
        sum_query,
        r_heads[:, wide : 2 * wide],
        r_heads[:, 2 * wide :],
        r_gate,
        r_out,
        sum_pair.reshape(heads, -1).T,
        r_ac,
        sum_ac,
        sum_gain2,
        r_scale2,
        sum_scale2,
        r_shift2,
        r_hg,
        r_hu,
        r_down,
        r_tc,
        sum_tc,
    )


def solution(mesh):
    placed = (
        P("samp", "head", None),
        P("samp", "head", None),
        P(None, "head", "samp", None),
        P(),
        P("samp"),
        P("samp", "head", None),
        P(),
        P(),
        P(),
        P(),
        P(),
        P(),
        P(),
        P(),
        P(),
        P(),
        P(),
        P(),
        P(),
        P(),
        P(),
        P(),
        P(),
        P(),
        P(),
        P(),
        P(),
        P(),
    )
    return jax.shard_map(
        on_device,
        mesh=mesh,
        in_specs=placed,
        out_specs=(
            P("samp", "head", None),
            P("samp", "head", None),
            P(None, "head", "samp", None),
            P(),
            P("samp", "head"),
            P(),
            P("samp", "head"),
            P("samp", "head"),
            P(),
            P("samp", "head"),
            P("samp", "head"),
            P("samp", "head"),
            P("samp", "head"),
            P(),
            P("samp", "head"),
            P(),
            P(),
            P("samp", "head"),
            P(),
            P("samp", "head"),
            P("samp", "head"),
            P("samp", "head"),
            P("samp", "head"),
            P("samp", "head"),
            P(),
        ),
        check_vma=False,
    )
```

```python
import functools
import math

import jax
import jax.numpy as jnp
from jax import lax
from jax.experimental import pallas as pl
from jax.experimental.pallas import tpu as pltpu
from jax.sharding import PartitionSpec as P

f32, bf16 = jnp.float32, jnp.bfloat16
epsilon = 1e-05
fill_value = -1e30
LOG2E = math.log2(math.e)
VMEM_BYTES = 60 << 20
PAIR_LINES = (8, 16, 24, 32, 64, 192)
NN, NT, TN = ((1,), (0,)), ((1,), (1,)), ((0,), (0,))


LIGHT = pl.CostEstimate(flops=1 << 20, bytes_accessed=1 << 20, transcendentals=0)


def dot(a, b, dims):
    return lax.dot_general(a, b, (dims, ((), ())), preferred_element_type=f32)


def norm_rows(inputs):
    mean_val = jnp.mean(inputs, axis=-1, keepdims=True)
    centered = inputs - mean_val
    variance = jnp.mean(centered * centered, axis=-1, keepdims=True)
    inverse = lax.rsqrt(variance + epsilon)
    return (centered * inverse, inverse)


def norm_back(normed, inverse, upstream):
    mean_grad = jnp.mean(upstream, axis=-1, keepdims=True)
    mean_dot = jnp.mean(upstream * normed, axis=-1, keepdims=True)
    return inverse * (upstream - mean_grad - normed * mean_dot)


def tile_of(tokens, sizes=(8, 16, 32, 64, 128, 256)):
    return max(t for t in sizes if tokens % t == 0)


def fixed(shape):
    return pl.BlockSpec(shape, lambda *_: (0,) * len(shape), pipeline_mode=pl.Buffered(1))


META = 6


def attend_kernel(meta, x0, x1, x2, x3, w_ref, bq_ref, *rest, which, nh, hd, rows, jc, nchunk, qscale):
    bias_hbm = rest[:nchunk]
    o_ref, far_ref, p_ref, q_ref, k_ref, v_ref, l_ref, xs, ks, ss, bias_ref, sems = rest[nchunk:]
    b = pl.program_id(0)
    g = meta[0]
    cplx = meta[META + b]
    per_block = nchunk // 4

    def copies():
        return [
            pltpu.make_async_copy(
                bias_hbm[i] if which[i] is None else bias_hbm[i].at[which[i]],
                bias_ref.at[meta[META + pl.num_programs(0) + i]],
                sems.at[i],
            )
            for i in range(nchunk)
        ]

    @pl.when(b == 0)
    def _():
        for copy in copies():
            copy.start()

    for r, x in enumerate((x0, x1, x2, x3)):
        xs[r * rows : (r + 1) * rows, :] = x[0]
    wch = nh * hd
    q = dot(w_ref[0:wch, :], xs[0 : 2 * rows, :], NT) + bq_ref[...]
    q_ref[0] = (q * qscale).astype(bf16)
    kv = dot(w_ref[wch : 3 * wch, :], xs[...], NT).astype(bf16)
    k_ref[0] = kv[0:wch]
    v_ref[0] = kv[wch:]

    @pl.when(b == 0)
    def _():
        for copy in copies():
            copy.wait()

    ones = jnp.ones((16, kv.shape[1]), bf16)
    outs = []
    sums = []
    before = None
    for h in range(nh + 1):
        if h < nh:
            ks[h % 2, :, :] = jnp.transpose(k_ref[0, h * hd : (h + 1) * hd, :])
            qT = q_ref[0, h * hd : (h + 1) * hd, :]
        m = None
        for t in range(nchunk):
            part = slice(t * jc, (t + 1) * jc)
            if h < nh:
                s_idx = ((t // per_block) ^ g) * per_block + t % per_block
                s = dot(ks[h % 2, part, :], qT, NN) + bias_ref[s_idx, cplx, h].astype(f32)
                ss[h % 2, part, :] = s
                mt = jnp.max(s.reshape(jc // 8, 8, s.shape[1]), axis=0)
                m = mt if m is None else jnp.maximum(m, mt)
            if h > 0:
                p_ref[0, h - 1, part, :] = jnp.exp2(ss[(h - 1) % 2, part, :] - before).astype(bf16)
        if h < nh:
            m = jnp.max(m, axis=0, keepdims=True)
        if h > 0:
            va = jnp.concatenate([v_ref[0, (h - 1) * hd : h * hd, :], ones], axis=0)
            oT = dot(va, p_ref[0, h - 1], NN)
            l = oT[hd : hd + 1, :]
            outs.append(oT[:hd] / l)
            sums.append(l)
        before = m
    l_ref[0] = jnp.concatenate(sums, axis=0)
    o = jnp.transpose(jnp.concatenate(outs, axis=0)).astype(bf16)
    o_ref[0] = o[:rows]
    far_ref[0] = o[rows:]


def attend(meta, xb, wT, bq, biases, *, nh, hd):
    B, rows, C = xb[0].shape
    nchunk = len(biases)
    biases, which = zip(*biases)
    ncx, _, jc, qi = biases[0].shape[-4:]
    L = nchunk * jc
    wch = nh * hd
    kern = functools.partial(
        attend_kernel, which=which, nh=nh, hd=hd, rows=rows, jc=jc, nchunk=nchunk, qscale=LOG2E / math.sqrt(hd)
    )
    xspec = pl.BlockSpec((1, rows, C), lambda b, m: (b, 0, 0))
    per = lambda shape: pl.BlockSpec((1,) + shape, lambda b, m: (b,) + (0,) * len(shape))
    return pl.pallas_call(
        kern,
        grid_spec=pltpu.PrefetchScalarGridSpec(
            num_scalar_prefetch=1,
            grid=(B,),
            in_specs=[xspec] * 4
            + [fixed(wT.shape), fixed(bq.shape)]
            + [pl.BlockSpec(memory_space=pl.ANY)] * nchunk,
            out_specs=[
                per((rows, wch)),
                per((rows, wch)),
                per((nh, L, qi)),
                per((wch, qi)),
                per((wch, L)),
                per((wch, L)),
                per((nh, qi)),
            ],
            scratch_shapes=[
                pltpu.VMEM((L, C), bf16),
                pltpu.VMEM((2, L, hd), bf16),
                pltpu.VMEM((2, L, qi), f32),
                pltpu.VMEM((nchunk, ncx, nh, jc, qi), bf16),
                pltpu.SemaphoreType.DMA((nchunk,)),
            ],
        ),
        out_shape=[
            jax.ShapeDtypeStruct((B, rows, wch), bf16),
            jax.ShapeDtypeStruct((B, rows, wch), bf16),
            jax.ShapeDtypeStruct((B, nh, L, qi), bf16),
            jax.ShapeDtypeStruct((B, wch, qi), bf16),
            jax.ShapeDtypeStruct((B, wch, L), bf16),
            jax.ShapeDtypeStruct((B, wch, L), bf16),
            jax.ShapeDtypeStruct((B, nh, qi), f32),
        ],
        compiler_params=pltpu.CompilerParams(vmem_limit_bytes=VMEM_BYTES),
        cost_estimate=LIGHT,
        name="attend",
    )(meta, *xb, wT, bq, *biases)


def attend_back_kernel(
    meta, p_ref, q_ref, k_ref, v_ref, l_ref, o0, o1, do0, do1, *rest, base, nh, hd, jc, nchunk, scale, fast
):
    dq_ref, dkv_ref = rest[:2]
    vs, ds, acc = rest[-3:]
    b = pl.program_id(0)
    g = meta[0]
    cplx = meta[META + b]
    per_block = nchunk // 4
    wch = nh * hd
    L = nchunk * jc

    @pl.when(b == 0)
    def _():
        acc[...] = jnp.zeros_like(acc)

    dO = jnp.transpose(jnp.concatenate([do0[0], do1[0]], axis=0).astype(f32))
    O = jnp.transpose(jnp.concatenate([o0[0], o1[0]], axis=0).astype(f32))
    prod = dO * O
    qi = dO.shape[1]
    row = lax.broadcasted_iota(jnp.int32, (16, qi), 0)
    ones = jnp.ones((16, L), bf16)
    for h in range(nh + 1):
        if h < nh:
            hs = slice(h * hd, (h + 1) * hd)
            his = slice((base + h) * hd, (base + h + 1) * hd)
            linv = 1.0 / l_ref[0, base + h : base + h + 1, :]
            dOh = (dO[his] * linv).astype(bf16)
            delta = jnp.sum(prod[his], axis=0, keepdims=True) * linv
            hi = delta.astype(bf16).astype(f32)
            extra = jnp.where(row == 0, -hi, jnp.where(row == 1, hi - delta, 0.0)).astype(bf16)
            dOa = jnp.concatenate([dOh, extra], axis=0)
            vs[h % 2] = jnp.transpose(jnp.concatenate([v_ref[0, hs, :], ones], axis=0))
        if h > 0:
            ps = slice((h - 1) * hd, h * hd)
            dk_parts, dv_parts = [], []
            kk, qq = k_ref[0, ps, :], q_ref[0, ps, :]
        for t in range(nchunk):
            r, u = t // per_block, t % per_block
            s_idx = (r ^ g) * per_block + u
            ts = slice(t * jc, (t + 1) * jc)
            if h < nh:
                d = dot(vs[h % 2, ts, :], dOa, NN) * p_ref[0, h, ts, :].astype(f32)
                acc[s_idx, cplx, h] += d
                ds[h % 2, ts, :] = d.astype(bf16)
            if h > 0:
                dk_parts.append(dot(ds[(h - 1) % 2, ts, :], qq, NT))
                dv_parts.append(dot(p_ref[0, h - 1, ts, :], dO_before, NT))
        if h > 0:
            dq_ref[0, ps, :] = (dot(kk, ds[(h - 1) % 2], NN) * scale).astype(bf16)
            dk = jnp.transpose(jnp.concatenate(dk_parts, axis=0)) * (1.0 / LOG2E)
            dkv_ref[0, ps, :] = dk.astype(bf16)
            dv = jnp.transpose(jnp.concatenate(dv_parts, axis=0))
            dkv_ref[0, wch + (h - 1) * hd : wch + h * hd, :] = dv.astype(bf16)
        if h < nh:
            dO_before = dOh

    @pl.when(b == pl.num_programs(0) - 1)
    def _():
        if fast:
            for i in range(4):
                for e in range(2):
                    block = acc[meta[2 + i] * 2 + (meta[1] ^ e)].astype(bf16)
                    for c in range(block.shape[0]):
                        rest[2 + 2 * c + e][i] = block[c]
        else:
            rest[2][...] = acc[...].astype(bf16)


def attend_back(meta, p, q, k, v, l, o0, o1, do0, do1, nchunk, ncx, *, base, nh, hd, fast):
    B, held, L, qi = p.shape
    rows = o0.shape[1]
    jc = L // nchunk
    wch = nh * hd
    kern = functools.partial(
        attend_back_kernel, base=base, nh=nh, hd=hd, jc=jc, nchunk=nchunk, scale=1.0 / math.sqrt(hd), fast=fast
    )
    per = lambda shape: pl.BlockSpec((1,) + shape, lambda b, m: (b,) + (0,) * len(shape))
    some = lambda shape: pl.BlockSpec((1,) + shape, lambda b, m: (b, base // nh) + (0,) * (len(shape) - 1))
    db = (nchunk, ncx, nh, jc, qi)
    outs = [((4,) + db[2:], bf16)] * (2 * ncx) if fast else [(db, bf16)]
    return pl.pallas_call(
        kern,
        grid_spec=pltpu.PrefetchScalarGridSpec(
            num_scalar_prefetch=1,
            grid=(B,),
            in_specs=[some((nh, L, qi)), some((wch, qi)), some((wch, L)), some((wch, L)), per((held, qi))]
            + [per((rows, held * hd))] * 4,
            out_specs=[per((wch, qi)), per((2 * wch, L))] + [fixed(s) for s, _ in outs],
            scratch_shapes=[
                pltpu.VMEM((2, L, hd + 16), bf16),
                pltpu.VMEM((2, L, qi), bf16),
                pltpu.VMEM(db, f32),
            ],
        ),
        out_shape=[jax.ShapeDtypeStruct((B, wch, qi), bf16), jax.ShapeDtypeStruct((B, 2 * wch, L), bf16)]
        + [jax.ShapeDtypeStruct(s, d) for s, d in outs],
        compiler_params=pltpu.CompilerParams(vmem_limit_bytes=VMEM_BYTES),
        cost_estimate=LIGHT,
        name="attend_back",
    )(meta, p, q, k, v, l, o0, o1, do0, do1)


def heads_back_kernel(meta, x0, x1, x2, x3, wq_ref, wkv_ref, *rest, parts, rows, wch, fast, chained):
    n = len(parts)
    dqs, dkvs, rest = rest[:n], rest[n : 2 * n], rest[2 * n :]
    if chained:
        start_b, start_q, start_kv = rest[:3]
        rest = rest[3:]
    near_ref, cross_ref, far_ref, own_ref, gb_ref = rest[:5]
    if fast:
        keep_ref, send_ref, xs, dq, dkv, gq, gkv, gt = rest[5:]
    else:
        gq, gkv, xs, dq, dkv = rest[5:]
    b = pl.program_id(0)

    @pl.when(b == 0)
    def _():
        gq[...] = start_q[...] if chained else jnp.zeros_like(gq)
        gkv[...] = start_kv[...] if chained else jnp.zeros_like(gkv)
        gb_ref[...] = start_b[...] if chained else jnp.zeros_like(gb_ref)

    for r, x in enumerate((x0, x1, x2, x3)):
        xs[r * rows : (r + 1) * rows, :] = x[0]
    for (chunk, at, size), q, kv in zip(parts, dqs, dkvs):
        start = chunk * wch + at
        dq[start : start + size, :] = q[0]
        start = 2 * chunk * wch + at
        dkv[start : start + size, :] = kv[0, :size]
        dkv[start + wch : start + wch + size, :] = kv[0, size:]
    q, kv = dq[...], dkv[...]
    gb_ref[...] += jnp.sum(q.astype(f32), axis=1, keepdims=True)
    gq[...] += dot(q, xs[0 : 2 * rows, :], NN)
    gkv[...] += dot(kv, xs[...], NN)
    kv = jnp.transpose(kv)
    q = jnp.transpose(q)
    dx = dot(kv[2 * rows :], wkv_ref[...], NN).astype(bf16)
    far_ref[0] = dx[:rows]
    cross_ref[0] = dx[rows:]
    dx = (dot(kv[: 2 * rows], wkv_ref[...], NN) + dot(q, wq_ref[...], NN)).astype(bf16)
    own_ref[0] = dx[:rows]
    near_ref[0] = dx[rows:]

    if fast:

        @pl.when(b == pl.num_programs(0) - 1)
        def _():
            for e, ref in enumerate((keep_ref, send_ref)):
                chunk = (meta[0] // 2) ^ e
                half = pl.ds(pl.multiple_of(chunk * wch, wch), wch)
                gt[:, 0:wch] = jnp.transpose(gq[half, :])
                both = pl.ds(pl.multiple_of(chunk * 2 * wch, wch), 2 * wch)
                gt[:, wch:] = jnp.transpose(gkv[both, :])
                count = gt.shape[0] // 8
                for i in range(8):
                    ref[i] = gt[emit_rows(meta, i, count), :].astype(bf16)


def heads_back(meta, xb, wq, wkv, grads, parts, *, wch, fast, span=None, start=()):
    rows, C = xb[0].shape[1:]
    off, B = span or (0, xb[0].shape[0])
    L = 4 * rows
    total = wq.shape[0]
    row = pl.BlockSpec((1, rows, C), lambda b, m: (b, 0, 0))
    row_in = pl.BlockSpec((1, rows, C), lambda b, m: (b + off, 0, 0))
    per = lambda shape: pl.BlockSpec((1,) + shape, lambda b, m: (b + off,) + (0,) * len(shape))
    dqs, dkvs = [g[0] for g in grads], [g[1] for g in grads]
    sums = [((total, C), f32), ((2 * total, C), f32)]
    held = [pltpu.VMEM((L, C), bf16), pltpu.VMEM((total, 2 * rows), bf16), pltpu.VMEM((2 * total, L), bf16)]
    if fast:
        outs = [((8, C // 8, 3 * wch), bf16)] * 2
        held += [pltpu.VMEM(s, d) for s, d in sums] + [pltpu.VMEM((C, 3 * wch), f32)]
    else:
        outs = sums
    outs = [((total, 1), f32)] + outs
    return pl.pallas_call(
        functools.partial(heads_back_kernel, parts=parts, rows=rows, wch=wch, fast=fast, chained=bool(start)),
        grid_spec=pltpu.PrefetchScalarGridSpec(
            num_scalar_prefetch=1,
            grid=(B,),
            in_specs=[row_in] * 4
            + [fixed(wq.shape), fixed(wkv.shape)]
            + [per(v.shape[1:]) for v in dqs + dkvs]
            + [fixed(v.shape) for v in start],
            out_specs=[row] * 4 + [fixed(s) for s, _ in outs],
            scratch_shapes=held,
        ),
        out_shape=[jax.ShapeDtypeStruct((B, rows, C), bf16)] * 4 + [jax.ShapeDtypeStruct(s, d) for s, d in outs],
        compiler_params=pltpu.CompilerParams(vmem_limit_bytes=VMEM_BYTES),
        cost_estimate=LIGHT,
        name="heads_back",
    )(meta, *xb, wq, wkv, *dqs, *dkvs, *start)


def blocked(w, count):
    across, heads = w.shape
    wide = jnp.tile(jnp.transpose(w), (count, count))
    row = lax.broadcasted_iota(jnp.int32, wide.shape, 0) // heads
    column = lax.broadcasted_iota(jnp.int32, wide.shape, 1) // across
    return jnp.where(row == column, wide, jnp.zeros_like(wide))


def pair_bias_kernel(meta, lens, pair_ref, wb_ref, low_ref, inv_ref, raw_ref, *rest, few, blocks, group):
    outs, scr = rest[:-1], rest[-1]
    c, t = pl.program_id(0), pl.program_id(1)
    lines, columns, cz = pair_ref.shape[1:]
    heads = few * blocks
    per = lines // group
    mean = jnp.full((cz, cz), 1.0 / cz, bf16)
    lane = lax.broadcasted_iota(jnp.int32, (columns, group * heads), 1) // heads
    table = []
    for n in range(per):
        x = [pair_ref[0, n * group + i] for i in range(group)]
        flat = columns % 16 == 0
        if flat:
            x = [jnp.concatenate(x, axis=0)]
        lows, inverses = [], []
        for v in x:
            centered = v.astype(f32) - dot(v, mean, NN)
            inverse = lax.rsqrt(dot((centered * centered).astype(bf16), mean, NN) + epsilon)
            lows.append((centered * inverse).astype(bf16))
            inverses.append(inverse)
        if flat:
            lows = [lows[0][i * columns : (i + 1) * columns] for i in range(group)]
            inverses = [inverses[0][i * columns : (i + 1) * columns] for i in range(group)]
        spread = inverses[0][:, : group * heads]
        for i in range(1, group):
            spread = jnp.where(lane == i, inverses[i][:, : group * heads], spread)
        inv_ref[0, n] = spread
        for i in range(group):
            low_ref[0, n * group + i] = lows[i]
        table.append(jnp.concatenate(lows, axis=1))
    out = dot(jnp.concatenate(table, axis=0), wb_ref[...], NT)
    for n in range(per):
        part = out[n * columns : (n + 1) * columns]
        raw_ref[0, n] = part
        start = pl.multiple_of((t * per + n) * group * heads, group * heads)
        scr[pl.ds(start, group * heads), :] = jnp.transpose(part)

    @pl.when(t == pl.num_programs(1) - 1)
    def _():
        core = meta[0] % 2
        rows = scr.shape[0] // heads
        place = lax.broadcasted_iota(jnp.int32, (columns, rows), 0) + meta[1] * columns
        valid = place < lens[c]
        half = len(outs) // 2
        for k in range(half):
            for f in range(few):
                for e in range(2):
                    h = (2 * k + (core ^ e)) * few + f
                    v = jnp.transpose(scr[pl.ds(h, rows, stride=heads), :])
                    outs[e * half + k][0, f] = jnp.where(valid, v * LOG2E, fill_value).astype(bf16)


def pair_specs(pair, heads, group):
    lines = tile_of(pair.shape[1], PAIR_LINES)
    columns, cz = pair.shape[2:]
    return (
        lines,
        pl.BlockSpec((1, lines, columns, cz), lambda c, t, *_: (c, t, 0, 0)),
        pl.BlockSpec((1, lines // group, columns, group * heads), lambda c, t, *_: (c, t, 0, 0)),
        jax.ShapeDtypeStruct((pair.shape[0], pair.shape[1] // group, columns, group * heads), f32),
    )


def pair_bias(meta, lens, pair, wb, *, few, blocks, group):
    ncx, rows, columns, cz = pair.shape
    heads = few * blocks
    lines, spec, thin, thin_shape = pair_specs(pair, heads, group)
    out = jax.ShapeDtypeStruct((ncx, few, columns, rows), bf16)
    return pl.pallas_call(
        functools.partial(pair_bias_kernel, few=few, blocks=blocks, group=group),
        grid_spec=pltpu.PrefetchScalarGridSpec(
            num_scalar_prefetch=2,
            grid=(ncx, rows // lines),
            in_specs=[spec, fixed(wb.shape)],
            out_specs=[spec, thin, thin]
            + [pl.BlockSpec((1, few, columns, rows), lambda c, t, *_: (c, 0, 0, 0))] * blocks,
            scratch_shapes=[pltpu.VMEM((rows * heads, columns), f32)],
        ),
        out_shape=[jax.ShapeDtypeStruct(pair.shape, bf16), thin_shape, thin_shape] + [out] * blocks,
        compiler_params=pltpu.CompilerParams(vmem_limit_bytes=VMEM_BYTES),
        cost_estimate=LIGHT,
        name="pair_bias",
    )(meta, lens, pair, wb)


def pair_back_kernel(meta, low_ref, inv_ref, raw_ref, w2_ref, mean_ref, *rest, few, blocks, group):
    grads = rest[:blocks]
    out_ref, gw_ref, scr, acc = rest[blocks:]
    c, t = pl.program_id(0), pl.program_id(1)
    lines, columns, cz = low_ref.shape[1:]
    heads = few * blocks
    per = lines // group

    @pl.when((c == 0) & (t == 0))
    def _():
        acc[...] = jnp.zeros_like(acc)

    @pl.when(t == 0)
    def _():
        core = meta[0] % 2
        rows = scr.shape[0] // heads
        half = blocks // 2
        for k in range(half):
            for f in range(few):
                for e in range(2):
                    h = (2 * k + (core ^ e)) * few + f
                    scr[pl.ds(h, rows, stride=heads), :] = jnp.transpose(grads[e * half + k][0, f].astype(f32))

    ds, prods, xs = [], [], []
    for n in range(per):
        start = pl.multiple_of((t * per + n) * group * heads, group * heads)
        x = jnp.transpose(scr[pl.ds(start, group * heads), :])
        d = x * inv_ref[0, n]
        prod = d * raw_ref[0, n]
        hi = prod.astype(bf16)
        d = d.astype(bf16)
        xs.append(x.astype(bf16))
        ds.append(jnp.concatenate([d, d], axis=1))
        prods.append(jnp.concatenate([hi, (prod - hi.astype(f32)).astype(bf16)], axis=1))
    upstream = dot(jnp.concatenate(ds, axis=0), w2_ref[...], NN)
    along = dot(jnp.concatenate(prods, axis=0), mean_ref[...], NN)
    table = []
    for n in range(per):
        lows = [low_ref[0, n * group + i] for i in range(group)]
        ns = slice(n * columns, (n + 1) * columns)
        for i in range(group):
            zs = slice(i * cz, (i + 1) * cz)
            out_ref[0, n * group + i] = upstream[ns, zs] - lows[i].astype(f32) * along[ns, zs]
        table.append(jnp.concatenate(lows, axis=1))
    acc[...] += dot(jnp.concatenate(xs, axis=0), jnp.concatenate(table, axis=0), TN)

    @pl.when((c == pl.num_programs(0) - 1) & (t == pl.num_programs(1) - 1))
    def _():
        total = acc[0:heads, 0:cz]
        for i in range(1, group):
            total += acc[i * heads : (i + 1) * heads, i * cz : (i + 1) * cz]
        gw_ref[...] = total


def pair_back(meta, low, inv, raw, w, grads, *, few, blocks, group):
    ncx, rows, columns, cz = low.shape
    heads = few * blocks
    lines, spec, thin, _ = pair_specs(low, heads, group)
    mean = jnp.mean(w.astype(f32), axis=0, keepdims=True)
    w2 = jnp.concatenate([blocked(w, group), blocked(jnp.broadcast_to(-mean, w.shape).astype(bf16), group)], axis=0)
    ones = blocked(jnp.full(w.shape, 1.0 / cz, bf16), group)
    ones = jnp.concatenate([ones, ones], axis=0)
    return pl.pallas_call(
        functools.partial(pair_back_kernel, few=few, blocks=blocks, group=group),
        grid_spec=pltpu.PrefetchScalarGridSpec(
            num_scalar_prefetch=1,
            grid=(ncx, rows // lines),
            in_specs=[spec, thin, thin, fixed(w2.shape), fixed(ones.shape)]
            + [pl.BlockSpec((1, few, columns, rows), lambda c, t, *_: (c, 0, 0, 0))] * blocks,
            out_specs=[spec, fixed((heads, cz))],
            scratch_shapes=[pltpu.VMEM((rows * heads, columns), f32), pltpu.VMEM((group * heads, group * cz), f32)],
        ),
        out_shape=[jax.ShapeDtypeStruct(low.shape, f32), jax.ShapeDtypeStruct((heads, cz), f32)],
        compiler_params=pltpu.CompilerParams(vmem_limit_bytes=VMEM_BYTES),
        cost_estimate=LIGHT,
        name="pair_back",
    )(meta, low, inv, raw, w2, ones, *grads)


def column_sum(v):
    return jnp.sum(v, axis=0, keepdims=True)


def tiled(rows, width, steps):
    return pl.BlockSpec((rows, width), lambda t, *_: (jnp.minimum(t, steps - 1), 0))


def adapt_kernel(single_ref, cond_ref, gain, w_scale, b_scale, w_shift, x_ref):
    normed, _ = norm_rows(single_ref[...].astype(f32))
    cond_hat, _ = norm_rows(cond_ref[...].astype(f32))
    cond_low = (cond_hat * gain[...].astype(f32)).astype(bf16)
    gate = jax.nn.sigmoid(dot(cond_low, w_scale[...], NN) + b_scale[...].astype(f32))
    x_ref[...] = (gate * normed + dot(cond_low, w_shift[...], NN)).astype(bf16)


def adapt(single, cond, gain, w_scale, b_scale, w_shift):
    tokens, width = single.shape
    tile = tile_of(tokens)
    steps = tokens // tile
    return pl.pallas_call(
        adapt_kernel,
        grid=(steps,),
        in_specs=[tiled(tile, width, steps), tiled(tile, cond.shape[1], steps)]
        + [fixed(v.shape) for v in (gain, w_scale, b_scale, w_shift)],
        out_specs=tiled(tile, width, steps),
        out_shape=jax.ShapeDtypeStruct((tokens, width), bf16),
        compiler_params=pltpu.CompilerParams(vmem_limit_bytes=VMEM_BYTES),
        cost_estimate=LIGHT,
        name="adapt",
    )(single, cond, gain, w_scale, b_scale, w_shift)


def emit_rows(meta, step, count):
    place = meta[2 + step % 4] * 2 + (meta[1] ^ (step // 4))
    return pl.ds(pl.multiple_of(place * count, count), count)


def before_kernel(
    x_ref, cond_ref, cot_ref, w_gate, w_ac, b_ac, gain, w_scale, b_scale, w_shift, w_dn, w_tc, b_tc,
    gate_ref, acond_ref, tcond_ref, scale_ref, shift_ref, dh_ref,
):
    cond = cond_ref[...]
    tcond = jax.nn.sigmoid(dot(cond, w_tc[...], NN) + b_tc[...].astype(f32))
    tcond_ref[...] = tcond.astype(tcond_ref.dtype)
    d_tr = (tcond * cot_ref[...].astype(f32)).astype(bf16)
    dh_ref[...] = dot(d_tr, w_dn[...], NT).astype(dh_ref.dtype)
    acond_ref[...] = jax.nn.sigmoid(dot(cond, w_ac[...], NN) + b_ac[...].astype(f32)).astype(acond_ref.dtype)
    cond_hat, _ = norm_rows(cond.astype(f32))
    cond_low = (cond_hat * gain[...].astype(f32)).astype(bf16)
    scale = jax.nn.sigmoid(dot(cond_low, w_scale[...], NN) + b_scale[...].astype(f32))
    scale_ref[...] = scale.astype(scale_ref.dtype)
    shift_ref[...] = dot(cond_low, w_shift[...], NN).astype(shift_ref.dtype)
    gate_ref[...] = jax.nn.sigmoid(dot(x_ref[...], w_gate[...], NN)).astype(gate_ref.dtype)


def before(x_one, cond, cot, weights):
    w_gate, w_out, w_ac, b_ac, gain, w_scale, b_scale, w_shift, w_hg, w_hu, w_dn, w_tc, b_tc = weights
    used = (w_gate, w_ac, b_ac, gain, w_scale, b_scale, w_shift, w_dn, w_tc, b_tc)
    tokens, width = x_one.shape
    tile = tile_of(tokens)
    steps = tokens // tile
    outs = [(width, f32)] * 4 + [(width, bf16), (w_dn.shape[0], bf16)]
    return pl.pallas_call(
        before_kernel,
        grid=(steps,),
        in_specs=[tiled(tile, w, steps) for w in (width, cond.shape[1], width)] + [fixed(w.shape) for w in used],
        out_specs=[tiled(tile, w, steps) for w, _ in outs],
        out_shape=[jax.ShapeDtypeStruct((tokens, w), d) for w, d in outs],
        compiler_params=pltpu.CompilerParams(vmem_limit_bytes=VMEM_BYTES),
        cost_estimate=LIGHT,
        name="before",
    )(x_one, cond, cot, *used)


def middle_kernel(
    meta, x_ref, single_ref, cond_ref, cot_ref, gate_ref, acond_ref, tcond_ref, scale_ref, shift_ref, dh_ref,
    a0, a1, a2, a3, w_gate, w_out, gain, w_scale, w_shift, w_hg, w_hu, w_dn,
    out_ref, dmid_ref, dxg_ref, da0, da1, da2, da3, s_ac, s_scale, s_tc, s_gain, *rest, tiles, fast,
):
    core = meta[0] % 2
    step = pl.program_id(0)
    if fast:
        out_w, g_hidden, g_square, g_cond, g_norm, g_dn = rest
    else:
        g_hidden, g_square, g_cond, g_norm, g_dn = rest

    @pl.when(step == 0)
    def _():
        for ref in (g_hidden, g_square, g_cond, g_norm, g_dn, s_ac, s_scale, s_tc, s_gain):
            ref[...] = jnp.zeros_like(ref)

    @pl.when(step < tiles)
    def _():
        cond = cond_ref[...]
        first = core == 0

        def attended():
            return jnp.concatenate(
                [
                    jnp.where(first, a0[...], a1[...]),
                    jnp.where(first, a1[...], a0[...]),
                    jnp.where(first, a2[...], a3[...]),
                    jnp.where(first, a3[...], a2[...]),
                ],
                axis=1,
            ).astype(f32)

        gated = (attended() * gate_ref[...]).astype(bf16)
        branch = dot(gated, w_out[...], NN)
        mid = single_ref[...].astype(f32) + acond_ref[...] * branch
        normed, inverse = norm_rows(mid)
        x_two = (scale_ref[...] * normed + shift_ref[...].astype(f32)).astype(bf16)
        hgate = dot(x_two, w_hg[...], NN)
        hup = dot(x_two, w_hu[...], NN)
        sig = jax.nn.sigmoid(hgate)
        silu = hgate * sig
        hidden = (silu * hup).astype(bf16)
        d_hidden = dh_ref[...].astype(f32)
        d_hg = (d_hidden * hup * sig * (1.0 + hgate * (1.0 - sig))).astype(bf16)
        d_hu = (d_hidden * silu).astype(bf16)
        tcond = tcond_ref[...]
        dy = cot_ref[...].astype(f32)
        tr_branch = dot(hidden, w_dn[...], NN)
        out_ref[...] = (mid + tcond * tr_branch).astype(bf16)
        d_trc = dy * tr_branch * tcond * (1.0 - tcond)
        s_tc[...] += column_sum(d_trc)
        g_cond[0] += dot(cond, d_trc.astype(bf16), TN)
        g_dn[...] += dot(hidden, (tcond * dy).astype(bf16), TN)
        g_hidden[0] += dot(x_two, d_hg, TN)
        g_hidden[1] += dot(x_two, d_hu, TN)
        g_two = dot(d_hg, w_hg[...], NT) + dot(d_hu, w_hu[...], NT)
        scale = scale_ref[...]
        cond_hat, _ = norm_rows(cond.astype(f32))
        cond_low = (cond_hat * gain[...].astype(f32)).astype(bf16)
        d_scale = g_two * normed * scale * (1.0 - scale)
        s_scale[...] += column_sum(d_scale)
        d_scale = d_scale.astype(bf16)
        d_shift = g_two.astype(bf16)
        g_norm[0] += dot(cond_low, d_scale, TN)
        g_norm[1] += dot(cond_low, d_shift, TN)
        d_cond = dot(d_scale, w_scale[...], NT) + dot(d_shift, w_shift[...], NT)
        s_gain[...] += column_sum(d_cond * cond_hat)
        d_mid = dy + norm_back(normed, inverse, g_two * scale)
        dmid_ref[...] = d_mid
        acond = acond_ref[...]
        d_attn = (acond * d_mid).astype(bf16)
        d_ac = d_mid * branch * acond * (1.0 - acond)
        s_ac[...] += column_sum(d_ac)
        g_cond[1] += dot(cond, d_ac.astype(bf16), TN)
        g_square[0] += dot(gated, d_attn, TN)
        d_gated = dot(d_attn, w_out[...], NT)
        gate = gate_ref[...]
        d_att = (d_gated * gate).astype(bf16)
        d_gate = (d_gated * attended() * gate * (1.0 - gate)).astype(bf16)
        g_square[1] += dot(x_ref[...], d_gate, TN)
        dxg_ref[...] = dot(d_gate, w_gate[...], NT).astype(bf16)
        q = d_att.shape[1] // 4
        parts = [d_att[:, i * q : (i + 1) * q] for i in range(4)]
        da0[...] = jnp.where(first, parts[0], parts[1])
        da1[...] = jnp.where(first, parts[1], parts[0])
        da2[...] = jnp.where(first, parts[2], parts[3])
        da3[...] = jnp.where(first, parts[3], parts[2])

    if fast:

        @pl.when(step >= tiles)
        def _():
            emit = step - tiles
            place = meta[2 + emit % 4] * 2 + (meta[1] ^ (emit // 4))
            for g in range(4):
                at = 0
                for one, two, count in (
                    (g_hidden.at[0], None, 8),
                    (g_hidden.at[1], None, 8),
                    (g_square.at[0], g_square.at[1], 8),
                    (g_cond.at[0], g_cond.at[1], 8),
                    (g_norm.at[0], g_norm.at[1], 8),
                    (g_dn, g_dn, 16),
                ):
                    n, lanes = one.shape[0] // count, one.shape[1] // 4
                    take = lambda ref, row: ref[pl.ds(pl.multiple_of(row, n), n), g * lanes : (g + 1) * lanes]
                    if two is None:
                        part = take(one, place * n)
                    elif one is two:
                        part = jnp.concatenate([take(one, 2 * place * n), take(one, (2 * place + 1) * n)], axis=1)
                    else:
                        part = jnp.concatenate([take(one, place * n), take(two, place * n)], axis=1)
                    out_w[g, 0, at : at + n, :] = part.astype(bf16)
                    at += n


def middle(meta, x_one, single, cond, cot, gates, atts, weights, fast):
    tokens, width = single.shape
    tile = tile_of(tokens)
    tiles = tokens // tile
    cs = cond.shape[1]
    quarter = atts[0].shape[1]
    w_gate, w_out, w_ac, b_ac, gain, w_scale, b_scale, w_shift, w_hg, w_hu, w_dn, w_tc, b_tc = weights
    fold = lambda n: jax.ShapeDtypeStruct((1, n), f32)
    sums = [fold(width), fold(width), fold(width), fold(cs)]
    grads = [(2,) + w_hg.shape, (2,) + w_out.shape, (2,) + w_ac.shape, (2,) + w_scale.shape, w_dn.shape]
    row_out = [(width, bf16), (width, f32), (width, bf16)] + [(quarter, bf16)] * 4
    used = (w_gate, w_out, gain, w_scale, w_shift, w_hg, w_hu, w_dn)
    if fast:
        lanes = width // 2
        rows = sum(w.size for w in weights if w.shape[0] > 1) // (8 * 4 * lanes)
        more_specs = [pl.BlockSpec((4, 1, rows, lanes), lambda t, *_: (0, jnp.maximum(t - tiles, 0), 0, 0))]
        more = [jax.ShapeDtypeStruct((4, 8, rows, lanes), bf16)]
        scratch = [pltpu.VMEM(g, f32) for g in grads]
    else:
        more_specs = [fixed(g) for g in grads]
        more = [jax.ShapeDtypeStruct(g, f32) for g in grads]
        scratch = []
    return pl.pallas_call(
        functools.partial(middle_kernel, tiles=tiles, fast=fast),
        grid_spec=pltpu.PrefetchScalarGridSpec(
            num_scalar_prefetch=1,
            grid=(tiles + 8 * fast,),
            in_specs=[tiled(tile, w, tiles) for w in (width, width, cs, width)]
            + [tiled(tile, v.shape[1], tiles) for v in gates]
            + [tiled(tile, quarter, tiles)] * 4
            + [fixed(w.shape) for w in used],
            out_specs=[tiled(tile, w, tiles) for w, _ in row_out] + [fixed(g.shape) for g in sums] + more_specs,
            scratch_shapes=scratch,
        ),
        out_shape=[jax.ShapeDtypeStruct((tokens, w), d) for w, d in row_out] + sums + more,
        compiler_params=pltpu.CompilerParams(vmem_limit_bytes=VMEM_BYTES),
        cost_estimate=LIGHT,
        name="middle",
    )(meta, x_one, single, cond, cot, *gates, *atts, *used)


def last_kernel(
    meta, d0, d1, d2, d3, d4, d5, d6, single_ref, cond_ref, dmid_ref, gain, w_scale, b_scale, w_shift,
    out_ref, s_scale, s_gain, *rest, fast,
):
    if fast:
        keep_ref, send_ref, g_norm = rest
    else:
        (g_norm,) = rest

    @pl.when(pl.program_id(0) == 0)
    def _():
        for ref in (g_norm, s_scale, s_gain):
            ref[...] = jnp.zeros_like(ref)

    late_half = pl.program_id(0) >= pl.num_programs(0) // 2
    g_one = d6[...].astype(f32)
    for one, two in ((d0, d1), (d2, d3), (d4, d5)):
        g_one += jnp.where(late_half, two[...], one[...]).astype(f32)
    normed, inverse = norm_rows(single_ref[...].astype(f32))
    cond_hat, _ = norm_rows(cond_ref[...].astype(f32))
    cond_low = (cond_hat * gain[...].astype(f32)).astype(bf16)
    scale = jax.nn.sigmoid(dot(cond_low, w_scale[...], NN) + b_scale[...].astype(f32))
    d_scale = g_one * normed * scale * (1.0 - scale)
    s_scale[...] += column_sum(d_scale)
    d_scale = d_scale.astype(bf16)
    d_shift = g_one.astype(bf16)
    g_norm[0] += dot(cond_low, d_scale, TN)
    g_norm[1] += dot(cond_low, d_shift, TN)
    d_cond = dot(d_scale, w_scale[...], NT) + dot(d_shift, w_shift[...], NT)
    s_gain[...] += column_sum(d_cond * cond_hat)
    out_ref[...] = dmid_ref[...] + norm_back(normed, inverse, g_one * scale)

    if fast:

        @pl.when(pl.program_id(0) == pl.num_programs(0) - 1)
        def _():
            n, wide = g_norm.shape[1] // 8, g_norm.shape[2] // 2
            for e, ref in enumerate((keep_ref, send_ref)):
                for p in range(2):
                    lanes = pl.ds(pl.multiple_of(((meta[0] // 2) ^ p) * wide, wide), wide)
                    for i in range(8):
                        ref[p, i] = g_norm[(meta[0] % 2) ^ e, emit_rows(meta, i, n), lanes].astype(bf16)


def last(meta, ds, single, cond, dmid, gain, w_scale, b_scale, w_shift, fast):
    tokens, width = single.shape
    tile = tile_of(tokens)
    steps = tokens // tile
    cs = cond.shape[1]
    grads = (2,) + w_scale.shape
    if fast:
        more = [jax.ShapeDtypeStruct((2, 8, cs // 8, width // 2), bf16)] * 2
        scratch = [pltpu.VMEM(grads, f32)]
    else:
        more = [jax.ShapeDtypeStruct(grads, f32)]
        scratch = []
    more = [jax.ShapeDtypeStruct((1, width), f32), jax.ShapeDtypeStruct((1, cs), f32)] + more
    row = tiled(tile, width, steps)
    half = steps // 2
    early_row = pl.BlockSpec((tile, width), lambda t, *_: (jnp.minimum(t, half - 1), 0))
    late_row = pl.BlockSpec((tile, width), lambda t, *_: (jnp.maximum(t - half, 0), 0))
    return pl.pallas_call(
        functools.partial(last_kernel, fast=fast),
        grid_spec=pltpu.PrefetchScalarGridSpec(
            num_scalar_prefetch=1,
            grid=(steps,),
            in_specs=[early_row, late_row] * 3
            + [row, row]
            + [tiled(tile, cs, steps), row]
            + [fixed(w.shape) for w in (gain, w_scale, b_scale, w_shift)],
            out_specs=[row] + [fixed(g.shape) for g in more],
            scratch_shapes=scratch,
        ),
        out_shape=[jax.ShapeDtypeStruct((tokens, width), f32)] + more,
        compiler_params=pltpu.CompilerParams(vmem_limit_bytes=VMEM_BYTES),
        cost_estimate=LIGHT,
        name="last",
    )(meta, *ds, single, cond, dmid, gain, w_scale, b_scale, w_shift)


def swap(value, bit):
    return lax.ppermute(value, "head", [(i, i ^ bit) for i in range(lax.axis_size("head"))])


def across(value):
    return lax.ppermute(value, "samp", [(i, i ^ 1) for i in range(8)])


def slot(value, bit):
    return lax.ppermute(value, "samp", [(i, i ^ (2 * bit)) for i in range(8)])


def add(*terms):
    total = terms[0].astype(f32)
    for term in terms[1:]:
        total = total + term.astype(f32)
    return total


def tie(value, *others):
    return lax.optimization_barrier((value,) + others)[0]


def low(*terms):
    return add(*terms).astype(bf16)


Z_ORDER = (0, 2, 1, 3)


def x_step(block):
    return block[:4], across(block[4:])


def z_first(keep, got):
    return slot(low(keep[2:], got[2:]), 1)


def z_second(keep, got, z_got):
    return slot(low(keep[1], got[1], z_got[1]), 2)


def z_total(keep, got, z_got, last_got):
    return add(keep[0], got[0], z_got[0], last_got)


def fence(*values):
    return lax.optimization_barrier(values)


def total_step(vector, step):
    if step < 2:
        return vector + swap(vector, 1 << step)
    if step == 2:
        return vector + across(vector)
    return vector + slot(vector, step - 2)


def pack_w(w_heads, wide):
    return (
        jnp.concatenate([w[:wide] for w in w_heads], axis=0),
        jnp.concatenate([w[wide:] for w in w_heads], axis=0),
    )


def on_device(
    single,
    cond,
    pair,
    complex_length,
    sample_complex,
    cotangent,
    gain_one,
    w_scale_one,
    b_scale_one,
    w_shift_one,
    w_query,
    b_query,
    w_key,
    w_value,
    w_gate,
    w_out,
    w_pair,
    w_attn_cond,
    b_attn_cond,
    gain_two,
    w_scale_two,
    b_scale_two,
    w_shift_two,
    w_hidden_gate,
    w_hidden_up,
    w_hidden_down,
    w_tr_cond,
    b_tr_cond,
):
    groups = lax.axis_size("head")
    devices = lax.axis_size("samp")
    me = lax.axis_index("head")
    place = lax.axis_index("samp")
    core = me % 2
    part = me // 2
    samples, rows, width = single.shape
    cs = cond.shape[2]
    tokens = samples * rows
    length = rows * groups
    heads = w_pair.shape[1]
    few = heads // groups
    dim = width // heads
    wide = few * dim
    complexes, _, columns, _ = pair.shape
    chunks = 2 * groups
    chunk = length // chunks
    halves = range(groups // 2)
    fast = devices == 8 and groups == 4 and columns == chunk
    line = lambda v: v.reshape(1, -1)
    flat = lambda v: v.reshape(tokens, width)
    first = core == 0

    if fast:
        z, x = place // 2, place % 2
        order = z ^ jnp.array(Z_ORDER, jnp.int32)
        slots = jnp.stack([order * 2 + x, order * 2 + 1 - x], axis=1).reshape(8)
    else:
        x = jnp.zeros((), jnp.int32)
        order, slots = jnp.zeros((4,), jnp.int32), jnp.arange(chunks, dtype=jnp.int32)
    meta = jnp.concatenate([jnp.stack([me, x]).astype(jnp.int32), order, sample_complex, slots])
    pair_meta = jnp.stack([me, place]).astype(jnp.int32)
    group = 8
    sizes = dict(few=few, blocks=groups, group=group)
    single_t, cond_t, cot_t = flat(single), cond.reshape(tokens, cs), flat(cotangent)
    weights_one = (line(gain_one), w_scale_one, line(b_scale_one), w_shift_one)
    weights_two = (
        w_gate, w_out, w_attn_cond, line(b_attn_cond), line(gain_two), w_scale_two, line(b_scale_two), w_shift_two,
        w_hidden_gate, w_hidden_up, w_hidden_down, w_tr_cond, line(b_tr_cond),
    )

    def own_heads(*weights):
        columns_of = lambda w, k: lax.dynamic_slice_in_dim(w, (2 * k + core) * wide, wide, w.ndim - 1)
        w_heads = [jnp.concatenate([columns_of(w, k).T for w in weights[:3]], axis=0) for k in halves]
        b_heads = [columns_of(weights[3].astype(f32), k)[:, None] for k in halves]
        return w_heads, b_heads, *pack_w(w_heads, wide)

    parts = [(k, 0, wide) for k in halves]
    by_sample = lambda v: v.reshape(samples, rows, -1)
    by_token = lambda v: v.reshape(-1, v.shape[-1])
    attend_one = lambda k, blocks, biases: attend(meta, blocks, w_heads[k], b_heads[k], biases, nh=few, hd=dim)
    middle_one = lambda x_one, gates, atts: middle(meta, x_one, single_t, cond_t, cot_t, gates, atts, weights_two, fast)
    back_one = lambda kept, own, near: attend_back(
        meta, *kept[2:], *kept[:2], own, near, chunks, complexes, base=0, nh=few, hd=dim, fast=fast
    )

    def q_sums(gb):
        zero = jnp.zeros((wide,), f32)
        out = []
        for k in halves:
            mine = gb[k * wide : (k + 1) * wide].reshape(-1)
            out += [jnp.where(first, mine, zero), jnp.where(first, zero, mine)]
        return out

    w_blocked = blocked(w_pair, group)
    pair_low, pair_inverse, pair_raw, *bias = pair_bias(pair_meta, complex_length, pair, w_blocked, **sizes)
    near_bias = [swap(v, 1) for v in bias[groups // 2 :]]
    owns = [jnp.concatenate([bias[k], near_bias[k]], axis=-1) for k in halves]

    if fast:
        both_owns = jnp.stack(owns)
        owns, both_owns, single_t = fence(owns, both_owns, single_t)
        far_0, z_0, x_own = slot(owns[0], 2), [slot(owns[0], 1)], across(both_owns)
        x_one = adapt(single_t, cond_t, *weights_one)
        far_0, z_0, x_own, x_one, owns = fence(far_0, z_0, x_own, x_one, owns)
        x_far = swap(x_one, 2)
        far_1 = slot(owns[1], 2)
        z_0.append(slot(far_0, 1))
        x_0 = [across(far_0), across(z_0[0])]
        far_1, z_0, x_0, owns, x_mid, qkv = fence(far_1, z_0, x_0, owns, x_one, (w_query, w_key, w_value, b_query))
        w_heads, b_heads, w_q, w_kv = own_heads(*qkv)
        x_0.append(across(z_0[1]))
        x_1 = [across(far_1)]
        z_1 = [slot(owns[1], 1), slot(far_1, 1)]
        gates = before(x_mid, cond_t, cot_t, weights_two)
        x_far, x_0, x_1, z_1, gates, x_mid, w_heads, b_heads, w_q, w_kv = fence(
            x_far, x_0, x_1, z_1, gates, x_mid, w_heads, b_heads, w_q, w_kv
        )
        x_cross, x_near = swap(x_far, 1), swap(x_mid, 1)
        x_1 += [across(v) for v in z_1]
        blocks = [by_sample(v) for v in (x_one, x_near, x_far, x_cross)]
        pairs_of = lambda k, here, there: [
            pair_of for v, w in zip(here, [(x_own, k)] + [(u, None) for u in there]) for pair_of in ((v, None), w)
        ]
        kept = [attend_one(0, blocks, pairs_of(0, [owns[0], far_0] + z_0, x_0))]
        kept, x_1 = fence(kept, x_1)
        near_atts = [swap(kept[0][1], 1)]
        kept.append(attend_one(1, blocks, pairs_of(1, [owns[1], far_1] + z_1, x_1)))
        kept, near_atts = fence(kept, near_atts)
        near_atts.append(swap(kept[1][1], 1))
        atts = [by_token(v) for k in halves for v in (kept[k][0], near_atts[k])]

        block_out, d_mid, d_xg, da0, da1, da2, da3, s_ac, s_scale2, s_tc, s_gain2, w_mid = middle_one(x_one, gates, atts)
        near_att = [swap(by_sample(v), 1) for v in (da1, da3)]
        near_att, w_mid = fence(near_att, w_mid)
        mid = lax.psum_scatter(w_mid, "head", scatter_dimension=0, tiled=False)

        dq_0, dkv_0, *db_0 = back_one(kept[0], by_sample(da0), near_att[0])
        db_0, kept_1 = fence(db_0, kept[1])
        keep_a, got_a, keep_b, got_b = db_0[0], across(db_0[1]), db_0[2], across(db_0[3])
        dq_1, dkv_1, *db_1 = back_one(kept_1, by_sample(da2), near_att[1])
        dq_1, db_1, got_a = fence(dq_1, db_1, got_a)
        keep_c, got_c, keep_d = db_1[0], across(db_1[1]), db_1[2]
        zs_a = z_first(keep_a, got_a)
        cut = samples // 2
        back_heads = lambda grads, span, start, full: heads_back(
            meta, blocks, w_q, w_kv, grads, parts, wch=wide, fast=full, span=span, start=start
        )
        near_1, cross_1, far_1, own_1, *start = back_heads([(dq_0, dkv_0), (dq_1, dkv_1)], (0, cut), (), False)
        near_1, cross_1, far_1, start, zs_a, dq_1 = fence(near_1, cross_1, far_1, start, zs_a, dq_1)
        cross_1 = swap(cross_1, 1)
        cross_1, dq_1, got_b = fence(cross_1, dq_1, got_b)
        half_1 = low(far_1, cross_1)
        half_1, dq_1 = fence(half_1, dq_1)
        far_x, near_x = [swap(half_1, 2)], [swap(near_1, 1)]
        zs_b, last_a = z_first(keep_b, got_b), z_second(keep_a, got_a, zs_a)
        near_2, cross_2, far_2, own_2, gb, keep_w, send_w = back_heads(
            [(dq_0, dkv_0), (dq_1, dkv_1)], (cut, samples - cut), start, True
        )
        near_2, cross_2, far_2, send_w, send_d, last_a, zs_b, far_x[0] = fence(
            near_2, cross_2, far_2, send_w, db_1[3], last_a, zs_b, far_x[0]
        )
        cross_2, got_d = swap(cross_2, 1), across(send_d)
        cross_2, got_c = fence(cross_2, got_c)
        far_x.append(swap(low(far_2, cross_2), 2))
        zs_c, last_b = z_first(keep_c, got_c), z_second(keep_b, got_b, zs_b)
        far_x[1], got_d, zs_c, last_b, send_w, mid, near_2 = fence(far_x[1], got_d, zs_c, last_b, send_w, mid, near_2)
        zs_d, last_c = z_first(keep_d, got_d), z_second(keep_c, got_c, zs_c)
        keep_m, got_m = x_step(mid)
        far_w = swap(send_w, 2)
        sums = [low(z_total(keep_a, got_a, zs_a, last_a)), low(z_total(keep_b, got_b, zs_b, last_b))]
        zs_d, last_c, sums, near_2 = fence(zs_d, last_c, sums, near_2)
        near_x.append(swap(near_2, 1))
        sums.append(low(z_total(keep_c, got_c, zs_c, last_c)))
        last_d = z_second(keep_d, got_d, zs_d)
        near_x, sums = fence(near_x, sums)
        grad_single, s_scale1, s_gain1, keep_l, send_l = last(
            meta, (*map(by_token, (own_1, own_2, *near_x, *far_x)), d_xg), single_t, cond_t, d_mid, *weights_one, fast
        )
        last_d, got_m, far_w, keep_l, send_l, s_gain1, s_scale1 = fence(
            last_d, got_m, far_w, keep_l, send_l, s_gain1, s_scale1
        )
        sums.append(low(z_total(keep_d, got_d, zs_d, last_d)))
        far_rows = swap(jnp.stack([v[..., rows:] for v in sums]), 1)
        near_l = swap(send_l, 1)
        z_m = z_first(keep_m, got_m)
        keep_h, got_h = x_step(low(keep_w, far_w))
        others = jnp.concatenate(
            [v.reshape(-1) for v in (s_gain1, s_scale1, *q_sums(gb), s_gain2, s_ac, s_scale2, s_tc)]
        )
        far_rows, near_l, others = fence(far_rows, near_l, others)
        far_l = swap(low(keep_l[1], near_l[1]), 2)
        pair_grads = [jnp.stack([v[..., :rows] for v in sums[2 * k : 2 * k + 2]]) for k in halves]
        pair_grads += [far_rows[:2], far_rows[2:]]
        grad_pair, grad_pair_weight = pair_back(pair_meta, pair_low, pair_inverse, pair_raw, w_pair, pair_grads, **sizes)
        far_l, got_h, z_m, grad_pair_weight = fence(far_l, got_h, z_m, grad_pair_weight)
        late = total_step(jnp.concatenate([grad_pair_weight.reshape(-1), others]), 0)
        keep_l, got_l = x_step(low(keep_l[0], near_l[0], far_l))
        e_m = z_second(keep_m, got_m, z_m)
        z_h = z_first(keep_h, got_h)
        late, got_l = fence(late, got_l)

        def settle(block):
            size = block.shape[1] // 2
            left, right = block[:, :size], block[:, size:]
            got = swap(jnp.where(first, right, left), 1)
            held = jnp.where(first, left, right)
            return jnp.where(first, held, got), jnp.where(first, got, held)

        late = total_step(late, 1)
        z_l = z_first(keep_l, got_l)
        late, z_l, z_h, e_m = fence(late, z_l, z_h, e_m)
        late = total_step(late, 2)
        e_l = z_second(keep_l, got_l, z_l)
        e_h = z_second(keep_h, got_h, z_h)
        late, e_l, e_h = fence(late, e_l, e_h)
        r_scale1, r_shift1 = settle(z_total(keep_l, got_l, z_l, e_l))
        r_heads = z_total(keep_h, got_h, z_h, e_h)
        n, m, half = width // 8, cs // 8, width // 4
        r_mid = z_total(keep_m, got_m, z_m, e_m)
        r_hg, r_hu = r_mid[:n], r_mid[n : 2 * n]
        r_out, r_gate = r_mid[2 * n : 3 * n, :half], r_mid[2 * n : 3 * n, half:]
        r_tc, r_ac = r_mid[3 * n : 3 * n + m, :half], r_mid[3 * n : 3 * n + m, half:]
        r_scale2, r_shift2 = r_mid[3 * n + m : 3 * n + 2 * m, :half], r_mid[3 * n + m : 3 * n + 2 * m, half:]
        r_down = jnp.concatenate([r_mid[3 * n + 2 * m :, :half], r_mid[3 * n + 2 * m :, half:]], axis=0)
        late = total_step(total_step(late, 3), 4)
    else:
        w_heads, b_heads, w_q, w_kv = own_heads(w_query, w_key, w_value, b_query)
        biases = []
        for own in owns:
            gathered = lax.all_gather(own, "samp", axis=0)
            moved = gathered.transpose(1, 2, 0, 3, 4).reshape(complexes, few, chunks, chunk, 2 * rows)
            biases.append([(moved[:, :, i], None) for i in range(chunks)])
        x_one = adapt(single_t, cond_t, *weights_one)
        x_far = swap(x_one, 2)
        blocks = [by_sample(v) for v in (x_one, swap(x_one, 1), x_far, swap(x_far, 1))]
        kept = [attend_one(k, blocks, biases[k]) for k in halves]
        atts = [by_token(v) for k in halves for v in (kept[k][0], swap(kept[k][1], 1))]
        block_out, d_mid, d_xg, da0, da1, da2, da3, s_ac, s_scale2, s_tc, s_gain2, *w_mid = middle_one(x_one, before(x_one, cond_t, cot_t, weights_two), atts)
        head_grads, sums = [], []
        for k, (own, sent) in enumerate(((da0, da1), (da2, da3))):
            dq, dkv, db = back_one(kept[k], by_sample(own), swap(by_sample(sent), 1))
            head_grads.append((dq, dkv))
            moved = db.transpose(1, 2, 0, 3, 4).reshape(complexes, few, devices, columns, 2 * rows)
            sums.append(lax.psum_scatter(moved, "samp", scatter_dimension=2, tiled=False))
        d_near, d_cross, d_far, d_own, gb, gq, gkv = heads_back(
            meta, blocks, w_q, w_kv, head_grads, parts, wch=wide, fast=fast
        )
        far_x = swap(low(d_far, swap(d_cross, 1)), 2)
        grad_single, s_scale1, s_gain1, w_last = last(
            meta, (*(u for v in (d_own, swap(d_near, 1), far_x) for u in jnp.split(flat(v), 2)), d_xg),
            single_t, cond_t, d_mid, *weights_one, fast,
        )
        pair_grads = [v[..., :rows] for v in sums] + [swap(v[..., rows:], 1) for v in sums]
        grad_pair, grad_pair_weight = pair_back(pair_meta, pair_low, pair_inverse, pair_raw, w_pair, pair_grads, **sizes)

        def total_of(stack):
            axis = stack.ndim - 1
            half = lax.psum_scatter(stack.astype(bf16), "head", scatter_dimension=axis, tiled=True).astype(f32)
            return lax.psum_scatter(half, "samp", scatter_dimension=axis - 1, tiled=True)

        grads = [
            jnp.concatenate([gq[k * wide : (k + 1) * wide], gkv[2 * k * wide : 2 * (k + 1) * wide]], axis=0) for k in halves
        ]
        held = jnp.where(part == 0, grads[0], grads[1])
        sent = jnp.where(part == 0, grads[1], grads[0])
        r_heads = add(held, swap(sent.astype(bf16), 2))
        r_heads = lax.psum_scatter(r_heads.T, "samp", scatter_dimension=0, tiled=True)
        (r_hg, r_hu), (r_out, r_gate), (r_tc, r_ac), (r_scale2, r_shift2), r_down = [total_of(v) for v in w_mid]
        r_scale1, r_shift1 = total_of(w_last)
        late = jnp.concatenate(
            [v.reshape(-1) for v in (grad_pair_weight, s_gain1, s_scale1, *q_sums(gb), s_gain2, s_ac, s_scale2, s_tc)]
        )
        late = lax.psum(late, ("samp", "head"))

    cuts = [heads * w_pair.shape[0]]
    for size in (cs, width, width, cs, width, width):
        cuts.append(cuts[-1] + size)
    sum_pair, sum_gain1, sum_scale1, sum_query, sum_gain2, sum_ac, sum_scale2, sum_tc = jnp.split(late, cuts)
    whole = (samples, rows, width)
    return (
        block_out.reshape(whole),
        grad_single.reshape(whole),
        grad_pair,
        sum_gain1,
        r_scale1,
        sum_scale1,
        r_shift1,
        r_heads[:, :wide],
        sum_query,
        r_heads[:, wide : 2 * wide],
        r_heads[:, 2 * wide :],
        r_gate,
        r_out,
        sum_pair.reshape(heads, -1).T,
        r_ac,
        sum_ac,
        sum_gain2,
        r_scale2,
        sum_scale2,
        r_shift2,
        r_hg,
        r_hu,
        r_down,
        r_tc,
        sum_tc,
    )


def solution(mesh):
    placed = (
        P("samp", "head", None),
        P("samp", "head", None),
        P(None, "head", "samp", None),
        P(),
        P("samp"),
        P("samp", "head", None),
        P(),
        P(),
        P(),
        P(),
        P(),
        P(),
        P(),
        P(),
        P(),
        P(),
        P(),
        P(),
        P(),
        P(),
        P(),
        P(),
        P(),
        P(),
        P(),
        P(),
        P(),
        P(),
    )
    return jax.shard_map(
        on_device,
        mesh=mesh,
        in_specs=placed,
        out_specs=(
            P("samp", "head", None),
            P("samp", "head", None),
            P(None, "head", "samp", None),
            P(),
            P("samp", "head"),
            P(),
            P("samp", "head"),
            P("samp", "head"),
            P(),
            P("samp", "head"),
            P("samp", "head"),
            P("samp", "head"),
            P("samp", "head"),
            P(),
            P("samp", "head"),
            P(),
            P(),
            P("samp", "head"),
            P(),
            P("samp", "head"),
            P("samp", "head"),
            P("samp", "head"),
            P("samp", "head"),
            P("samp", "head"),
            P(),
        ),
        check_vma=False,
    )
```

```python
import functools
import math

import jax
import jax.numpy as jnp
from jax import lax
from jax.experimental import pallas as pl
from jax.experimental.pallas import tpu as pltpu
from jax.sharding import PartitionSpec as P

f32, bf16 = jnp.float32, jnp.bfloat16
epsilon = 1e-05
fill_value = -1e30
LOG2E = math.log2(math.e)
VMEM_BYTES = 60 << 20
PAIR_LINES = (8, 16, 24, 32, 64, 192)
NN, NT, TN = ((1,), (0,)), ((1,), (1,)), ((0,), (0,))


LIGHT = pl.CostEstimate(flops=1 << 20, bytes_accessed=1 << 20, transcendentals=0)


def dot(a, b, dims):
    return lax.dot_general(a, b, (dims, ((), ())), preferred_element_type=f32)


def norm_rows(inputs):
    mean_val = jnp.mean(inputs, axis=-1, keepdims=True)
    centered = inputs - mean_val
    variance = jnp.mean(centered * centered, axis=-1, keepdims=True)
    inverse = lax.rsqrt(variance + epsilon)
    return (centered * inverse, inverse)


def norm_back(normed, inverse, upstream):
    mean_grad = jnp.mean(upstream, axis=-1, keepdims=True)
    mean_dot = jnp.mean(upstream * normed, axis=-1, keepdims=True)
    return inverse * (upstream - mean_grad - normed * mean_dot)


def tile_of(tokens, sizes=(8, 16, 32, 64, 128, 256)):
    return max(t for t in sizes if tokens % t == 0)


def fixed(shape):
    return pl.BlockSpec(shape, lambda *_: (0,) * len(shape), pipeline_mode=pl.Buffered(1))


META = 6


def attend_kernel(meta, x0, x1, x2, x3, w_ref, bq_ref, *rest, which, nh, hd, rows, jc, nchunk, qscale):
    bias_hbm = rest[:nchunk]
    o_ref, far_ref, p_ref, q_ref, k_ref, v_ref, l_ref, xs, ks, ss, bias_ref, sems = rest[nchunk:]
    b = pl.program_id(0)
    g = meta[0]
    cplx = meta[META + b]
    per_block = nchunk // 4

    def copies():
        return [
            pltpu.make_async_copy(
                bias_hbm[i] if which[i] is None else bias_hbm[i].at[which[i]],
                bias_ref.at[meta[META + pl.num_programs(0) + i]],
                sems.at[i],
            )
            for i in range(nchunk)
        ]

    @pl.when(b == 0)
    def _():
        for copy in copies():
            copy.start()

    for r, x in enumerate((x0, x1, x2, x3)):
        xs[r * rows : (r + 1) * rows, :] = x[0]
    wch = nh * hd
    q = dot(w_ref[0:wch, :], xs[0 : 2 * rows, :], NT) + bq_ref[...]
    q_ref[0] = (q * qscale).astype(bf16)
    kv = dot(w_ref[wch : 3 * wch, :], xs[...], NT).astype(bf16)
    k_ref[0] = kv[0:wch]
    v_ref[0] = kv[wch:]

    @pl.when(b == 0)
    def _():
        for copy in copies():
            copy.wait()

    ones = jnp.ones((16, kv.shape[1]), bf16)
    outs = []
    sums = []
    before = None
    for h in range(nh + 1):
        if h < nh:
            ks[h % 2, :, :] = jnp.transpose(k_ref[0, h * hd : (h + 1) * hd, :])
            qT = q_ref[0, h * hd : (h + 1) * hd, :]
        m = None
        for t in range(nchunk):
            part = slice(t * jc, (t + 1) * jc)
            if h < nh:
                s_idx = ((t // per_block) ^ g) * per_block + t % per_block
                s = dot(ks[h % 2, part, :], qT, NN) + bias_ref[s_idx, cplx, h].astype(f32)
                ss[h % 2, part, :] = s
                mt = jnp.max(s.reshape(jc // 8, 8, s.shape[1]), axis=0)
                m = mt if m is None else jnp.maximum(m, mt)
            if h > 0:
                p_ref[0, h - 1, part, :] = jnp.exp2(ss[(h - 1) % 2, part, :] - before).astype(bf16)
        if h < nh:
            m = jnp.max(m, axis=0, keepdims=True)
        if h > 0:
            va = jnp.concatenate([v_ref[0, (h - 1) * hd : h * hd, :], ones], axis=0)
            oT = dot(va, p_ref[0, h - 1], NN)
            l = oT[hd : hd + 1, :]
            outs.append(oT[:hd] / l)
            sums.append(l)
        before = m
    l_ref[0] = jnp.concatenate(sums, axis=0)
    o = jnp.transpose(jnp.concatenate(outs, axis=0)).astype(bf16)
    o_ref[0] = o[:rows]
    far_ref[0] = o[rows:]


def attend(meta, xb, wT, bq, biases, *, nh, hd):
    B, rows, C = xb[0].shape
    nchunk = len(biases)
    biases, which = zip(*biases)
    ncx, _, jc, qi = biases[0].shape[-4:]
    L = nchunk * jc
    wch = nh * hd
    kern = functools.partial(
        attend_kernel, which=which, nh=nh, hd=hd, rows=rows, jc=jc, nchunk=nchunk, qscale=LOG2E / math.sqrt(hd)
    )
    xspec = pl.BlockSpec((1, rows, C), lambda b, m: (b, 0, 0))
    per = lambda shape: pl.BlockSpec((1,) + shape, lambda b, m: (b,) + (0,) * len(shape))
    return pl.pallas_call(
        kern,
        grid_spec=pltpu.PrefetchScalarGridSpec(
            num_scalar_prefetch=1,
            grid=(B,),
            in_specs=[xspec] * 4
            + [fixed(wT.shape), fixed(bq.shape)]
            + [pl.BlockSpec(memory_space=pl.ANY)] * nchunk,
            out_specs=[
                per((rows, wch)),
                per((rows, wch)),
                per((nh, L, qi)),
                per((wch, qi)),
                per((wch, L)),
                per((wch, L)),
                per((nh, qi)),
            ],
            scratch_shapes=[
                pltpu.VMEM((L, C), bf16),
                pltpu.VMEM((2, L, hd), bf16),
                pltpu.VMEM((2, L, qi), f32),
                pltpu.VMEM((nchunk, ncx, nh, jc, qi), bf16),
                pltpu.SemaphoreType.DMA((nchunk,)),
            ],
        ),
        out_shape=[
            jax.ShapeDtypeStruct((B, rows, wch), bf16),
            jax.ShapeDtypeStruct((B, rows, wch), bf16),
            jax.ShapeDtypeStruct((B, nh, L, qi), bf16),
            jax.ShapeDtypeStruct((B, wch, qi), bf16),
            jax.ShapeDtypeStruct((B, wch, L), bf16),
            jax.ShapeDtypeStruct((B, wch, L), bf16),
            jax.ShapeDtypeStruct((B, nh, qi), f32),
        ],
        compiler_params=pltpu.CompilerParams(vmem_limit_bytes=VMEM_BYTES),
        cost_estimate=LIGHT,
        name="attend",
    )(meta, *xb, wT, bq, *biases)


def attend_back_kernel(
    meta, p_ref, q_ref, k_ref, v_ref, l_ref, o0, o1, do0, do1, *rest, base, nh, hd, jc, nchunk, scale, fast
):
    dq_ref, dkv_ref = rest[:2]
    vs, ds, acc = rest[-3:]
    b = pl.program_id(0)
    g = meta[0]
    cplx = meta[META + b]
    per_block = nchunk // 4
    wch = nh * hd
    L = nchunk * jc

    @pl.when(b == 0)
    def _():
        acc[...] = jnp.zeros_like(acc)

    dO = jnp.transpose(jnp.concatenate([do0[0], do1[0]], axis=0).astype(f32))
    O = jnp.transpose(jnp.concatenate([o0[0], o1[0]], axis=0).astype(f32))
    prod = dO * O
    qi = dO.shape[1]
    row = lax.broadcasted_iota(jnp.int32, (16, qi), 0)
    ones = jnp.ones((16, L), bf16)
    for h in range(nh + 1):
        if h < nh:
            hs = slice(h * hd, (h + 1) * hd)
            his = slice((base + h) * hd, (base + h + 1) * hd)
            linv = 1.0 / l_ref[0, base + h : base + h + 1, :]
            dOh = (dO[his] * linv).astype(bf16)
            delta = jnp.sum(prod[his], axis=0, keepdims=True) * linv
            hi = delta.astype(bf16).astype(f32)
            extra = jnp.where(row == 0, -hi, jnp.where(row == 1, hi - delta, 0.0)).astype(bf16)
            dOa = jnp.concatenate([dOh, extra], axis=0)
            vs[h % 2] = jnp.transpose(jnp.concatenate([v_ref[0, hs, :], ones], axis=0))
        if h > 0:
            ps = slice((h - 1) * hd, h * hd)
            dk_parts, dv_parts = [], []
            kk, qq = k_ref[0, ps, :], q_ref[0, ps, :]
        for t in range(nchunk):
            r, u = t // per_block, t % per_block
            s_idx = (r ^ g) * per_block + u
            ts = slice(t * jc, (t + 1) * jc)
            if h < nh:
                d = dot(vs[h % 2, ts, :], dOa, NN) * p_ref[0, h, ts, :].astype(f32)
                acc[s_idx, cplx, h] += d
                ds[h % 2, ts, :] = d.astype(bf16)
            if h > 0:
                dk_parts.append(dot(ds[(h - 1) % 2, ts, :], qq, NT))
                dv_parts.append(dot(p_ref[0, h - 1, ts, :], dO_before, NT))
        if h > 0:
            dq_ref[0, ps, :] = (dot(kk, ds[(h - 1) % 2], NN) * scale).astype(bf16)
            dk = jnp.transpose(jnp.concatenate(dk_parts, axis=0)) * (1.0 / LOG2E)
            dkv_ref[0, ps, :] = dk.astype(bf16)
            dv = jnp.transpose(jnp.concatenate(dv_parts, axis=0))
            dkv_ref[0, wch + (h - 1) * hd : wch + h * hd, :] = dv.astype(bf16)
        if h < nh:
            dO_before = dOh

    @pl.when(b == pl.num_programs(0) - 1)
    def _():
        if fast:
            for i in range(4):
                for e in range(2):
                    block = acc[meta[2 + i] * 2 + (meta[1] ^ e)].astype(bf16)
                    for c in range(block.shape[0]):
                        rest[2 + 2 * c + e][i] = block[c]
        else:
            rest[2][...] = acc[...].astype(bf16)


def attend_back(meta, p, q, k, v, l, o0, o1, do0, do1, nchunk, ncx, *, base, nh, hd, fast):
    B, held, L, qi = p.shape
    rows = o0.shape[1]
    jc = L // nchunk
    wch = nh * hd
    kern = functools.partial(
        attend_back_kernel, base=base, nh=nh, hd=hd, jc=jc, nchunk=nchunk, scale=1.0 / math.sqrt(hd), fast=fast
    )
    per = lambda shape: pl.BlockSpec((1,) + shape, lambda b, m: (b,) + (0,) * len(shape))
    some = lambda shape: pl.BlockSpec((1,) + shape, lambda b, m: (b, base // nh) + (0,) * (len(shape) - 1))
    db = (nchunk, ncx, nh, jc, qi)
    outs = [((4,) + db[2:], bf16)] * (2 * ncx) if fast else [(db, bf16)]
    return pl.pallas_call(
        kern,
        grid_spec=pltpu.PrefetchScalarGridSpec(
            num_scalar_prefetch=1,
            grid=(B,),
            in_specs=[some((nh, L, qi)), some((wch, qi)), some((wch, L)), some((wch, L)), per((held, qi))]
            + [per((rows, held * hd))] * 4,
            out_specs=[per((wch, qi)), per((2 * wch, L))] + [fixed(s) for s, _ in outs],
            scratch_shapes=[
                pltpu.VMEM((2, L, hd + 16), bf16),
                pltpu.VMEM((2, L, qi), bf16),
                pltpu.VMEM(db, f32),
            ],
        ),
        out_shape=[jax.ShapeDtypeStruct((B, wch, qi), bf16), jax.ShapeDtypeStruct((B, 2 * wch, L), bf16)]
        + [jax.ShapeDtypeStruct(s, d) for s, d in outs],
        compiler_params=pltpu.CompilerParams(vmem_limit_bytes=VMEM_BYTES),
        cost_estimate=LIGHT,
        name="attend_back",
    )(meta, p, q, k, v, l, o0, o1, do0, do1)


def heads_back_kernel(meta, x0, x1, x2, x3, wq_ref, wkv_ref, *rest, parts, rows, wch, fast, chained):
    n = len(parts)
    dqs, dkvs, rest = rest[:n], rest[n : 2 * n], rest[2 * n :]
    if chained:
        start_b, start_q, start_kv = rest[:3]
        rest = rest[3:]
    near_ref, cross_ref, far_ref, own_ref, gb_ref = rest[:5]
    if fast:
        keep_ref, send_ref, xs, dq, dkv, gq, gkv, gt = rest[5:]
    else:
        gq, gkv, xs, dq, dkv = rest[5:]
    b = pl.program_id(0)

    @pl.when(b == 0)
    def _():
        gq[...] = start_q[...] if chained else jnp.zeros_like(gq)
        gkv[...] = start_kv[...] if chained else jnp.zeros_like(gkv)
        gb_ref[...] = start_b[...] if chained else jnp.zeros_like(gb_ref)

    for r, x in enumerate((x0, x1, x2, x3)):
        xs[r * rows : (r + 1) * rows, :] = x[0]
    for (chunk, at, size), q, kv in zip(parts, dqs, dkvs):
        start = chunk * wch + at
        dq[start : start + size, :] = q[0]
        start = 2 * chunk * wch + at
        dkv[start : start + size, :] = kv[0, :size]
        dkv[start + wch : start + wch + size, :] = kv[0, size:]
    q, kv = dq[...], dkv[...]
    gb_ref[...] += jnp.sum(q.astype(f32), axis=1, keepdims=True)
    gq[...] += dot(q, xs[0 : 2 * rows, :], NN)
    gkv[...] += dot(kv, xs[...], NN)
    kv = jnp.transpose(kv)
    q = jnp.transpose(q)
    dx = dot(kv[2 * rows :], wkv_ref[...], NN).astype(bf16)
    far_ref[0] = dx[:rows]
    cross_ref[0] = dx[rows:]
    dx = (dot(kv[: 2 * rows], wkv_ref[...], NN) + dot(q, wq_ref[...], NN)).astype(bf16)
    own_ref[0] = dx[:rows]
    near_ref[0] = dx[rows:]

    if fast:

        @pl.when(b == pl.num_programs(0) - 1)
        def _():
            for e, ref in enumerate((keep_ref, send_ref)):
                chunk = (meta[0] // 2) ^ e
                half = pl.ds(pl.multiple_of(chunk * wch, wch), wch)
                gt[:, 0:wch] = jnp.transpose(gq[half, :])
                both = pl.ds(pl.multiple_of(chunk * 2 * wch, wch), 2 * wch)
                gt[:, wch:] = jnp.transpose(gkv[both, :])
                count = gt.shape[0] // 8
                for i in range(8):
                    ref[i] = gt[emit_rows(meta, i, count), :].astype(bf16)


def heads_back(meta, xb, wq, wkv, grads, parts, *, wch, fast, span=None, start=()):
    rows, C = xb[0].shape[1:]
    off, B = span or (0, xb[0].shape[0])
    L = 4 * rows
    total = wq.shape[0]
    row = pl.BlockSpec((1, rows, C), lambda b, m: (b, 0, 0))
    row_in = pl.BlockSpec((1, rows, C), lambda b, m: (b + off, 0, 0))
    per = lambda shape: pl.BlockSpec((1,) + shape, lambda b, m: (b + off,) + (0,) * len(shape))
    dqs, dkvs = [g[0] for g in grads], [g[1] for g in grads]
    sums = [((total, C), f32), ((2 * total, C), f32)]
    held = [pltpu.VMEM((L, C), bf16), pltpu.VMEM((total, 2 * rows), bf16), pltpu.VMEM((2 * total, L), bf16)]
    if fast:
        outs = [((8, C // 8, 3 * wch), bf16)] * 2
        held += [pltpu.VMEM(s, d) for s, d in sums] + [pltpu.VMEM((C, 3 * wch), f32)]
    else:
        outs = sums
    outs = [((total, 1), f32)] + outs
    return pl.pallas_call(
        functools.partial(heads_back_kernel, parts=parts, rows=rows, wch=wch, fast=fast, chained=bool(start)),
        grid_spec=pltpu.PrefetchScalarGridSpec(
            num_scalar_prefetch=1,
            grid=(B,),
            in_specs=[row_in] * 4
            + [fixed(wq.shape), fixed(wkv.shape)]
            + [per(v.shape[1:]) for v in dqs + dkvs]
            + [fixed(v.shape) for v in start],
            out_specs=[row] * 4 + [fixed(s) for s, _ in outs],
            scratch_shapes=held,
        ),
        out_shape=[jax.ShapeDtypeStruct((B, rows, C), bf16)] * 4 + [jax.ShapeDtypeStruct(s, d) for s, d in outs],
        compiler_params=pltpu.CompilerParams(vmem_limit_bytes=VMEM_BYTES),
        cost_estimate=LIGHT,
        name="heads_back",
    )(meta, *xb, wq, wkv, *dqs, *dkvs, *start)


def blocked(w, count):
    across, heads = w.shape
    wide = jnp.tile(jnp.transpose(w), (count, count))
    row = lax.broadcasted_iota(jnp.int32, wide.shape, 0) // heads
    column = lax.broadcasted_iota(jnp.int32, wide.shape, 1) // across
    return jnp.where(row == column, wide, jnp.zeros_like(wide))


def pair_bias_kernel(meta, lens, pair_ref, wb_ref, low_ref, inv_ref, raw_ref, *rest, few, blocks, group):
    outs, scr = rest[:-1], rest[-1]
    c, t = pl.program_id(0), pl.program_id(1)
    lines, columns, cz = pair_ref.shape[1:]
    heads = few * blocks
    per = lines // group
    mean = jnp.full((cz, cz), 1.0 / cz, bf16)
    lane = lax.broadcasted_iota(jnp.int32, (columns, group * heads), 1) // heads
    table = []
    for n in range(per):
        x = [pair_ref[0, n * group + i] for i in range(group)]
        flat = columns % 16 == 0
        if flat:
            x = [jnp.concatenate(x, axis=0)]
        lows, inverses = [], []
        for v in x:
            centered = v.astype(f32) - dot(v, mean, NN)
            inverse = lax.rsqrt(dot((centered * centered).astype(bf16), mean, NN) + epsilon)
            lows.append((centered * inverse).astype(bf16))
            inverses.append(inverse)
        if flat:
            lows = [lows[0][i * columns : (i + 1) * columns] for i in range(group)]
            inverses = [inverses[0][i * columns : (i + 1) * columns] for i in range(group)]
        spread = inverses[0][:, : group * heads]
        for i in range(1, group):
            spread = jnp.where(lane == i, inverses[i][:, : group * heads], spread)
        inv_ref[0, n] = spread
        for i in range(group):
            low_ref[0, n * group + i] = lows[i]
        table.append(jnp.concatenate(lows, axis=1))
    out = dot(jnp.concatenate(table, axis=0), wb_ref[...], NT)
    for n in range(per):
        part = out[n * columns : (n + 1) * columns]
        raw_ref[0, n] = part
        start = pl.multiple_of((t * per + n) * group * heads, group * heads)
        scr[pl.ds(start, group * heads), :] = jnp.transpose(part)

    @pl.when(t == pl.num_programs(1) - 1)
    def _():
        core = meta[0] % 2
        rows = scr.shape[0] // heads
        place = lax.broadcasted_iota(jnp.int32, (columns, rows), 0) + meta[1] * columns
        valid = place < lens[c]
        half = len(outs) // 2
        for k in range(half):
            for f in range(few):
                for e in range(2):
                    h = (2 * k + (core ^ e)) * few + f
                    v = jnp.transpose(scr[pl.ds(h, rows, stride=heads), :])
                    outs[e * half + k][0, f] = jnp.where(valid, v * LOG2E, fill_value).astype(bf16)


def pair_specs(pair, heads, group):
    lines = tile_of(pair.shape[1], PAIR_LINES)
    columns, cz = pair.shape[2:]
    return (
        lines,
        pl.BlockSpec((1, lines, columns, cz), lambda c, t, *_: (c, t, 0, 0)),
        pl.BlockSpec((1, lines // group, columns, group * heads), lambda c, t, *_: (c, t, 0, 0)),
        jax.ShapeDtypeStruct((pair.shape[0], pair.shape[1] // group, columns, group * heads), f32),
    )


def pair_bias(meta, lens, pair, wb, *, few, blocks, group):
    ncx, rows, columns, cz = pair.shape
    heads = few * blocks
    lines, spec, thin, thin_shape = pair_specs(pair, heads, group)
    out = jax.ShapeDtypeStruct((ncx, few, columns, rows), bf16)
    return pl.pallas_call(
        functools.partial(pair_bias_kernel, few=few, blocks=blocks, group=group),
        grid_spec=pltpu.PrefetchScalarGridSpec(
            num_scalar_prefetch=2,
            grid=(ncx, rows // lines),
            in_specs=[spec, fixed(wb.shape)],
            out_specs=[spec, thin, thin]
            + [pl.BlockSpec((1, few, columns, rows), lambda c, t, *_: (c, 0, 0, 0))] * blocks,
            scratch_shapes=[pltpu.VMEM((rows * heads, columns), f32)],
        ),
        out_shape=[jax.ShapeDtypeStruct(pair.shape, bf16), thin_shape, thin_shape] + [out] * blocks,
        compiler_params=pltpu.CompilerParams(vmem_limit_bytes=VMEM_BYTES),
        cost_estimate=LIGHT,
        name="pair_bias",
    )(meta, lens, pair, wb)


def pair_back_kernel(meta, low_ref, inv_ref, raw_ref, w2_ref, mean_ref, *rest, few, blocks, group):
    grads = rest[:blocks]
    out_ref, gw_ref, scr, acc = rest[blocks:]
    c, t = pl.program_id(0), pl.program_id(1)
    lines, columns, cz = low_ref.shape[1:]
    heads = few * blocks
    per = lines // group

    @pl.when((c == 0) & (t == 0))
    def _():
        acc[...] = jnp.zeros_like(acc)

    @pl.when(t == 0)
    def _():
        core = meta[0] % 2
        rows = scr.shape[0] // heads
        half = blocks // 2
        for k in range(half):
            for f in range(few):
                for e in range(2):
                    h = (2 * k + (core ^ e)) * few + f
                    scr[pl.ds(h, rows, stride=heads), :] = jnp.transpose(grads[e * half + k][0, f].astype(f32))

    ds, prods, xs = [], [], []
    for n in range(per):
        start = pl.multiple_of((t * per + n) * group * heads, group * heads)
        x = jnp.transpose(scr[pl.ds(start, group * heads), :])
        d = x * inv_ref[0, n]
        prod = d * raw_ref[0, n]
        hi = prod.astype(bf16)
        d = d.astype(bf16)
        xs.append(x.astype(bf16))
        ds.append(jnp.concatenate([d, d], axis=1))
        prods.append(jnp.concatenate([hi, (prod - hi.astype(f32)).astype(bf16)], axis=1))
    upstream = dot(jnp.concatenate(ds, axis=0), w2_ref[...], NN)
    along = dot(jnp.concatenate(prods, axis=0), mean_ref[...], NN)
    table = []
    for n in range(per):
        lows = [low_ref[0, n * group + i] for i in range(group)]
        ns = slice(n * columns, (n + 1) * columns)
        for i in range(group):
            zs = slice(i * cz, (i + 1) * cz)
            out_ref[0, n * group + i] = upstream[ns, zs] - lows[i].astype(f32) * along[ns, zs]
        table.append(jnp.concatenate(lows, axis=1))
    acc[...] += dot(jnp.concatenate(xs, axis=0), jnp.concatenate(table, axis=0), TN)

    @pl.when((c == pl.num_programs(0) - 1) & (t == pl.num_programs(1) - 1))
    def _():
        total = acc[0:heads, 0:cz]
        for i in range(1, group):
            total += acc[i * heads : (i + 1) * heads, i * cz : (i + 1) * cz]
        gw_ref[...] = total


def pair_weights(w, group):
    cz = w.shape[0]
    mean = jnp.mean(w.astype(f32), axis=0, keepdims=True)
    w2 = jnp.concatenate([blocked(w, group), blocked(jnp.broadcast_to(-mean, w.shape).astype(bf16), group)], axis=0)
    ones = blocked(jnp.full(w.shape, 1.0 / cz, bf16), group)
    return w2, jnp.concatenate([ones, ones], axis=0)


def pair_back(meta, low, inv, raw, weights, grads, *, few, blocks, group):
    ncx, rows, columns, cz = low.shape
    heads = few * blocks
    lines, spec, thin, _ = pair_specs(low, heads, group)
    w2, ones = weights
    return pl.pallas_call(
        functools.partial(pair_back_kernel, few=few, blocks=blocks, group=group),
        grid_spec=pltpu.PrefetchScalarGridSpec(
            num_scalar_prefetch=1,
            grid=(ncx, rows // lines),
            in_specs=[spec, thin, thin, fixed(w2.shape), fixed(ones.shape)]
            + [pl.BlockSpec((1, few, columns, rows), lambda c, t, *_: (c, 0, 0, 0))] * blocks,
            out_specs=[spec, fixed((heads, cz))],
            scratch_shapes=[pltpu.VMEM((rows * heads, columns), f32), pltpu.VMEM((group * heads, group * cz), f32)],
        ),
        out_shape=[jax.ShapeDtypeStruct(low.shape, f32), jax.ShapeDtypeStruct((heads, cz), f32)],
        compiler_params=pltpu.CompilerParams(vmem_limit_bytes=VMEM_BYTES),
        cost_estimate=LIGHT,
        name="pair_back",
    )(meta, low, inv, raw, w2, ones, *grads)


def column_sum(v):
    return jnp.sum(v, axis=0, keepdims=True)


def tiled(rows, width, steps):
    return pl.BlockSpec((rows, width), lambda t, *_: (jnp.minimum(t, steps - 1), 0))


def adapt_kernel(single_ref, cond_ref, gain, w_scale, b_scale, w_shift, x_ref):
    normed, _ = norm_rows(single_ref[...].astype(f32))
    cond_hat, _ = norm_rows(cond_ref[...].astype(f32))
    cond_low = (cond_hat * gain[...].astype(f32)).astype(bf16)
    gate = jax.nn.sigmoid(dot(cond_low, w_scale[...], NN) + b_scale[...].astype(f32))
    x_ref[...] = (gate * normed + dot(cond_low, w_shift[...], NN)).astype(bf16)


def adapt(single, cond, gain, w_scale, b_scale, w_shift):
    tokens, width = single.shape
    tile = tile_of(tokens)
    steps = tokens // tile
    return pl.pallas_call(
        adapt_kernel,
        grid=(steps,),
        in_specs=[tiled(tile, width, steps), tiled(tile, cond.shape[1], steps)]
        + [fixed(v.shape) for v in (gain, w_scale, b_scale, w_shift)],
        out_specs=tiled(tile, width, steps),
        out_shape=jax.ShapeDtypeStruct((tokens, width), bf16),
        compiler_params=pltpu.CompilerParams(vmem_limit_bytes=VMEM_BYTES),
        cost_estimate=LIGHT,
        name="adapt",
    )(single, cond, gain, w_scale, b_scale, w_shift)


def emit_rows(meta, step, count):
    place = meta[2 + step % 4] * 2 + (meta[1] ^ (step // 4))
    return pl.ds(pl.multiple_of(place * count, count), count)


def before_kernel(
    x_ref, cond_ref, cot_ref, w_gate, w_ac, b_ac, gain, w_scale, b_scale, w_shift, w_dn, w_tc, b_tc,
    gate_ref, acond_ref, tcond_ref, scale_ref, shift_ref, dh_ref,
):
    cond = cond_ref[...]
    tcond = jax.nn.sigmoid(dot(cond, w_tc[...], NN) + b_tc[...].astype(f32))
    tcond_ref[...] = tcond.astype(tcond_ref.dtype)
    d_tr = (tcond * cot_ref[...].astype(f32)).astype(bf16)
    dh_ref[...] = dot(d_tr, w_dn[...], NT).astype(dh_ref.dtype)
    acond_ref[...] = jax.nn.sigmoid(dot(cond, w_ac[...], NN) + b_ac[...].astype(f32)).astype(acond_ref.dtype)
    cond_hat, _ = norm_rows(cond.astype(f32))
    cond_low = (cond_hat * gain[...].astype(f32)).astype(bf16)
    scale = jax.nn.sigmoid(dot(cond_low, w_scale[...], NN) + b_scale[...].astype(f32))
    scale_ref[...] = scale.astype(scale_ref.dtype)
    shift_ref[...] = dot(cond_low, w_shift[...], NN).astype(shift_ref.dtype)
    gate_ref[...] = jax.nn.sigmoid(dot(x_ref[...], w_gate[...], NN)).astype(gate_ref.dtype)


def before(x_one, cond, cot, weights):
    w_gate, w_out, w_ac, b_ac, gain, w_scale, b_scale, w_shift, w_hg, w_hu, w_dn, w_tc, b_tc = weights
    used = (w_gate, w_ac, b_ac, gain, w_scale, b_scale, w_shift, w_dn, w_tc, b_tc)
    tokens, width = x_one.shape
    tile = tile_of(tokens)
    steps = tokens // tile
    outs = [(width, f32)] * 4 + [(width, bf16), (w_dn.shape[0], bf16)]
    return pl.pallas_call(
        before_kernel,
        grid=(steps,),
        in_specs=[tiled(tile, w, steps) for w in (width, cond.shape[1], width)] + [fixed(w.shape) for w in used],
        out_specs=[tiled(tile, w, steps) for w, _ in outs],
        out_shape=[jax.ShapeDtypeStruct((tokens, w), d) for w, d in outs],
        compiler_params=pltpu.CompilerParams(vmem_limit_bytes=VMEM_BYTES),
        cost_estimate=LIGHT,
        name="before",
    )(x_one, cond, cot, *used)


def middle_kernel(
    meta, x_ref, single_ref, cond_ref, cot_ref, gate_ref, acond_ref, tcond_ref, scale_ref, shift_ref, dh_ref,
    a0, a1, a2, a3, w_gate, w_out, gain, w_scale, w_shift, w_hg, w_hu, w_dn,
    out_ref, dmid_ref, dxg_ref, da0, da1, da2, da3, s_ac, s_scale, s_tc, s_gain, *rest, tiles, fast,
):
    core = meta[0] % 2
    step = pl.program_id(0)
    if fast:
        out_w, g_hidden, g_square, g_cond, g_norm, g_dn = rest
    else:
        g_hidden, g_square, g_cond, g_norm, g_dn = rest

    @pl.when(step == 0)
    def _():
        for ref in (g_hidden, g_square, g_cond, g_norm, g_dn, s_ac, s_scale, s_tc, s_gain):
            ref[...] = jnp.zeros_like(ref)

    @pl.when(step < tiles)
    def _():
        cond = cond_ref[...]
        first = core == 0

        def attended():
            return jnp.concatenate(
                [
                    jnp.where(first, a0[...], a1[...]),
                    jnp.where(first, a1[...], a0[...]),
                    jnp.where(first, a2[...], a3[...]),
                    jnp.where(first, a3[...], a2[...]),
                ],
                axis=1,
            ).astype(f32)

        gated = (attended() * gate_ref[...]).astype(bf16)
        branch = dot(gated, w_out[...], NN)
        mid = single_ref[...].astype(f32) + acond_ref[...] * branch
        normed, inverse = norm_rows(mid)
        x_two = (scale_ref[...] * normed + shift_ref[...].astype(f32)).astype(bf16)
        hgate = dot(x_two, w_hg[...], NN)
        hup = dot(x_two, w_hu[...], NN)
        sig = jax.nn.sigmoid(hgate)
        silu = hgate * sig
        hidden = (silu * hup).astype(bf16)
        d_hidden = dh_ref[...].astype(f32)
        d_hg = (d_hidden * hup * sig * (1.0 + hgate * (1.0 - sig))).astype(bf16)
        d_hu = (d_hidden * silu).astype(bf16)
        tcond = tcond_ref[...]
        dy = cot_ref[...].astype(f32)
        tr_branch = dot(hidden, w_dn[...], NN)
        out_ref[...] = (mid + tcond * tr_branch).astype(bf16)
        d_trc = dy * tr_branch * tcond * (1.0 - tcond)
        s_tc[...] += column_sum(d_trc)
        g_cond[0] += dot(cond, d_trc.astype(bf16), TN)
        g_dn[...] += dot(hidden, (tcond * dy).astype(bf16), TN)
        g_hidden[0] += dot(x_two, d_hg, TN)
        g_hidden[1] += dot(x_two, d_hu, TN)
        g_two = dot(d_hg, w_hg[...], NT) + dot(d_hu, w_hu[...], NT)
        scale = scale_ref[...]
        cond_hat, _ = norm_rows(cond.astype(f32))
        cond_low = (cond_hat * gain[...].astype(f32)).astype(bf16)
        d_scale = g_two * normed * scale * (1.0 - scale)
        s_scale[...] += column_sum(d_scale)
        d_scale = d_scale.astype(bf16)
        d_shift = g_two.astype(bf16)
        g_norm[0] += dot(cond_low, d_scale, TN)
        g_norm[1] += dot(cond_low, d_shift, TN)
        d_cond = dot(d_scale, w_scale[...], NT) + dot(d_shift, w_shift[...], NT)
        s_gain[...] += column_sum(d_cond * cond_hat)
        d_mid = dy + norm_back(normed, inverse, g_two * scale)
        dmid_ref[...] = d_mid
        acond = acond_ref[...]
        d_attn = (acond * d_mid).astype(bf16)
        d_ac = d_mid * branch * acond * (1.0 - acond)
        s_ac[...] += column_sum(d_ac)
        g_cond[1] += dot(cond, d_ac.astype(bf16), TN)
        g_square[0] += dot(gated, d_attn, TN)
        d_gated = dot(d_attn, w_out[...], NT)
        gate = gate_ref[...]
        d_att = (d_gated * gate).astype(bf16)
        d_gate = (d_gated * attended() * gate * (1.0 - gate)).astype(bf16)
        g_square[1] += dot(x_ref[...], d_gate, TN)
        dxg_ref[...] = dot(d_gate, w_gate[...], NT).astype(bf16)
        q = d_att.shape[1] // 4
        parts = [d_att[:, i * q : (i + 1) * q] for i in range(4)]
        da0[...] = jnp.where(first, parts[0], parts[1])
        da1[...] = jnp.where(first, parts[1], parts[0])
        da2[...] = jnp.where(first, parts[2], parts[3])
        da3[...] = jnp.where(first, parts[3], parts[2])

    if fast:

        @pl.when(step >= tiles)
        def _():
            emit = step - tiles
            place = meta[2 + emit % 4] * 2 + (meta[1] ^ (emit // 4))
            for g in range(4):
                at = 0
                for one, two, count in (
                    (g_hidden.at[0], None, 8),
                    (g_hidden.at[1], None, 8),
                    (g_square.at[0], g_square.at[1], 8),
                    (g_cond.at[0], g_cond.at[1], 8),
                    (g_norm.at[0], g_norm.at[1], 8),
                    (g_dn, g_dn, 16),
                ):
                    n, lanes = one.shape[0] // count, one.shape[1] // 4
                    take = lambda ref, row: ref[pl.ds(pl.multiple_of(row, n), n), g * lanes : (g + 1) * lanes]
                    if two is None:
                        part = take(one, place * n)
                    elif one is two:
                        part = jnp.concatenate([take(one, 2 * place * n), take(one, (2 * place + 1) * n)], axis=1)
                    else:
                        part = jnp.concatenate([take(one, place * n), take(two, place * n)], axis=1)
                    out_w[g, 0, at : at + n, :] = part.astype(bf16)
                    at += n


def middle(meta, x_one, single, cond, cot, gates, atts, weights, fast):
    tokens, width = single.shape
    tile = tile_of(tokens)
    tiles = tokens // tile
    cs = cond.shape[1]
    quarter = atts[0].shape[1]
    w_gate, w_out, w_ac, b_ac, gain, w_scale, b_scale, w_shift, w_hg, w_hu, w_dn, w_tc, b_tc = weights
    fold = lambda n: jax.ShapeDtypeStruct((1, n), f32)
    sums = [fold(width), fold(width), fold(width), fold(cs)]
    grads = [(2,) + w_hg.shape, (2,) + w_out.shape, (2,) + w_ac.shape, (2,) + w_scale.shape, w_dn.shape]
    row_out = [(width, bf16), (width, f32), (width, bf16)] + [(quarter, bf16)] * 4
    used = (w_gate, w_out, gain, w_scale, w_shift, w_hg, w_hu, w_dn)
    if fast:
        lanes = width // 2
        rows = sum(w.size for w in weights if w.shape[0] > 1) // (8 * 4 * lanes)
        more_specs = [pl.BlockSpec((4, 1, rows, lanes), lambda t, *_: (0, jnp.maximum(t - tiles, 0), 0, 0))]
        more = [jax.ShapeDtypeStruct((4, 8, rows, lanes), bf16)]
        scratch = [pltpu.VMEM(g, f32) for g in grads]
    else:
        more_specs = [fixed(g) for g in grads]
        more = [jax.ShapeDtypeStruct(g, f32) for g in grads]
        scratch = []
    return pl.pallas_call(
        functools.partial(middle_kernel, tiles=tiles, fast=fast),
        grid_spec=pltpu.PrefetchScalarGridSpec(
            num_scalar_prefetch=1,
            grid=(tiles + 8 * fast,),
            in_specs=[tiled(tile, w, tiles) for w in (width, width, cs, width)]
            + [tiled(tile, v.shape[1], tiles) for v in gates]
            + [tiled(tile, quarter, tiles)] * 4
            + [fixed(w.shape) for w in used],
            out_specs=[tiled(tile, w, tiles) for w, _ in row_out] + [fixed(g.shape) for g in sums] + more_specs,
            scratch_shapes=scratch,
        ),
        out_shape=[jax.ShapeDtypeStruct((tokens, w), d) for w, d in row_out] + sums + more,
        compiler_params=pltpu.CompilerParams(vmem_limit_bytes=VMEM_BYTES),
        cost_estimate=LIGHT,
        name="middle",
    )(meta, x_one, single, cond, cot, *gates, *atts, *used)


def last_kernel(
    meta, d0, d1, d2, d3, d4, d5, d6, single_ref, cond_ref, dmid_ref, gain, w_scale, b_scale, w_shift,
    out_ref, s_scale, s_gain, *rest, fast,
):
    if fast:
        keep_ref, send_ref, g_norm = rest
    else:
        (g_norm,) = rest

    @pl.when(pl.program_id(0) == 0)
    def _():
        for ref in (g_norm, s_scale, s_gain):
            ref[...] = jnp.zeros_like(ref)

    late_half = pl.program_id(0) >= pl.num_programs(0) // 2
    g_one = d6[...].astype(f32)
    for one, two in ((d0, d1), (d2, d3), (d4, d5)):
        g_one += jnp.where(late_half, two[...], one[...]).astype(f32)
    normed, inverse = norm_rows(single_ref[...].astype(f32))
    cond_hat, _ = norm_rows(cond_ref[...].astype(f32))
    cond_low = (cond_hat * gain[...].astype(f32)).astype(bf16)
    scale = jax.nn.sigmoid(dot(cond_low, w_scale[...], NN) + b_scale[...].astype(f32))
    d_scale = g_one * normed * scale * (1.0 - scale)
    s_scale[...] += column_sum(d_scale)
    d_scale = d_scale.astype(bf16)
    d_shift = g_one.astype(bf16)
    g_norm[0] += dot(cond_low, d_scale, TN)
    g_norm[1] += dot(cond_low, d_shift, TN)
    d_cond = dot(d_scale, w_scale[...], NT) + dot(d_shift, w_shift[...], NT)
    s_gain[...] += column_sum(d_cond * cond_hat)
    out_ref[...] = dmid_ref[...] + norm_back(normed, inverse, g_one * scale)

    if fast:

        @pl.when(pl.program_id(0) == pl.num_programs(0) - 1)
        def _():
            n, wide = g_norm.shape[1] // 8, g_norm.shape[2] // 2
            for e, ref in enumerate((keep_ref, send_ref)):
                for p in range(2):
                    lanes = pl.ds(pl.multiple_of(((meta[0] // 2) ^ p) * wide, wide), wide)
                    for i in range(8):
                        ref[p, i] = g_norm[(meta[0] % 2) ^ e, emit_rows(meta, i, n), lanes].astype(bf16)


def last(meta, ds, single, cond, dmid, gain, w_scale, b_scale, w_shift, fast):
    tokens, width = single.shape
    tile = tile_of(tokens)
    steps = tokens // tile
    cs = cond.shape[1]
    grads = (2,) + w_scale.shape
    if fast:
        more = [jax.ShapeDtypeStruct((2, 8, cs // 8, width // 2), bf16)] * 2
        scratch = [pltpu.VMEM(grads, f32)]
    else:
        more = [jax.ShapeDtypeStruct(grads, f32)]
        scratch = []
    more = [jax.ShapeDtypeStruct((1, width), f32), jax.ShapeDtypeStruct((1, cs), f32)] + more
    row = tiled(tile, width, steps)
    half = steps // 2
    early_row = pl.BlockSpec((tile, width), lambda t, *_: (jnp.minimum(t, half - 1), 0))
    late_row = pl.BlockSpec((tile, width), lambda t, *_: (jnp.maximum(t - half, 0), 0))
    return pl.pallas_call(
        functools.partial(last_kernel, fast=fast),
        grid_spec=pltpu.PrefetchScalarGridSpec(
            num_scalar_prefetch=1,
            grid=(steps,),
            in_specs=[early_row, late_row] * 3
            + [row, row]
            + [tiled(tile, cs, steps), row]
            + [fixed(w.shape) for w in (gain, w_scale, b_scale, w_shift)],
            out_specs=[row] + [fixed(g.shape) for g in more],
            scratch_shapes=scratch,
        ),
        out_shape=[jax.ShapeDtypeStruct((tokens, width), f32)] + more,
        compiler_params=pltpu.CompilerParams(vmem_limit_bytes=VMEM_BYTES),
        cost_estimate=LIGHT,
        name="last",
    )(meta, *ds, single, cond, dmid, gain, w_scale, b_scale, w_shift)


def swap(value, bit):
    return lax.ppermute(value, "head", [(i, i ^ bit) for i in range(lax.axis_size("head"))])


def across(value):
    return lax.ppermute(value, "samp", [(i, i ^ 1) for i in range(8)])


def slot(value, bit):
    return lax.ppermute(value, "samp", [(i, i ^ (2 * bit)) for i in range(8)])


def add(*terms):
    total = terms[0].astype(f32)
    for term in terms[1:]:
        total = total + term.astype(f32)
    return total


def tie(value, *others):
    return lax.optimization_barrier((value,) + others)[0]


def low(*terms):
    return add(*terms).astype(bf16)


Z_ORDER = (0, 2, 1, 3)


def x_step(block):
    return block[:4], across(block[4:])


def z_first(keep, got):
    return slot(low(keep[2:], got[2:]), 1)


def z_second(keep, got, z_got):
    return slot(low(keep[1], got[1], z_got[1]), 2)


def z_total(keep, got, z_got, last_got):
    return add(keep[0], got[0], z_got[0], last_got)


def fence(*values):
    return lax.optimization_barrier(values)


def total_step(vector, step):
    if step < 2:
        return vector + swap(vector, 1 << step)
    if step == 2:
        return vector + across(vector)
    return vector + slot(vector, step - 2)


def pack_w(w_heads, wide):
    return (
        jnp.concatenate([w[:wide] for w in w_heads], axis=0),
        jnp.concatenate([w[wide:] for w in w_heads], axis=0),
    )


def on_device(
    single,
    cond,
    pair,
    complex_length,
    sample_complex,
    cotangent,
    gain_one,
    w_scale_one,
    b_scale_one,
    w_shift_one,
    w_query,
    b_query,
    w_key,
    w_value,
    w_gate,
    w_out,
    w_pair,
    w_attn_cond,
    b_attn_cond,
    gain_two,
    w_scale_two,
    b_scale_two,
    w_shift_two,
    w_hidden_gate,
    w_hidden_up,
    w_hidden_down,
    w_tr_cond,
    b_tr_cond,
):
    groups = lax.axis_size("head")
    devices = lax.axis_size("samp")
    me = lax.axis_index("head")
    place = lax.axis_index("samp")
    core = me % 2
    part = me // 2
    samples, rows, width = single.shape
    cs = cond.shape[2]
    tokens = samples * rows
    length = rows * groups
    heads = w_pair.shape[1]
    few = heads // groups
    dim = width // heads
    wide = few * dim
    complexes, _, columns, _ = pair.shape
    chunks = 2 * groups
    chunk = length // chunks
    halves = range(groups // 2)
    fast = devices == 8 and groups == 4 and columns == chunk
    line = lambda v: v.reshape(1, -1)
    flat = lambda v: v.reshape(tokens, width)
    first = core == 0

    if fast:
        z, x = place // 2, place % 2
        order = z ^ jnp.array(Z_ORDER, jnp.int32)
        slots = jnp.stack([order * 2 + x, order * 2 + 1 - x], axis=1).reshape(8)
    else:
        x = jnp.zeros((), jnp.int32)
        order, slots = jnp.zeros((4,), jnp.int32), jnp.arange(chunks, dtype=jnp.int32)
    meta = jnp.concatenate([jnp.stack([me, x]).astype(jnp.int32), order, sample_complex, slots])
    pair_meta = jnp.stack([me, place]).astype(jnp.int32)
    group = 8
    sizes = dict(few=few, blocks=groups, group=group)
    single_t, cond_t, cot_t = flat(single), cond.reshape(tokens, cs), flat(cotangent)
    weights_one = (line(gain_one), w_scale_one, line(b_scale_one), w_shift_one)
    weights_two = (
        w_gate, w_out, w_attn_cond, line(b_attn_cond), line(gain_two), w_scale_two, line(b_scale_two), w_shift_two,
        w_hidden_gate, w_hidden_up, w_hidden_down, w_tr_cond, line(b_tr_cond),
    )

    def own_heads(*weights):
        columns_of = lambda w, k: lax.dynamic_slice_in_dim(w, (2 * k + core) * wide, wide, w.ndim - 1)
        w_heads = [jnp.concatenate([columns_of(w, k).T for w in weights[:3]], axis=0) for k in halves]
        b_heads = [columns_of(weights[3].astype(f32), k)[:, None] for k in halves]
        return w_heads, b_heads, *pack_w(w_heads, wide)

    parts = [(k, 0, wide) for k in halves]
    by_sample = lambda v: v.reshape(samples, rows, -1)
    by_token = lambda v: v.reshape(-1, v.shape[-1])
    attend_one = lambda k, blocks, biases: attend(meta, blocks, w_heads[k], b_heads[k], biases, nh=few, hd=dim)
    middle_one = lambda x_one, gates, atts: middle(meta, x_one, single_t, cond_t, cot_t, gates, atts, weights_two, fast)
    back_one = lambda kept, own, near: attend_back(
        meta, *kept[2:], *kept[:2], own, near, chunks, complexes, base=0, nh=few, hd=dim, fast=fast
    )

    def q_sums(gb):
        zero = jnp.zeros((wide,), f32)
        out = []
        for k in halves:
            mine = gb[k * wide : (k + 1) * wide].reshape(-1)
            out += [jnp.where(first, mine, zero), jnp.where(first, zero, mine)]
        return out

    w_blocked = blocked(w_pair, group)
    pair_low, pair_inverse, pair_raw, *bias = pair_bias(pair_meta, complex_length, pair, w_blocked, **sizes)
    near_bias = [swap(v, 1) for v in bias[groups // 2 :]]
    owns = [jnp.concatenate([bias[k], near_bias[k]], axis=-1) for k in halves]

    if fast:
        both_owns = jnp.stack(owns)
        owns, both_owns, single_t = fence(owns, both_owns, single_t)
        far_0, z_0, x_own = slot(owns[0], 2), [slot(owns[0], 1)], across(both_owns)
        x_one = adapt(single_t, cond_t, *weights_one)
        far_0, z_0, x_own, x_one, owns = fence(far_0, z_0, x_own, x_one, owns)
        x_far = swap(x_one, 2)
        far_1 = slot(owns[1], 2)
        z_0.append(slot(far_0, 1))
        x_0 = [across(far_0), across(z_0[0])]
        far_1, z_0, x_0, owns, x_mid, qkv = fence(far_1, z_0, x_0, owns, x_one, (w_query, w_key, w_value, b_query))
        w_heads, b_heads, w_q, w_kv = own_heads(*qkv)
        x_0.append(across(z_0[1]))
        x_1 = [across(far_1)]
        z_1 = [slot(owns[1], 1), slot(far_1, 1)]
        gates = before(x_mid, cond_t, cot_t, weights_two)
        x_far, x_0, x_1, z_1, gates, x_mid, w_heads, b_heads, w_q, w_kv = fence(
            x_far, x_0, x_1, z_1, gates, x_mid, w_heads, b_heads, w_q, w_kv
        )
        x_cross, x_near = swap(x_far, 1), swap(x_mid, 1)
        x_1 += [across(v) for v in z_1]
        blocks = [by_sample(v) for v in (x_one, x_near, x_far, x_cross)]
        pairs_of = lambda k, here, there: [
            pair_of for v, w in zip(here, [(x_own, k)] + [(u, None) for u in there]) for pair_of in ((v, None), w)
        ]
        kept = [attend_one(0, blocks, pairs_of(0, [owns[0], far_0] + z_0, x_0))]
        kept, x_1 = fence(kept, x_1)
        near_atts = [swap(kept[0][1], 1)]
        kept.append(attend_one(1, blocks, pairs_of(1, [owns[1], far_1] + z_1, x_1)))
        kept, near_atts = fence(kept, near_atts)
        near_atts.append(swap(kept[1][1], 1))
        atts = [by_token(v) for k in halves for v in (kept[k][0], near_atts[k])]

        block_out, d_mid, d_xg, da0, da1, da2, da3, s_ac, s_scale2, s_tc, s_gain2, w_mid = middle_one(x_one, gates, atts)
        near_att = [swap(by_sample(v), 1) for v in (da1, da3)]
        w_two = pair_weights(tie(w_pair, da1), group)
        near_att, w_mid, w_two = fence(near_att, w_mid, w_two)
        mid = lax.psum_scatter(w_mid, "head", scatter_dimension=0, tiled=False)

        dq_0, dkv_0, *db_0 = back_one(kept[0], by_sample(da0), near_att[0])
        db_0, kept_1 = fence(db_0, kept[1])
        keep_a, got_a, keep_b, got_b = db_0[0], across(db_0[1]), db_0[2], across(db_0[3])
        dq_1, dkv_1, *db_1 = back_one(kept_1, by_sample(da2), near_att[1])
        dq_1, db_1, got_a = fence(dq_1, db_1, got_a)
        keep_c, got_c, keep_d = db_1[0], across(db_1[1]), db_1[2]
        zs_a = z_first(keep_a, got_a)
        cut = samples // 2
        back_heads = lambda grads, span, start, full: heads_back(
            meta, blocks, w_q, w_kv, grads, parts, wch=wide, fast=full, span=span, start=start
        )
        near_1, cross_1, far_1, own_1, *start = back_heads([(dq_0, dkv_0), (dq_1, dkv_1)], (0, cut), (), False)
        near_1, cross_1, far_1, start, zs_a, dq_1 = fence(near_1, cross_1, far_1, start, zs_a, dq_1)
        cross_1 = swap(cross_1, 1)
        cross_1, dq_1, got_b = fence(cross_1, dq_1, got_b)
        half_1 = low(far_1, cross_1)
        half_1, dq_1 = fence(half_1, dq_1)
        far_x, near_x = [swap(half_1, 2)], [swap(near_1, 1)]
        zs_b, last_a = z_first(keep_b, got_b), z_second(keep_a, got_a, zs_a)
        near_2, cross_2, far_2, own_2, gb, keep_w, send_w = back_heads(
            [(dq_0, dkv_0), (dq_1, dkv_1)], (cut, samples - cut), start, True
        )
        near_2, cross_2, far_2, send_w, send_d, last_a, zs_b, far_x[0] = fence(
            near_2, cross_2, far_2, send_w, db_1[3], last_a, zs_b, far_x[0]
        )
        cross_2, got_d = swap(cross_2, 1), across(send_d)
        cross_2, got_c = fence(cross_2, got_c)
        far_x.append(swap(low(far_2, cross_2), 2))
        zs_c, last_b = z_first(keep_c, got_c), z_second(keep_b, got_b, zs_b)
        far_x[1], got_d, zs_c, last_b, send_w, mid, near_2 = fence(far_x[1], got_d, zs_c, last_b, send_w, mid, near_2)
        zs_d, last_c = z_first(keep_d, got_d), z_second(keep_c, got_c, zs_c)
        keep_m, got_m = x_step(mid)
        far_w = swap(send_w, 2)
        sums = [low(z_total(keep_a, got_a, zs_a, last_a)), low(z_total(keep_b, got_b, zs_b, last_b))]
        zs_d, last_c, sums, near_2 = fence(zs_d, last_c, sums, near_2)
        near_x.append(swap(near_2, 1))
        sums.append(low(z_total(keep_c, got_c, zs_c, last_c)))
        last_d = z_second(keep_d, got_d, zs_d)
        near_x, sums = fence(near_x, sums)
        grad_single, s_scale1, s_gain1, keep_l, send_l = last(
            meta, (*map(by_token, (own_1, own_2, *near_x, *far_x)), d_xg), single_t, cond_t, d_mid, *weights_one, fast
        )
        last_d, got_m, far_w, keep_l, send_l, s_gain1, s_scale1 = fence(
            last_d, got_m, far_w, keep_l, send_l, s_gain1, s_scale1
        )
        sums.append(low(z_total(keep_d, got_d, zs_d, last_d)))
        far_rows = swap(jnp.stack([v[..., rows:] for v in sums]), 1)
        near_l = swap(send_l, 1)
        z_m = z_first(keep_m, got_m)
        keep_h, got_h = x_step(low(keep_w, far_w))
        others = jnp.concatenate(
            [v.reshape(-1) for v in (s_gain1, s_scale1, *q_sums(gb), s_gain2, s_ac, s_scale2, s_tc)]
        )
        far_rows, near_l, others = fence(far_rows, near_l, others)
        far_l = swap(low(keep_l[1], near_l[1]), 2)
        pair_grads = [jnp.stack([v[..., :rows] for v in sums[2 * k : 2 * k + 2]]) for k in halves]
        pair_grads += [far_rows[:2], far_rows[2:]]
        grad_pair, grad_pair_weight = pair_back(pair_meta, pair_low, pair_inverse, pair_raw, w_two, pair_grads, **sizes)
        far_l, got_h, z_m, grad_pair_weight = fence(far_l, got_h, z_m, grad_pair_weight)
        late = total_step(jnp.concatenate([grad_pair_weight.reshape(-1), others]), 0)
        keep_l, got_l = x_step(low(keep_l[0], near_l[0], far_l))
        e_m = z_second(keep_m, got_m, z_m)
        z_h = z_first(keep_h, got_h)
        late, got_l = fence(late, got_l)

        def settle(block):
            size = block.shape[1] // 2
            left, right = block[:, :size], block[:, size:]
            got = swap(jnp.where(first, right, left), 1)
            held = jnp.where(first, left, right)
            return jnp.where(first, held, got), jnp.where(first, got, held)

        late = total_step(late, 1)
        z_l = z_first(keep_l, got_l)
        late, z_l, z_h, e_m = fence(late, z_l, z_h, e_m)
        late = total_step(late, 2)
        e_l = z_second(keep_l, got_l, z_l)
        e_h = z_second(keep_h, got_h, z_h)
        late, e_l, e_h = fence(late, e_l, e_h)
        r_scale1, r_shift1 = settle(z_total(keep_l, got_l, z_l, e_l))
        r_heads = z_total(keep_h, got_h, z_h, e_h)
        n, m, half = width // 8, cs // 8, width // 4
        r_mid = z_total(keep_m, got_m, z_m, e_m)
        r_hg, r_hu = r_mid[:n], r_mid[n : 2 * n]
        r_out, r_gate = r_mid[2 * n : 3 * n, :half], r_mid[2 * n : 3 * n, half:]
        r_tc, r_ac = r_mid[3 * n : 3 * n + m, :half], r_mid[3 * n : 3 * n + m, half:]
        r_scale2, r_shift2 = r_mid[3 * n + m : 3 * n + 2 * m, :half], r_mid[3 * n + m : 3 * n + 2 * m, half:]
        r_down = jnp.concatenate([r_mid[3 * n + 2 * m :, :half], r_mid[3 * n + 2 * m :, half:]], axis=0)
        late = total_step(total_step(late, 3), 4)
    else:
        w_heads, b_heads, w_q, w_kv = own_heads(w_query, w_key, w_value, b_query)
        w_two = pair_weights(w_pair, group)
        biases = []
        for own in owns:
            gathered = lax.all_gather(own, "samp", axis=0)
            moved = gathered.transpose(1, 2, 0, 3, 4).reshape(complexes, few, chunks, chunk, 2 * rows)
            biases.append([(moved[:, :, i], None) for i in range(chunks)])
        x_one = adapt(single_t, cond_t, *weights_one)
        x_far = swap(x_one, 2)
        blocks = [by_sample(v) for v in (x_one, swap(x_one, 1), x_far, swap(x_far, 1))]
        kept = [attend_one(k, blocks, biases[k]) for k in halves]
        atts = [by_token(v) for k in halves for v in (kept[k][0], swap(kept[k][1], 1))]
        block_out, d_mid, d_xg, da0, da1, da2, da3, s_ac, s_scale2, s_tc, s_gain2, *w_mid = middle_one(x_one, before(x_one, cond_t, cot_t, weights_two), atts)
        head_grads, sums = [], []
        for k, (own, sent) in enumerate(((da0, da1), (da2, da3))):
            dq, dkv, db = back_one(kept[k], by_sample(own), swap(by_sample(sent), 1))
            head_grads.append((dq, dkv))
            moved = db.transpose(1, 2, 0, 3, 4).reshape(complexes, few, devices, columns, 2 * rows)
            sums.append(lax.psum_scatter(moved, "samp", scatter_dimension=2, tiled=False))
        d_near, d_cross, d_far, d_own, gb, gq, gkv = heads_back(
            meta, blocks, w_q, w_kv, head_grads, parts, wch=wide, fast=fast
        )
        far_x = swap(low(d_far, swap(d_cross, 1)), 2)
        grad_single, s_scale1, s_gain1, w_last = last(
            meta, (*(u for v in (d_own, swap(d_near, 1), far_x) for u in jnp.split(flat(v), 2)), d_xg),
            single_t, cond_t, d_mid, *weights_one, fast,
        )
        pair_grads = [v[..., :rows] for v in sums] + [swap(v[..., rows:], 1) for v in sums]
        grad_pair, grad_pair_weight = pair_back(pair_meta, pair_low, pair_inverse, pair_raw, w_two, pair_grads, **sizes)

        def total_of(stack):
            axis = stack.ndim - 1
            half = lax.psum_scatter(stack.astype(bf16), "head", scatter_dimension=axis, tiled=True).astype(f32)
            return lax.psum_scatter(half, "samp", scatter_dimension=axis - 1, tiled=True)

        grads = [
            jnp.concatenate([gq[k * wide : (k + 1) * wide], gkv[2 * k * wide : 2 * (k + 1) * wide]], axis=0) for k in halves
        ]
        held = jnp.where(part == 0, grads[0], grads[1])
        sent = jnp.where(part == 0, grads[1], grads[0])
        r_heads = add(held, swap(sent.astype(bf16), 2))
        r_heads = lax.psum_scatter(r_heads.T, "samp", scatter_dimension=0, tiled=True)
        (r_hg, r_hu), (r_out, r_gate), (r_tc, r_ac), (r_scale2, r_shift2), r_down = [total_of(v) for v in w_mid]
        r_scale1, r_shift1 = total_of(w_last)
        late = jnp.concatenate(
            [v.reshape(-1) for v in (grad_pair_weight, s_gain1, s_scale1, *q_sums(gb), s_gain2, s_ac, s_scale2, s_tc)]
        )
        late = lax.psum(late, ("samp", "head"))

    cuts = [heads * w_pair.shape[0]]
    for size in (cs, width, width, cs, width, width):
        cuts.append(cuts[-1] + size)
    sum_pair, sum_gain1, sum_scale1, sum_query, sum_gain2, sum_ac, sum_scale2, sum_tc = jnp.split(late, cuts)
    whole = (samples, rows, width)
    return (
        block_out.reshape(whole),
        grad_single.reshape(whole),
        grad_pair,
        sum_gain1,
        r_scale1,
        sum_scale1,
        r_shift1,
        r_heads[:, :wide],
        sum_query,
        r_heads[:, wide : 2 * wide],
        r_heads[:, 2 * wide :],
        r_gate,
        r_out,
        sum_pair.reshape(heads, -1).T,
        r_ac,
        sum_ac,
        sum_gain2,
        r_scale2,
        sum_scale2,
        r_shift2,
        r_hg,
        r_hu,
        r_down,
        r_tc,
        sum_tc,
    )


def solution(mesh):
    placed = (
        P("samp", "head", None),
        P("samp", "head", None),
        P(None, "head", "samp", None),
        P(),
        P("samp"),
        P("samp", "head", None),
        P(),
        P(),
        P(),
        P(),
        P(),
        P(),
        P(),
        P(),
        P(),
        P(),
        P(),
        P(),
        P(),
        P(),
        P(),
        P(),
        P(),
        P(),
        P(),
        P(),
        P(),
        P(),
    )
    return jax.shard_map(
        on_device,
        mesh=mesh,
        in_specs=placed,
        out_specs=(
            P("samp", "head", None),
            P("samp", "head", None),
            P(None, "head", "samp", None),
            P(),
            P("samp", "head"),
            P(),
            P("samp", "head"),
            P("samp", "head"),
            P(),
            P("samp", "head"),
            P("samp", "head"),
            P("samp", "head"),
            P("samp", "head"),
            P(),
            P("samp", "head"),
            P(),
            P(),
            P("samp", "head"),
            P(),
            P("samp", "head"),
            P("samp", "head"),
            P("samp", "head"),
            P("samp", "head"),
            P("samp", "head"),
            P(),
        ),
        check_vma=False,
    )
```
